32 devices in a mesh: dp: 8 (over z, y), ctx: 4 (over x, core).
Axes of the slice: x: 2, y: 2, z: 4, core: 2. Of those that a mesh axis runs over, the one named last changes fastest.
Arguments:
- tokens: bfloat16 [16384, 1024], P(('dp', 'ctx'))
- positions: int32 [3, 16384], P(None, ('dp', 'ctx')), may hold values from 0 to 15
- ln1_gain: bfloat16 [1024], P(('dp', 'ctx')), may hold values from 0.25 to 1.75
- ln1_shift: bfloat16 [1024], P(('dp', 'ctx')), may hold values from -4 to 4
- qkv_weight: bfloat16 [1024, 3072], P(('dp', 'ctx')), may hold values from -0.21875 to 0.21875
- qkv_bias: bfloat16 [3072], P(('dp', 'ctx')), may hold values from -4 to 4
- out_weight: bfloat16 [1024, 1024], P(('dp', 'ctx')), may hold values from -0.75 to 0.75
- out_bias: bfloat16 [1024], P(('dp', 'ctx')), may hold values from -4 to 4
- ln2_gain: bfloat16 [1024], P(('dp', 'ctx')), may hold values from 0.25 to 1.75
- ln2_shift: bfloat16 [1024], P(('dp', 'ctx')), may hold values from -4 to 4
- up_weight: bfloat16 [1024, 4096], P(('dp', 'ctx')), may hold values from -0.1875 to 0.1875
- up_bias: bfloat16 [4096], P(('dp', 'ctx')), may hold values from -6 to 6
- down_weight: bfloat16 [4096, 1024], P(('dp', 'ctx')), may hold values from -0.125 to 0.125
- down_bias: bfloat16 [1024], P(('dp', 'ctx')), may hold values from -4 to 4
- cotangent: bfloat16 [16384, 1024], P(('dp', 'ctx')), may hold values from -6 to 6
Outputs:
- output: bfloat16 [16384, 1024], P(('dp', 'ctx'))
- input_grad: float32 [16384, 1024], P(('dp', 'ctx'))
- ln1_gain_grad: float32 [1024], P(('dp', 'ctx'))
- ln1_shift_grad: float32 [1024], P(('dp', 'ctx'))
- qkv_weight_grad: float32 [1024, 3072], P(('dp', 'ctx'))
- qkv_bias_grad: float32 [3072], P(('dp', 'ctx'))
- out_weight_grad: float32 [1024, 1024], P(('dp', 'ctx'))
- out_bias_grad: float32 [1024], P(('dp', 'ctx'))
- ln2_gain_grad: float32 [1024], P(('dp', 'ctx'))
- ln2_shift_grad: float32 [1024], P(('dp', 'ctx'))
- up_weight_grad: float32 [1024, 4096], P(('dp', 'ctx'))
- up_bias_grad: float32 [4096], P(('dp', 'ctx'))
- down_weight_grad: float32 [4096, 1024], P(('dp', 'ctx'))
- down_bias_grad: float32 [1024], P(('dp', 'ctx'))
- norm_stats: float32 [5], replicated
The draws below stay inside these ranges and needn't reach their ends.
All inputs are finite; a program needn't handle non-finite values.
Results may differ from the reference program's by a relative error of at most 0.014.
Values may be sent and summed in bfloat16 or wider, within the bound.
No kernel may reach another device: no remote copies, remote signals or barrier semaphores. Data moves between devices by JAX's collectives and lax.ppermute only.
A program may use at most 256 MiB of HBM per device.

```python
import math
import jax
import jax.numpy as jnp
from jax import lax

D = 1024
H = 16
HD = 64
FF = 4096
CLIP = 2048
CLIPS = 8
TOKENS = 16384


def draw_tokens(key, part):
    key = jax.random.fold_in(key, 11)
    key_base, key_jitter = jax.random.split(key, 2)
    position = jnp.arange(TOKENS, dtype=jnp.float32)[:, None] / TOKENS
    jitter = jnp.exp(jax.random.uniform(key_jitter, (TOKENS, 1), jnp.float32, 0.0, math.log(3.0)))
    base_draw = jax.random.normal(key_base, (TOKENS, D), jnp.float32)
    return (base_draw * (0.5 * jnp.power(3.0, position) * jitter)).astype(jnp.bfloat16)


def touch_ends(result, rng, smallest, largest):
    longest = result.shape.index(max(result.shape))
    spots = []
    for shift in (0, 1):
        where = [jax.random.randint(jax.random.fold_in(rng, axis), (), 0, length) for axis, length in enumerate(result.shape)]
        where[longest] = (where[longest] + shift) % result.shape[longest]
        spots.append(tuple(where))
    return result.at[spots[0]].set(smallest).at[spots[1]].set(largest)


def block_levels(rng, extent, cuts, smallest, high):
    factor_of, own = 1.0, jax.random.fold_in(rng, 6)
    for dim, parts in cuts:
        draws = jnp.exp(jax.random.uniform(jax.random.fold_in(own, dim), (parts,), jnp.float32, smallest / len(cuts), high / len(cuts)))
        factor_of = factor_of * jnp.repeat(draws, extent[dim] // parts).reshape([-1 if axis == dim else 1 for axis in range(len(extent))])
    return factor_of


def normal_values(rng, extent, scale, most, pieces=(), kind=jnp.bfloat16):
    entries = jax.random.normal(rng, extent, jnp.float32) * scale
    if len(pieces) > 0:
        entries = block_levels(rng, extent, pieces, -0.22, 0.18) * entries
    return jnp.clip(entries, min=-most, max=most).astype(kind)


def setup_inputs(seed: int = 0) -> dict:
    key_list = jax.random.split(jax.random.key(seed), 16)
    return {
        "tokens": draw_tokens(jax.random.fold_in(key_list[15], 71), 0),
        "positions": touch_ends(jax.random.randint(key_list[1], (3, TOKENS), 0, 16), jax.random.fold_in(key_list[1], 1), 0, 15).astype(jnp.int32),
        "ln1_gain": jnp.clip(1.0 + 0.15 * jax.random.normal(key_list[2], (D,), jnp.float32), 0.25, 1.75).astype(jnp.bfloat16),
        "ln1_shift": normal_values(key_list[3], (D,), 0.3, 4.0, ((0, 32),)),
        "qkv_weight": normal_values(key_list[4], (D, 3 * D), (2 * D // 3) ** -0.5, 0.21875, ((0, 32),)),
        "qkv_bias": normal_values(key_list[5], (3 * D,), 0.3, 4.0, ((0, 32),)),
        "out_weight": normal_values(key_list[6], (D, D), (D // 16) ** -0.5, 0.75, ((0, 32),)),
        "out_bias": normal_values(key_list[7], (D,), 0.3, 4.0, ((0, 32),)),
        "ln2_gain": jnp.clip(1.0 + 0.15 * jax.random.normal(key_list[8], (D,), jnp.float32), 0.25, 1.75).astype(jnp.bfloat16),
        "ln2_shift": normal_values(key_list[9], (D,), 0.3, 4.0, ((0, 32),)),
        "up_weight": normal_values(key_list[10], (D, FF), D ** -0.5, 0.1875, ((0, 32),)),
        "up_bias": normal_values(key_list[11], (FF,), 0.5, 6.0, ((0, 32),)),
        "down_weight": normal_values(key_list[12], (FF, D), (FF // 2) ** -0.5, 0.125, ((0, 32),)),
        "down_bias": normal_values(key_list[13], (D,), 0.3, 4.0, ((0, 32),)),
        "cotangent": normal_values(key_list[14], (TOKENS, D), 1.0, 6.0, ((0, 32),)),
    }


EPSILON = 1e-06
HIGHEST = lax.Precision.HIGHEST

@jax.custom_vjp
def low(v):
    return lax.optimization_barrier(v.astype(jnp.bfloat16)).astype(jnp.float32)

@jax.custom_vjp
def low_back(v):
    return v

def low_keep(v):
    return (low(v), None)

def low_pass(kept, grad):
    return (grad,)

def back_keep(v):
    return (v, None)

def back_low(kept, grad):
    return (low(grad),)
low.defvjp(low_keep, low_pass)
low_back.defvjp(back_keep, back_low)

def layer_norm(values, norm_gain, norm_shift):
    average = lax.optimization_barrier(jnp.mean(values, axis=-1, keepdims=True))
    centred = values - average
    spread = lax.optimization_barrier(jnp.mean(centred * centred, axis=-1, keepdims=True))
    return centred * lax.rsqrt(spread + EPSILON) * norm_gain + norm_shift

def gelu_erf(values):
    return 0.5 * values * (1.0 + lax.erf(values * 0.7071067811865476))

def rotary_tables(positions, row_width, head_size):
    pair_gap = head_size // 6
    column = jnp.arange(row_width) % head_size
    segment = column // (2 * pair_gap)
    within = column % (2 * pair_gap)
    freq_index = (within % pair_gap).astype(jnp.float32)
    frequency = jnp.power(10000.0, -freq_index / pair_gap)
    places = positions.astype(jnp.float32)
    angles = jnp.zeros((positions.shape[1], row_width), jnp.float32)
    for axis_num in range(3):
        angles = angles + places[axis_num][:, None] * jnp.where(segment == axis_num, frequency, 0.0)[None, :]
    rotated = segment < 3
    cosine_table = jnp.where(rotated, jnp.cos(angles), 1.0)
    sine_table = jnp.where(rotated, jnp.sin(angles), 0.0)
    leading = within < pair_gap
    return (cosine_table, sine_table, leading)

def rotate(values, cosine_table, sine_table, leading, pair_gap):
    partner = jnp.where(leading, -jnp.roll(values, -pair_gap, axis=1), jnp.roll(values, pair_gap, axis=1))
    return values * cosine_table + partner * sine_table

def clip_attention(operands):
    queries, keys_low, values_low = operands
    q_heads = queries.reshape(CLIP, H, HD)
    k_heads = keys_low.reshape(CLIP, H, HD)
    v_heads = values_low.reshape(CLIP, H, HD)
    scores = low_back(jnp.einsum('qhd,khd->hqk', q_heads, k_heads, precision=HIGHEST))
    row_top = lax.optimization_barrier(jnp.max(scores, axis=-1, keepdims=True))
    exponent = jnp.exp(scores - row_top)
    row_total = lax.optimization_barrier(jnp.sum(exponent, axis=-1, keepdims=True))
    probs_low = low(exponent / row_total)
    mixed_heads = jnp.einsum('hqk,khd->qhd', probs_low, v_heads, precision=HIGHEST)
    return mixed_heads.reshape(CLIP, D)

def forward(tokens_f, positions, ln1_gain, ln1_shift, qkv_weight, qkv_bias, out_weight, out_bias, ln2_gain, ln2_shift, up_weight, up_bias, down_weight, down_bias):
    row_count = tokens_f.shape[0]
    pair_gap = HD // 6
    scaling = 1.0 / math.sqrt(HD)
    normed = low(layer_norm(tokens_f, ln1_gain, ln1_shift))
    joined = low_back(jnp.dot(normed, qkv_weight, precision=HIGHEST) + qkv_bias)
    cosine_table, sine_table, leading = rotary_tables(positions, D, HD)
    queries = low(rotate(joined[:, :D], cosine_table, sine_table, leading, pair_gap) * scaling)
    keys_low = low(rotate(joined[:, D:2 * D], cosine_table, sine_table, leading, pair_gap))
    values_low = low(joined[:, 2 * D:])
    clip_count = row_count // CLIP
    mixed_heads = lax.map(jax.checkpoint(clip_attention), (queries.reshape(clip_count, CLIP, D), keys_low.reshape(clip_count, CLIP, D), values_low.reshape(clip_count, CLIP, D))).reshape(row_count, D)
    mixed_heads = low(low_back(mixed_heads))
    attn_out = low_back(jnp.dot(mixed_heads, out_weight, precision=HIGHEST) + out_bias)
    middle = tokens_f + attn_out
    normed_two = low(layer_norm(middle, ln2_gain, ln2_shift))
    upward = low_back(jnp.dot(normed_two, up_weight, precision=HIGHEST) + up_bias)
    active = low(gelu_erf(upward))
    mlp_out = low_back(jnp.dot(active, down_weight, precision=HIGHEST) + down_bias)
    final_out = middle + mlp_out
    squares = jnp.stack([jnp.sum(tokens_f * tokens_f), jnp.sum(attn_out * attn_out), jnp.sum(middle * middle), jnp.sum(mlp_out * mlp_out), jnp.sum(final_out * final_out)])
    return (final_out, squares)

def reference(tokens, positions, ln1_gain, ln1_shift, qkv_weight, qkv_bias, out_weight, out_bias, ln2_gain, ln2_shift, up_weight, up_bias, down_weight, down_bias, cotangent):
    per_step = max(1, 4096 // CLIP)
    group_clips = max((divisor for divisor in range(1, CLIPS + 1) if CLIPS % divisor == 0 and divisor <= per_step))
    step_count = CLIPS // group_clips
    group_rows = group_clips * CLIP
    token_blocks = tokens.astype(jnp.float32).reshape(step_count, group_rows, D)
    place_blocks = positions.reshape(3, step_count, group_rows).transpose(1, 0, 2)
    cot_blocks = cotangent.astype(jnp.float32).reshape(step_count, group_rows, D)
    weights_f = tuple((param.astype(jnp.float32) for param in (ln1_gain, ln1_shift, qkv_weight, qkv_bias, out_weight, out_bias, ln2_gain, ln2_shift, up_weight, up_bias, down_weight, down_bias)))

    def step_fn(carried, inputs):
        grads_acc, squares_acc = carried
        block_in, places, cot_block = inputs

        def apply_block(block_values, *weight_list):
            return forward(block_values, places, *weight_list)
        (final_out, squares), pullback = jax.vjp(apply_block, block_in, *weights_f)
        gradients = pullback((cot_block, jnp.zeros((5,), jnp.float32)))
        grads_acc = tuple((left + right for left, right in zip(grads_acc, gradients[1:])))
        return ((grads_acc, squares_acc + squares), (final_out.astype(jnp.bfloat16), gradients[0]))
    initial = (tuple((jnp.zeros_like(param) for param in weights_f)), jnp.zeros((5,), jnp.float32))
    (gradients, squares), (outputs, in_grads) = lax.scan(step_fn, initial, (token_blocks, place_blocks, cot_blocks))
    norm_stats = jnp.sqrt(squares / (TOKENS * D))
    return (outputs.reshape(TOKENS, D), in_grads.reshape(TOKENS, D), gradients[0], gradients[1], gradients[2], gradients[3], gradients[4], gradients[5], gradients[6], gradients[7], gradients[8], gradients[9], gradients[10], gradients[11], norm_stats)
```

```python
import math

import jax
import jax.numpy as jnp
from jax import lax
from jax.experimental import pallas as pl
from jax.experimental.pallas import tpu as pltpu
from jax.sharding import Mesh
from jax.sharding import PartitionSpec as P

D = 1024
HD = 64
GAP = HD // 6
EPSILON = 1e-06
BF = jnp.bfloat16
F32 = jnp.float32
ALL = ("o", "y", "x", "c")
SWAP = ((0, 1), (1, 0))
DIAGONAL = ((0, 3), (1, 2), (2, 1), (3, 0))
NT = (((1,), (1,)), ((), ()))
NN = (((1,), (0,)), ((), ()))
TN = (((0,), (0,)), ((), ()))
VMEM_LIMIT = 50 * 2**20


def dot(left, right, dims=NN):
    return lax.dot_general(left, right, dims, preferred_element_type=F32)


def swap(values, axis):
    return lax.ppermute(values, axis, SWAP)


def by_place(flag, own, other):
    return jnp.where(flag == 0, own, other), jnp.where(flag == 0, other, own)


def place_four(high, low, parts):
    first = by_place(low, parts[0], parts[1])
    second = by_place(low, parts[2], parts[3])
    even = by_place(high, first[0], second[0])
    odd = by_place(high, first[1], second[1])
    return even[0], odd[0], even[1], odd[1]


def norm_parts(values):
    average = jnp.mean(values, axis=-1, keepdims=True)
    centred = values - average
    spread = jnp.mean(centred * centred, axis=-1, keepdims=True)
    scale = lax.rsqrt(spread + EPSILON)
    return centred * scale, scale


def norm_back(unit, scale, grad, gain):
    scaled = grad * gain
    return scale * (
        scaled
        - jnp.mean(scaled, axis=-1, keepdims=True)
        - unit * jnp.mean(scaled * unit, axis=-1, keepdims=True)
    )


def rotary_tables(places, width):
    column = jnp.arange(width) % HD
    segment = column // (2 * GAP)
    within = column % (2 * GAP)
    freq_index = (within % GAP).astype(F32)
    frequency = jnp.power(10000.0, -freq_index / GAP)
    angles = jnp.zeros((places.shape[1], width), F32)
    for axis_num in range(3):
        angles = (
            angles
            + places[axis_num][:, None] * jnp.where(segment == axis_num, frequency, 0.0)[None, :]
        )
    rotated = segment < 3
    cosine = jnp.where(rotated, jnp.cos(angles), 1.0)
    sine = jnp.where(rotated, jnp.sin(angles), 0.0)
    return cosine, sine, within < GAP


def partner_of(values, leading):
    return jnp.where(leading, -jnp.roll(values, -GAP, axis=1), jnp.roll(values, GAP, axis=1))


def attend_kernel(q_ref, k_ref, v_ref, o_ref, wide_ref, lse_ref):
    q, k, v = q_ref[...], k_ref[...], v_ref[...]
    lane = lax.broadcasted_iota(jnp.int32, (1, 2 * HD), 1)
    mixed, logs = [], []
    for head in range(2):
        mine = (lane < HD) if head == 0 else (lane >= HD)
        scores = dot(jnp.where(mine, q, 0), k, NT)
        top = jnp.max(scores, axis=1, keepdims=True)
        weight = jnp.exp(scores - top)
        total = jnp.sum(weight, axis=1, keepdims=True)
        mixed.append(dot(weight.astype(BF), v) / total)
        logs.append(top + jnp.log(total))
    out = jnp.where(lane < HD, mixed[0], mixed[1])
    o_ref[...] = out.astype(BF)
    wide_ref[...] = out
    lse_ref[...] = jnp.where(lane < HD, logs[0], logs[1])


def attend(q, k, v, rows=256):
    count, width = q.shape
    part = pl.BlockSpec((rows, 2 * HD), lambda pair, i: (i, pair))
    full = pl.BlockSpec((count, 2 * HD), lambda pair, i: (0, pair))
    return pl.pallas_call(
        attend_kernel,
        grid=(width // (2 * HD), count // rows),
        in_specs=[part, full, full],
        out_specs=[part, part, part],
        out_shape=[
            jax.ShapeDtypeStruct(q.shape, BF),
            jax.ShapeDtypeStruct(q.shape, F32),
            jax.ShapeDtypeStruct(q.shape, F32),
        ],
        compiler_params=pltpu.CompilerParams(vmem_limit_bytes=VMEM_LIMIT),
        cost_estimate=pl.CostEstimate(
            flops=35 * 10**9, bytes_accessed=8 * 2**20, transcendentals=count * count * 4
        ),
        name="attend",
    )(q, k, v)


def attend_back_kernel(
    q_ref, go_ref, wide_ref, lse_ref, k_ref, v_ref, gq_ref, gk_ref, gv_ref
):
    @pl.when(pl.program_id(1) == 0)
    def _():
        gk_ref[...] = jnp.zeros_like(gk_ref)
        gv_ref[...] = jnp.zeros_like(gv_ref)

    q, go, k, v, lse = q_ref[...], go_ref[...], k_ref[...], v_ref[...], lse_ref[...]
    lane = lax.broadcasted_iota(jnp.int32, (1, 2 * HD), 1)
    product = go.astype(F32) * wide_ref[...]
    grads = []
    for head in range(2):
        mine = (lane < HD) if head == 0 else (lane >= HD)
        q_head, go_head = jnp.where(mine, q, 0), jnp.where(mine, go, 0)
        inner = jnp.sum(jnp.where(mine, product, 0.0), axis=1, keepdims=True)
        weight = jnp.exp(dot(q_head, k, NT) - lse[:, HD * head : HD * head + 1])
        pull = (weight * (dot(go_head, v, NT) - inner)).astype(BF)
        grads.append(dot(pull, k))
        gk_ref[...] += dot(q_head.T, pull)
        gv_ref[...] += dot(go_head.T, weight.astype(BF))
    gq_ref[...] = jnp.where(lane < HD, grads[0], grads[1])


def attend_back(q, k, v, go, wide, lse, rows=256):
    count, width = q.shape
    part = pl.BlockSpec((rows, 2 * HD), lambda pair, i: (i, pair))
    full = pl.BlockSpec((count, 2 * HD), lambda pair, i: (0, pair))
    turned = pl.BlockSpec((2 * HD, count), lambda pair, i: (pair, 0))
    return pl.pallas_call(
        attend_back_kernel,
        grid=(width // (2 * HD), count // rows),
        in_specs=[part, part, part, part, full, full],
        out_specs=[part, turned, turned],
        out_shape=[
            jax.ShapeDtypeStruct(q.shape, F32),
            jax.ShapeDtypeStruct((width, count), F32),
            jax.ShapeDtypeStruct((width, count), F32),
        ],
        compiler_params=pltpu.CompilerParams(vmem_limit_bytes=VMEM_LIMIT),
        cost_estimate=pl.CostEstimate(
            flops=50 * 10**9, bytes_accessed=12 * 2**20, transcendentals=count * count * 4
        ),
        name="attend_back",
    )(q, go, wide, lse, k, v)


def per_device(
    tokens,
    positions,
    ln1_gain,
    ln1_shift,
    qkv_weight,
    qkv_bias,
    out_weight,
    out_bias,
    ln2_gain,
    ln2_shift,
    up_weight,
    up_bias,
    down_weight,
    down_bias,
    cotangent,
):
    rows = tokens.shape[0]
    outer = lax.axis_size("o")
    y, x, c = lax.axis_index("y"), lax.axis_index("x"), lax.axis_index("c")
    ctx = 2 * x + c
    shard = ln1_gain.shape[0]
    blocks = D // shard
    half_blocks = blocks // 2
    tall = up_bias.shape[0]
    ff = tall * blocks
    ff_half = ff // 2
    scaling = 1.0 / math.sqrt(HD)
    group = D // 4

    place_rows = jnp.zeros((16, D), BF).at[:3, :rows].set(positions.astype(BF))
    sent = jnp.concatenate([tokens, place_rows], axis=0)
    from_x = swap(sent, "x")
    from_c = swap(jnp.stack([sent, from_x]), "c")
    clip_rows = jnp.concatenate(
        [tokens, from_c[0, :rows], from_x[:rows], from_c[1, :rows]], axis=0
    )
    places = jnp.concatenate(
        [
            positions.astype(F32),
            from_c[0, rows : rows + 3, :rows].astype(F32),
            from_x[rows : rows + 3, :rows].astype(F32),
            from_c[1, rows : rows + 3, :rows].astype(F32),
        ],
        axis=1,
    )
    cotangent_pair = jnp.concatenate([cotangent, swap(cotangent, "c")], axis=0)

    columns = jnp.concatenate(
        [
            ln1_gain[None],
            ln1_shift[None],
            qkv_bias.reshape(3, shard),
            out_bias[None],
            ln2_gain[None],
            ln2_shift[None],
            up_bias.reshape(-1, shard),
            down_bias[None],
        ],
        axis=0,
    )
    n_vectors = columns.shape[0]
    columns = jnp.pad(columns, ((0, 128 - n_vectors), (0, 0))).T
    packed = qkv_weight.reshape(shard, 3, 4, group).transpose(2, 0, 1, 3).reshape(4, shard, -1)
    packed = jnp.concatenate([packed, jnp.broadcast_to(columns, (4, shard, 128))], axis=2)
    packed = lax.all_to_all(packed, ("x", "c"), 0, 0, tiled=True)
    gathered = lax.all_gather(
        packed.reshape(4 * shard, -1), ("o", "y"), axis=0, tiled=True
    )
    qkv_full = gathered[:, : 3 * group]
    vectors = gathered[:, 3 * group : 3 * group + n_vectors].astype(F32).T
    gain_one, shift_one = vectors[0], vectors[1]
    bias_qkv = vectors[2:5].reshape(3, blocks, shard).transpose(1, 0, 2).reshape(3, 4, group)
    bias_qkv = lax.dynamic_index_in_dim(bias_qkv, ctx, 1, keepdims=False).reshape(-1)
    bias_out, gain_two, shift_two = vectors[5], vectors[6], vectors[7]
    bias_up = vectors[8:-1].reshape(-1, blocks, shard).transpose(1, 0, 2)
    bias_up = lax.dynamic_index_in_dim(
        bias_up.reshape(half_blocks, 2, tall), c, 1, keepdims=False
    ).reshape(-1)
    bias_down = vectors[-1]

    up_parts = up_weight.reshape(shard, half_blocks, 2, tall)
    out_parts = out_weight.reshape(shard, 2, D // 2)

    def column_half(which):
        return jnp.concatenate(
            [
                lax.dynamic_index_in_dim(up_parts, which, 2, keepdims=False).reshape(shard, -1),
                lax.dynamic_index_in_dim(out_parts, which, 1, keepdims=False),
            ],
            axis=1,
        )

    upper = jnp.concatenate(by_place(c, column_half(c), swap(column_half(1 - c), "c")), axis=0)
    upper = lax.all_gather(upper, "o", axis=0, tiled=False)
    upper_x = swap(upper, "x")
    upper_y = swap(upper, "y")
    upper_xy = swap(upper_x, "y")
    upper = jnp.stack(place_four(y, x, (upper, upper_x, upper_y, upper_xy)), axis=1)
    upper = upper.reshape(D, -1)
    up_half = upper[:, :ff_half]
    out_half = upper[:, ff_half:]
    out_full = jnp.concatenate(by_place(c, out_half, swap(out_half, "c")), axis=1)
    lower = lax.all_gather(down_weight, "o", axis=0, tiled=False)
    lower_y = swap(lower, "y")
    lower_x = swap(lower, "x")
    lower_xy = swap(lower_y, "x")
    lower = jnp.stack(place_four(y, x, (lower, lower_x, lower_y, lower_xy)), axis=1)
    down_half = lower.reshape(ff_half, D)

    inputs_f = tokens.astype(F32)
    clip_unit, _ = norm_parts(clip_rows.astype(F32))
    normed_low = (clip_unit * gain_one + shift_one).astype(BF)
    joined = dot(normed_low, qkv_full) + bias_qkv
    cosine, sine, leading = rotary_tables(places, 2 * HD)
    cosine, sine = jnp.tile(cosine, (1, 2)), jnp.tile(sine, (1, 2))
    leading = jnp.tile(leading, 2)

    def turn(part):
        return part * cosine + partner_of(part, leading) * sine

    queries = (turn(joined[:, :group]) * scaling).astype(BF)
    keys_low = turn(joined[:, group : 2 * group]).astype(BF)
    values_low = joined[:, 2 * group :].astype(BF)
    mixed, mixed_wide, row_logs = attend(queries, keys_low, values_low)

    def to_owners(values):
        parts = (
            values[:rows],
            swap(values[rows : 2 * rows], "c"),
            swap(values[2 * rows : 3 * rows], "x"),
            lax.ppermute(values[3 * rows :], ("x", "c"), DIAGONAL),
        )
        return jnp.concatenate(place_four(x, c, parts), axis=1)

    mixed_low = to_owners(mixed)
    attn_out = dot(mixed_low, out_full) + bias_out
    middle = inputs_f + attn_out
    unit_two, scale_two = norm_parts(middle)
    normed_two = (unit_two * gain_two + shift_two).astype(BF)

    normed_pair = jnp.concatenate([normed_two, swap(normed_two, "c")], axis=0)
    upward = dot(normed_pair, up_half) + bias_up
    bell = 0.5 * (1.0 + lax.erf(upward * 0.7071067811865476))
    active = (upward * bell).astype(BF)
    mlp_part = dot(active, down_half)
    grad_active = dot(cotangent_pair, down_half, NT)
    slope = bell + upward * jnp.exp(-0.5 * upward * upward) * (1.0 / math.sqrt(2.0 * math.pi))
    grad_up = (grad_active * slope).astype(BF)
    down_grad = dot(active, cotangent_pair, TN).astype(BF)
    up_grad = dot(normed_pair, grad_up, TN).astype(BF)
    up_bias_grad = jnp.sum(grad_up.astype(F32), axis=0)
    grad_two = dot(grad_up, up_half, NT)
    grad_two = grad_two[:rows] + swap(grad_two[rows:], "c")
    mlp_out = mlp_part[:rows] + swap(mlp_part[rows:], "c") + bias_down
    final_out = middle + mlp_out
    squares = jnp.stack(
        [
            jnp.sum(inputs_f * inputs_f),
            jnp.sum(attn_out * attn_out),
            jnp.sum(middle * middle),
            jnp.sum(mlp_out * mlp_out),
            jnp.sum(final_out * final_out),
        ]
    )
    squares = jnp.pad(squares[None], ((0, 7), (0, 123)))
    squares = lax.all_gather(squares, ALL, axis=0, tiled=False)
    entry_count = rows * lax.axis_size(ALL) * D
    norm_stats = jnp.sqrt(jnp.sum(squares[:, 0, :5], axis=0) / entry_count)

    grad_final = cotangent.astype(F32)
    down_bias_grad = jnp.sum(grad_final, axis=0)
    gain_two_grad = jnp.sum(grad_two * unit_two, axis=0)
    shift_two_grad = jnp.sum(grad_two, axis=0)
    grad_middle = grad_final + norm_back(unit_two, scale_two, grad_two, gain_two)
    grad_attn = grad_middle.astype(BF)
    out_bias_grad = jnp.sum(grad_attn.astype(F32), axis=0)
    out_grad = dot(mixed_low, grad_attn, TN).astype(BF).reshape(D, 2, D // 2)
    out_grad = lax.dynamic_index_in_dim(out_grad, c, 1, keepdims=False) + swap(
        lax.dynamic_index_in_dim(out_grad, 1 - c, 1, keepdims=False), "c"
    )
    grad_mixed = dot(grad_attn, out_full, NT).astype(BF)

    grad_groups = grad_mixed.reshape(rows, 4, group)

    def group_of(place):
        return lax.dynamic_index_in_dim(grad_groups, ctx ^ place, 1, keepdims=False)

    grad_mixed = jnp.concatenate(
        [
            group_of(0),
            swap(group_of(1), "c"),
            swap(group_of(2), "x"),
            lax.ppermute(group_of(3), ("x", "c"), DIAGONAL),
        ],
        axis=0,
    )

    def to_column(values, first, second):
        parts = values.reshape(outer, 2, 2, -1, values.shape[-1])
        flags = {"y": y, "x": x}

        def quarter(flip_first, flip_second):
            flips = {first: flip_first, second: flip_second}
            place = (flags["y"] ^ flips["y"]) * 2 + (flags["x"] ^ flips["x"])
            return lax.dynamic_index_in_dim(
                parts.reshape(outer, 4, -1, values.shape[-1]), place, 1, keepdims=False
            )

        passed = swap(quarter(1, 1), first)
        kept = swap(quarter(1, 0), first)
        passed = swap(quarter(0, 1) + passed, second)
        summed = quarter(0, 0) + kept + passed
        return lax.psum_scatter(summed, "o", scatter_dimension=0, tiled=False)

    down_weight_grad = to_column(down_grad, "x", "y").astype(F32)
    upper_grad = to_column(jnp.concatenate([up_grad, out_grad], axis=1), "y", "x")
    upper_grad = upper_grad.reshape(2, shard, -1)
    upper_own = lax.dynamic_index_in_dim(upper_grad, c, 0, keepdims=False)
    upper_other = swap(lax.dynamic_index_in_dim(upper_grad, 1 - c, 0, keepdims=False), "c")
    upper_even, upper_odd = by_place(c, upper_own.astype(F32), upper_other.astype(F32))
    up_weight_grad = jnp.stack(
        [
            upper_even[:, :ff_half].reshape(shard, half_blocks, tall),
            upper_odd[:, :ff_half].reshape(shard, half_blocks, tall),
        ],
        axis=2,
    ).reshape(shard, ff)
    out_weight_grad = jnp.concatenate([upper_even[:, ff_half:], upper_odd[:, ff_half:]], axis=1)

    grad_q, grad_k, grad_v = attend_back(
        queries, keys_low, values_low, grad_mixed, mixed_wide, row_logs
    )

    def turn_back(grad):
        return grad * cosine - partner_of(grad * sine, leading)

    grad_joined = jnp.concatenate(
        [turn_back(grad_q) * scaling, turn_back(grad_k.T), grad_v.T], axis=1
    ).astype(BF)
    qkv_grad = dot(normed_low, grad_joined, TN)
    qkv_bias_grad = jnp.sum(grad_joined.astype(F32), axis=0)
    grad_normed = dot(grad_joined, qkv_full, NT)

    grad_parts = grad_normed.reshape(4, rows, D)
    to_core = swap(grad_parts[1::2].astype(BF), "c").astype(F32)
    own_part = grad_parts[0] + to_core[0]
    grad_one = own_part + swap((grad_parts[2] + to_core[1]).astype(BF), "x").astype(F32)
    unit_one, scale_one = norm_parts(inputs_f)
    input_grad = grad_middle + norm_back(unit_one, scale_one, grad_one, gain_one)
    gain_one_grad = jnp.sum(grad_one * unit_one, axis=0)
    shift_one_grad = jnp.sum(grad_one, axis=0)

    mine = (jnp.arange(4) == ctx)[None, :, None]
    qkv_bias_grad = jnp.where(mine, qkv_bias_grad.reshape(3, 1, group), 0.0)
    qkv_bias_grad = qkv_bias_grad.reshape(blocks, 3, shard).transpose(1, 0, 2).reshape(3, D)
    mine = (jnp.arange(2) == c)[None, :, None]
    up_bias_grad = jnp.where(mine, up_bias_grad.reshape(half_blocks, 1, tall), 0.0)
    up_bias_grad = up_bias_grad.reshape(blocks, -1, shard).transpose(1, 0, 2).reshape(-1, D)
    vector_grads = jnp.concatenate(
        [
            gain_one_grad[None],
            shift_one_grad[None],
            qkv_bias_grad,
            out_bias_grad[None],
            gain_two_grad[None],
            shift_two_grad[None],
            up_bias_grad,
            down_bias_grad[None],
        ],
        axis=0,
    )
    vector_grads = jnp.pad(vector_grads, ((0, 128 - n_vectors), (0, 0))).T
    last = jnp.concatenate([qkv_grad, vector_grads], axis=1).astype(BF)
    last = last.reshape(outer, 2, 4 * shard, -1)
    last = lax.dynamic_index_in_dim(last, y, 1, keepdims=False) + swap(
        lax.dynamic_index_in_dim(last, 1 - y, 1, keepdims=False), "y"
    )
    last = lax.psum_scatter(last, "o", scatter_dimension=0, tiled=False)
    last = lax.all_to_all(last.reshape(4, shard, -1), ("x", "c"), 0, 0, tiled=True)
    last = last.astype(F32)
    qkv_weight_grad = (
        last[:, :, : 3 * group].reshape(4, shard, 3, group).transpose(1, 2, 0, 3)
    ).reshape(shard, 3 * D)
    vector_grads = jnp.sum(last[:, :, 3 * group : 3 * group + n_vectors], axis=0).T

    return (
        final_out.astype(BF),
        input_grad,
        vector_grads[0],
        vector_grads[1],
        qkv_weight_grad,
        vector_grads[2:5].reshape(-1),
        out_weight_grad,
        vector_grads[5],
        vector_grads[6],
        vector_grads[7],
        up_weight_grad,
        vector_grads[8:-1].reshape(-1),
        down_weight_grad,
        vector_grads[-1],
        norm_stats,
    )


def solution(mesh):
    devices = mesh.devices
    fine = Mesh(devices.reshape(-1, 2, 2, 2), ALL)
    rows, vector, whole = P(ALL, None), P(ALL), P()
    in_specs = (
        rows,
        P(None, ALL),
        vector,
        vector,
        rows,
        vector,
        rows,
        vector,
        vector,
        vector,
        rows,
        vector,
        rows,
        vector,
        rows,
    )
    out_specs = (
        rows,
        rows,
        vector,
        vector,
        rows,
        vector,
        rows,
        vector,
        vector,
        vector,
        rows,
        vector,
        rows,
        vector,
        whole,
    )
    return jax.shard_map(
        per_device, mesh=fine, in_specs=in_specs, out_specs=out_specs, check_vma=False
    )
```

```python
import functools
import math

import jax
import jax.numpy as jnp
from jax import lax
from jax.experimental import pallas as pl
from jax.experimental.pallas import tpu as pltpu
from jax.sharding import Mesh
from jax.sharding import PartitionSpec as P

D = 1024
HD = 64
GAP = HD // 6
PAIR = 2 * HD
GROUP = D // 4
EPSILON = 1e-06
BF = jnp.bfloat16
F32 = jnp.float32
ALL = ("o", "y", "x", "c")
SWAP = ((0, 1), (1, 0))
NT = (((1,), (1,)), ((), ()))
NN = (((1,), (0,)), ((), ()))
TN = (((0,), (0,)), ((), ()))
VMEM_LIMIT = 58 * 2**20
SMALL = pl.CostEstimate(flops=10**6, bytes_accessed=2**16, transcendentals=0)
MASK = (0, 2, 1, 3)


def dot(left, right, dims=NN):
    return lax.dot_general(left, right, dims, preferred_element_type=F32)


def swap(values, axis):
    return lax.ppermute(values, axis, SWAP)


def tie(*values):
    return lax.optimization_barrier(values)


def by_place(flag, own, other):
    return jnp.where(flag == 0, own, other), jnp.where(flag == 0, other, own)


def place_four(high, low, parts):
    first = by_place(low, parts[0], parts[1])
    second = by_place(low, parts[2], parts[3])
    even = by_place(high, first[0], second[0])
    odd = by_place(high, first[1], second[1])
    return even[0], odd[0], even[1], odd[1]


def far(values):
    return lax.ppermute(values, "o", [(i, i ^ 2) for i in range(4)])


def near(values):
    return lax.ppermute(values, "o", [(i, i ^ 1) for i in range(4)])


def level_place(own, level):
    return own ^ (level % 2 * 2 + level // 2)


def far_half(values):
    if lax.axis_size("o") != 4:
        return lax.all_gather(values, "o", axis=0, tiled=False)
    return far(values)


def near_half(values, came):
    if lax.axis_size("o") != 4:
        return came, came
    pair = jnp.stack([values, came])
    return pair, near(pair)


def all_blocks(halves):
    if lax.axis_size("o") != 4:
        return halves[0]
    return jnp.concatenate(halves, axis=0)


def near_sums(*terms):
    if lax.axis_size("o") != 4:
        return sum(terms)
    kept = sum(term[:2].astype(F32) for term in terms)
    return kept, near(sum(term[2:].astype(F32) for term in terms).astype(BF))


def far_sums(values):
    if lax.axis_size("o") != 4:
        return lax.psum_scatter(values, "o", scatter_dimension=0, tiled=False).astype(F32)
    kept, came = values
    sums = kept + came.astype(F32)
    return sums[0] + far(sums[1].astype(BF)).astype(F32)


def norm_parts(values):
    average = jnp.mean(values, axis=-1, keepdims=True)
    centred = values - average
    spread = jnp.mean(centred * centred, axis=-1, keepdims=True)
    scale = lax.rsqrt(spread + EPSILON)
    return centred * scale, scale


def norm_back(unit, scale, grad, gain):
    scaled = grad * gain
    return scale * (
        scaled
        - jnp.mean(scaled, axis=-1, keepdims=True)
        - unit * jnp.mean(scaled * unit, axis=-1, keepdims=True)
    )


def rotary_tables(places, width):
    column = jnp.arange(width) % HD
    segment = column // (2 * GAP)
    within = column % (2 * GAP)
    freq_index = (within % GAP).astype(F32)
    frequency = jnp.power(10000.0, -freq_index / GAP)
    angles = jnp.zeros((places.shape[1], width), F32)
    for axis_num in range(3):
        angles = (
            angles
            + places[axis_num][:, None] * jnp.where(segment == axis_num, frequency, 0.0)[None, :]
        )
    rotated = segment < 3
    return jnp.where(rotated, jnp.cos(angles), 1.0), jnp.where(rotated, jnp.sin(angles), 0.0)


def shifted(values, leading):
    ahead = pltpu.roll(values, PAIR - GAP, 1)
    behind = pltpu.roll(values, GAP, 1)
    return jnp.where(leading, -ahead, behind)


def leading_lanes():
    lane = lax.broadcasted_iota(jnp.int32, (1, PAIR), 1)
    return lane % HD % (2 * GAP) < GAP


def column_sums(values):
    return jnp.sum(values, axis=0, keepdims=True)


def params(aliases=None):
    return dict(
        compiler_params=pltpu.CompilerParams(vmem_limit_bytes=VMEM_LIMIT),
        cost_estimate=SMALL,
        input_output_aliases=aliases or {},
    )


def shape(dims, kind):
    return jax.ShapeDtypeStruct(dims, kind)


def pack_kernel(w_ref, *refs):
    vectors, out_ref = refs[:-1], refs[-1]
    shard = w_ref.shape[0]
    rows = []
    for ref in vectors:
        values = ref[...].astype(F32)
        rows += [values[:, low : low + shard] for low in range(0, values.shape[1], shard)]
    columns = jnp.concatenate(rows + [jnp.zeros((128 - len(rows), shard), F32)], axis=0).T
    for place in range(4):
        for part in range(3):
            start = part * D + place * GROUP
            out_ref[place, :, part * GROUP : (part + 1) * GROUP] = w_ref[:, start : start + GROUP]
        out_ref[place, :, 3 * GROUP :] = columns.astype(BF)


def pack(weight, vectors):
    return pl.pallas_call(
        pack_kernel,
        out_shape=shape((4, weight.shape[0], 3 * GROUP + 128), BF),
        name="pack",
        **params(),
    )(weight, *vectors)


def bias_places(place, shard):
    column = lax.broadcasted_iota(jnp.int32, (1, 3 * GROUP), 1)
    target = column // GROUP * D + place * GROUP + column % GROUP
    source = target // (3 * shard) * shard + target % shard
    hot = lax.broadcasted_iota(jnp.int32, (D, 3 * GROUP), 0) == source
    return jnp.where(hot, 1.0, 0.0).astype(BF), target % (3 * shard) // shard


def load_blocks(sources, target, semaphores):
    found = []
    for source, index, place in sources:
        block = source.at[index]
        height = block.shape[0]
        start = pl.multiple_of(place * height, height)
        found.append(
            pltpu.make_async_copy(
                block, target.at[pl.ds(start, height)], semaphores.at[len(found)]
            )
        )
    return found


def piece_blocks(arrays, place):
    if len(arrays) == 1:
        return [(arrays[0], 0, 0)]
    return [
        (source, level, level_place(place[3], level) * 4 + (place[1] ^ flip))
        for flip, source in enumerate(arrays)
        for level in range(4)
    ]


def project_kernel(place_ref, x_ref, cos_ref, sin_ref, *refs, shard, pieces):
    sources, refs = refs[:pieces], refs[pieces:]
    n_ref, q_ref, k_ref, v_ref, t_ref, w_ref, b_ref, semaphores = refs

    @pl.when(pl.program_id(0) == 0)
    def _():
        if pieces == 1:
            blocks = [(sources[0], 0, 0)]
        else:
            blocks = [
                (
                    source,
                    level,
                    (level_place(place_ref[3], level) ^ (piece // 2)) * 2
                    + (place_ref[2] ^ (piece % 2)),
                )
                for piece, source in enumerate(sources)
                for level in range(2)
            ]
        copies = load_blocks(blocks, w_ref, semaphores)
        for copy in copies:
            copy.start()
        for copy in copies:
            copy.wait()
        t_ref[...] = w_ref[:, 3 * GROUP :].astype(F32).T[: t_ref.shape[0]]
        hot, part = bias_places(place_ref[0], shard)
        found = dot(t_ref[...].astype(BF), hot)
        bias = jnp.where(part == 0, found[2:3], jnp.where(part == 1, found[3:4], found[4:5]))
        b_ref[...] = jnp.broadcast_to(bias, b_ref.shape)

    unit, _ = norm_parts(x_ref[...].astype(F32))
    normed = (unit * t_ref[0:1] + t_ref[1:2]).astype(BF)
    n_ref[...] = normed
    joined = dot(normed, w_ref[:, : 3 * GROUP]) + b_ref[0:1]
    cosine, sine, leading = cos_ref[...], sin_ref[...], leading_lanes()
    for ref, start, factor in ((q_ref, 0, 1.0 / math.sqrt(HD)), (k_ref, GROUP, 1.0)):
        for low in range(0, GROUP, PAIR):
            part = joined[:, start + low : start + low + PAIR]
            turned = part * cosine + shifted(part, leading) * sine
            ref[:, low : low + PAIR] = (turned * factor).astype(BF)
    v_ref[...] = joined[:, 2 * GROUP :].astype(BF)


def project(place, values, pieces, cosine, sine, shard, rows=256):
    count = values.shape[0]
    width = pieces[0].shape[-1]

    def part(cols):
        return pl.BlockSpec((rows, cols), lambda i, p: (i, 0))

    def whole(*dims):
        return pl.BlockSpec(dims, lambda i, p: (0, 0))

    return pl.pallas_call(
        functools.partial(project_kernel, shard=shard, pieces=len(pieces)),
        grid_spec=pltpu.PrefetchScalarGridSpec(
            num_scalar_prefetch=1,
            grid=(count // rows,),
            in_specs=[part(D), part(PAIR), part(PAIR)]
            + [pl.BlockSpec(memory_space=pl.ANY)] * len(pieces),
            out_specs=[part(D), part(GROUP), part(GROUP), part(GROUP), whole(16, D), whole(D, width)],
            scratch_shapes=[
                pltpu.VMEM((8, 3 * GROUP), F32),
                pltpu.SemaphoreType.DMA((len(pieces) * pieces[0].shape[0],)),
            ],
        ),
        out_shape=[
            shape((count, D), BF),
            shape((count, GROUP), BF),
            shape((count, GROUP), BF),
            shape((count, GROUP), BF),
            shape((16, D), F32),
            shape((D, width), BF),
        ],
        name="project",
        **params(),
    )(place, values, cosine, sine, *pieces)


def attend_kernel(q_ref, k_ref, v_ref, *refs):
    o_ref, wide_ref, lse_ref = refs[-3:]
    q, k, v = q_ref[...], k_ref[...], v_ref[...]
    lane = lax.broadcasted_iota(jnp.int32, (1, PAIR), 1)
    mixed, logs = [], []
    for head in range(2):
        mine = (lane < HD) if head == 0 else (lane >= HD)
        scores = dot(jnp.where(mine, q, 0), k, NT)
        top = jnp.max(scores, axis=1, keepdims=True)
        weight = jnp.exp(scores - top)
        total = jnp.sum(weight, axis=1, keepdims=True)
        mixed.append(dot(weight.astype(BF), v) / total)
        logs.append(top + jnp.log(total))
    out = jnp.where(lane < HD, mixed[0], mixed[1])
    o_ref[...] = out.astype(BF)
    wide_ref[...] = out
    lse_ref[...] = jnp.where(lane < HD, logs[0], logs[1])


def attend(q, k, v, side, pair=None, before=None, rows=256):
    count = q.shape[0]
    half = count // 2
    per = count // 4 // rows
    pairs = GROUP // PAIR if pair is None else 1
    first = 0 if pair is None else pair

    def block(i):
        return i // per * 2 * per + side * per + i % per

    full = pl.BlockSpec((count, PAIR), lambda j, i: (0, first + j))
    out = pl.BlockSpec((rows, PAIR), lambda j, i: (i, first + j))
    before = list(before or ())
    return pl.pallas_call(
        attend_kernel,
        grid=(pairs, half // rows),
        in_specs=[pl.BlockSpec((rows, PAIR), lambda j, i: (block(i), first + j)), full, full]
        + [pl.BlockSpec(memory_space=pl.ANY)] * len(before),
        out_specs=[out, out, out],
        out_shape=[shape((half, GROUP), BF), shape((half, GROUP), F32), shape((half, GROUP), F32)],
        name="attend",
        **params({3: 0, 4: 1, 5: 2} if before else None),
    )(q, k, v, *before)


def attend_back_kernel(
    q_ref, go_ref, go_other_ref, wide_ref, lse_ref, k_ref, v_ref, cos_ref, sin_ref, *refs, last, block
):
    step, rows = pl.program_id(1), q_ref.shape[0]
    if last:
        k_start, v_start, _, gq_ref, gk_ref, gv_ref, k_sum, v_sum = refs
    else:
        gq_ref, k_sum, v_sum = refs

    @pl.when(step == 0)
    def _():
        if last:
            k_sum[...] = k_start[...]
            v_sum[...] = v_start[...]
        else:
            k_sum[...] = jnp.zeros_like(k_sum)
            v_sum[...] = jnp.zeros_like(v_sum)

    q, k, v, lse = q_ref[...], k_ref[...], v_ref[...], lse_ref[...]
    go = jnp.where(step < pl.num_programs(1) // 2, go_ref[...], go_other_ref[...])
    lane = lax.broadcasted_iota(jnp.int32, (1, PAIR), 1)
    leading = leading_lanes()
    product = go.astype(F32) * wide_ref[...]
    grads = []
    for head in range(2):
        mine = (lane < HD) if head == 0 else (lane >= HD)
        q_head, go_head = jnp.where(mine, q, 0), jnp.where(mine, go, 0)
        inner = jnp.sum(jnp.where(mine, product, 0.0), axis=1, keepdims=True)
        weight = jnp.exp(dot(q_head, k, NT) - lse[:, HD * head : HD * head + 1])
        pull = (weight * (dot(go_head, v, NT) - inner)).astype(BF)
        grads.append(dot(pull, k))
        k_sum[...] += dot(q_head.T, pull)
        v_sum[...] += dot(go_head.T, weight.astype(BF))
    grad = jnp.where(lane < HD, grads[0], grads[1])
    here = pl.ds(pl.multiple_of(block(step) * rows, rows), rows)
    grad = grad * cos_ref[here] - shifted(grad * sin_ref[here], leading)
    gq_ref[...] = (grad * (1.0 / math.sqrt(HD))).astype(BF)

    if last:

        @pl.when(step == pl.num_programs(1) - 1)
        def _():
            grad = k_sum[...].T
            grad = grad * cos_ref[...] - shifted(grad * sin_ref[...], leading)
            gk_ref[...] = grad.astype(BF)
            gv_ref[...] = v_sum[...].T.astype(BF)


def attend_back(q, k, v, go, go_other, go_place, wide, lse, cosine, sine, side, before=None, rows=256):
    count = q.shape[0]
    half = count // 2
    per = count // 4 // rows
    last = before is not None

    def block(i):
        return i // per * 2 * per + side * per + i % per

    part = pl.BlockSpec((rows, PAIR), lambda pair, i: (block(i), pair))
    own = pl.BlockSpec((rows, PAIR), lambda pair, i: (i, pair))
    full = pl.BlockSpec((count, PAIR), lambda pair, i: (0, pair))
    table = pl.BlockSpec((count, PAIR), lambda pair, i: (0, 0))
    turned = pl.BlockSpec((PAIR, count), lambda pair, i: (pair, 0))
    sums = shape((GROUP, count), F32)
    grad = shape((count, GROUP), BF)
    low = pl.BlockSpec((rows, PAIR), lambda pair, i: (jnp.minimum(i, per - 1), pair))
    high = pl.BlockSpec(
        (rows, PAIR), lambda pair, i: (jnp.maximum(i - per, 0) + go_place * per, pair)
    )
    in_specs = [part, low, high, own, own, full, full, table, table]
    operands = [q, go, go_other, wide, lse, k, v, cosine, sine]
    if last:
        in_specs += [turned, turned, pl.BlockSpec(memory_space=pl.ANY)]
        operands += [before[1], before[2], before[0]]
        out_specs, out_shape = [part, full, full], [grad, grad, grad]
        scratch = [pltpu.VMEM((PAIR, count), F32)] * 2
    else:
        out_specs, out_shape, scratch = [part, turned, turned], [grad, sums, sums], []
    return pl.pallas_call(
        functools.partial(attend_back_kernel, last=last, block=block),
        grid=(GROUP // PAIR, half // rows),
        in_specs=in_specs,
        out_specs=out_specs,
        out_shape=out_shape,
        scratch_shapes=scratch,
        name="attend_back",
        **params({11: 0} if last else None),
    )(*operands)


def middle_kernel(place_ref, x_ref, t_ref, *refs, four):
    o_refs, sources, refs = refs[:4], refs[4:6], refs[6:]
    mid_ref, n_ref, s_ref, w_ref, semaphores = refs

    @pl.when(pl.program_id(0) == 0)
    def _():
        s_ref[...] = jnp.zeros_like(s_ref)
        if four:
            blocks = [
                (
                    source.at[flip],
                    level,
                    (level_place(place_ref[3], level) * 4 + (place_ref[1] ^ flip)) * 2
                    + (place_ref[0] % 2 ^ other),
                )
                for other, source in enumerate(sources)
                for flip in range(4)
                for level in range(4)
            ]
        else:
            blocks = [(sources[0].at[0], 0, 0)]
        copies = load_blocks(blocks, w_ref, semaphores)
        for copy in copies:
            copy.start()
        for copy in copies:
            copy.wait()

    x = x_ref[...].astype(F32)
    attn = t_ref[5:6]
    for mask, o_ref in zip(MASK, o_refs):
        start = pl.multiple_of((place_ref[0] ^ mask) * GROUP, GROUP)
        attn = attn + dot(o_ref[...], w_ref[pl.ds(start, GROUP)])
    mid = x + attn
    mid_ref[...] = mid
    unit, _ = norm_parts(mid)
    n_ref[...] = (unit * t_ref[6:7] + t_ref[7:8]).astype(BF)
    s_ref[0:1] += column_sums(x * x)
    s_ref[1:2] += column_sums(attn * attn)
    s_ref[2:3] += column_sums(mid * mid)


def group_specs():
    return [
        pl.BlockSpec((GROUP, D), lambda i, p, mask=mask: (p[0] ^ mask, 0)) for mask in MASK
    ]


def mixed_specs(count, rows):
    first = pl.BlockSpec((rows, GROUP), lambda i, p: (i, 0))
    second = pl.BlockSpec((rows, GROUP), lambda i, p: (i + count // rows, 0))
    return [first, first, first, second]


def middle(place, tokens, vectors, mixed, sources, four, rows=256):
    count = tokens.shape[0]
    full = pl.BlockSpec((rows, D), lambda i, p: (i, 0))

    def whole(*dims):
        return pl.BlockSpec(dims, lambda i, p: (0, 0))

    return pl.pallas_call(
        functools.partial(middle_kernel, four=four),
        grid_spec=pltpu.PrefetchScalarGridSpec(
            num_scalar_prefetch=1,
            grid=(count // rows,),
            in_specs=[full, whole(16, D)]
            + mixed_specs(count, rows)
            + [pl.BlockSpec(memory_space=pl.ANY)] * 2,
            out_specs=[full, full, whole(8, D), whole(D, D)],
            scratch_shapes=[pltpu.SemaphoreType.DMA((32,))],
        ),
        out_shape=[
            shape((count, D), F32),
            shape((count, D), BF),
            shape((8, D), F32),
            shape((D, D), BF),
        ],
        name="middle",
        **params(),
    )(place, tokens, vectors, *mixed, mixed[2], *sources)


def hidden_kernel(
    place_ref, t_ref, own_ref, other_ref, cot_ref, cot_other_ref, *refs, shard, tall, pieces
):
    up_pieces, down_pieces = refs[:pieces], refs[pieces : 2 * pieces]
    outs, (up, down, up_sem, down_sem) = refs[2 * pieces : -4], refs[-4:]
    act_ref, gu_ref, b_ref, gn_ref, gn_other_ref, mlp_ref, mlp_other_ref = outs
    step = pl.program_id(0)
    chunk = act_ref.shape[1]

    @pl.when(step == 0)
    def _():
        copies = load_blocks(piece_blocks(up_pieces, place_ref), up, up_sem)
        copies += load_blocks(piece_blocks(down_pieces, place_ref), down, down_sem)
        for copy in copies:
            copy.start()
        for copy in copies:
            copy.wait()
        for ref in (gn_ref, gn_other_ref, mlp_ref, mlp_other_ref):
            ref[...] = jnp.zeros_like(ref)

    column = lax.broadcasted_iota(jnp.int32, (1, chunk), 1) + step * chunk
    source = (column // tall * 2 + place_ref[0] % 2) * shard + column % shard
    which = column % tall // shard
    hot = lax.broadcasted_iota(jnp.int32, (D, chunk), 0) == source
    found = dot(t_ref[...].astype(BF), jnp.where(hot, 1.0, 0.0).astype(BF))
    bias = jnp.zeros((1, chunk), F32)
    for row in range(tall // shard):
        bias = jnp.where(which == row, found[8 + row : 9 + row], bias)

    here = pl.ds(pl.multiple_of(step * chunk, chunk), chunk)
    up_part, down_part = up[:, here], down[here, :]
    sums = jnp.zeros((1, chunk), F32)
    rows = own_ref.shape[0]
    for low, n_ref, c_ref, g_ref, m_ref in (
        (0, own_ref, cot_ref, gn_ref, mlp_ref),
        (rows, other_ref, cot_other_ref, gn_other_ref, mlp_other_ref),
    ):
        upward = dot(n_ref[...], up_part) + bias
        grad_active = dot(c_ref[...], down_part, NT)
        bell = 0.5 * (1.0 + lax.erf(upward * 0.7071067811865476))
        active = (upward * bell).astype(BF)
        slope = bell + upward * jnp.exp(-0.5 * upward * upward) * (1.0 / math.sqrt(2.0 * math.pi))
        grad_up = (grad_active * slope).astype(BF)
        act_ref[low : low + rows] = active
        gu_ref[low : low + rows] = grad_up
        sums += column_sums(grad_up.astype(F32))
        g_ref[...] += dot(grad_up, up_part, NT)
        m_ref[...] += dot(active, down_part)
    b_ref[...] = jnp.broadcast_to(sums, b_ref.shape)


def hidden(place, vectors, own, other, cot, cot_other, up_pieces, down_pieces, shard, tall, chunk=512):
    rows = own.shape[0]
    width = up_pieces[0].shape[-1]
    pieces = len(up_pieces)
    blocks = pieces * up_pieces[0].shape[0]

    def whole(*dims):
        return pl.BlockSpec(dims, lambda i, p: (0, 0))

    part = pl.BlockSpec((2 * rows, chunk), lambda i, p: (0, i))
    return pl.pallas_call(
        functools.partial(hidden_kernel, shard=shard, tall=tall, pieces=pieces),
        grid_spec=pltpu.PrefetchScalarGridSpec(
            num_scalar_prefetch=1,
            grid=(width // chunk,),
            in_specs=[whole(16, D)]
            + [whole(rows, D)] * 4
            + [pl.BlockSpec(memory_space=pl.ANY)] * (2 * pieces),
            out_specs=[part, part, pl.BlockSpec((8, chunk), lambda i, p: (0, i))]
            + [whole(rows, D)] * 4,
            scratch_shapes=[
                pltpu.VMEM((D, width), BF),
                pltpu.VMEM((width, D), BF),
                pltpu.SemaphoreType.DMA((blocks,)),
                pltpu.SemaphoreType.DMA((blocks,)),
            ],
        ),
        out_shape=[
            shape((2 * rows, width), BF),
            shape((2 * rows, width), BF),
            shape((8, width), F32),
        ]
        + [shape((rows, D), F32)] * 4,
        name="hidden",
        **params(),
    )(place, vectors, own, other, cot, cot_other, *up_pieces, *down_pieces)


def finish_kernel(mid_ref, mlp_ref, came_ref, t_ref, out_ref, s_ref, *, row):
    @pl.when(pl.program_id(0) == 0)
    def _():
        s_ref[...] = jnp.zeros_like(s_ref)

    mlp = mlp_ref[...] + came_ref[...] + t_ref[row : row + 1]
    final = mid_ref[...] + mlp
    out_ref[...] = final.astype(BF)
    s_ref[0:1] += column_sums(mlp * mlp)
    s_ref[1:2] += column_sums(final * final)


def finish(mid, mlp, came, vectors, row, rows=256):
    full = pl.BlockSpec((rows, D), lambda i: (i, 0))
    return pl.pallas_call(
        functools.partial(finish_kernel, row=row),
        grid=(mid.shape[0] // rows,),
        in_specs=[full, full, full, pl.BlockSpec((16, D), lambda i: (0, 0))],
        out_specs=[full, pl.BlockSpec((8, D), lambda i: (0, 0))],
        out_shape=[shape(mid.shape, BF), shape((8, D), F32)],
        name="finish",
        **params(),
    )(mid, mlp, came, vectors)


def quarters_kernel(place_ref, own_ref, other_ref, *refs, wide):
    outs, total = refs[-5:-1], refs[-1]
    rows = own_ref.shape[0]
    if wide:
        right = refs[0]
        total[...] = dot(own_ref[...], right[:rows], TN) + dot(other_ref[...], right[rows:], TN)
    else:
        left = refs[0]
        total[...] = dot(left[:rows], own_ref[...], TN) + dot(left[rows:], other_ref[...], TN)
    height = total.shape[0] // 4
    for flip, out in enumerate(outs):
        start = pl.multiple_of((place_ref[1] ^ flip) * height, height)
        out[0, :height] = total[pl.ds(start, height)].astype(BF)
        if not wide:
            out[0, height:] = refs[flip + 1][0, 0]


def level_of(flip):
    return flip % 2 * 2 + flip // 2


def up_quarters(place, own, other, grads):
    rows, width = own.shape[0], grads.shape[1]
    part = pl.BlockSpec((rows, D // 4), lambda i, p: (0, i))
    out = pl.BlockSpec((1, D // 16, width), lambda i, p: (level_of(i ^ p[3]), 0, 0))
    return pl.pallas_call(
        functools.partial(quarters_kernel, wide=True),
        grid_spec=pltpu.PrefetchScalarGridSpec(
            num_scalar_prefetch=1,
            grid=(4,),
            in_specs=[part, part, pl.BlockSpec(grads.shape, lambda i, p: (0, 0))],
            out_specs=[out] * 4,
            scratch_shapes=[pltpu.VMEM((D // 4, width), F32)],
        ),
        out_shape=[shape((4, D // 16, width), BF)] * 4,
        name="up_quarters",
        **params(),
    )(place, own, other, grads)


def down_quarters(place, own, other, active, out_sums):
    rows, width = own.shape[0], active.shape[1]
    shard = out_sums.shape[2]
    full = pl.BlockSpec((rows, D), lambda i, p: (0, 0))
    height = width // 16
    out = pl.BlockSpec((1, height + shard, D), lambda i, p: (level_of(i ^ p[3]), 0, 0))
    return pl.pallas_call(
        functools.partial(quarters_kernel, wide=False),
        grid_spec=pltpu.PrefetchScalarGridSpec(
            num_scalar_prefetch=1,
            grid=(4,),
            in_specs=[full, full, pl.BlockSpec((2 * rows, width // 4), lambda i, p: (0, i))]
            + [
                pl.BlockSpec((1, 1, shard, D), lambda i, p, flip=flip: (i, p[1] ^ flip, 0, 0))
                for flip in range(4)
            ],
            out_specs=[out] * 4,
            scratch_shapes=[pltpu.VMEM((width // 4, D), F32)],
        ),
        out_shape=[shape((4, height + shard, D), BF)] * 4,
        name="down_quarters",
        **params(),
    )(place, own, other, active, *([out_sums] * 4))


def middle_back_kernel(place_ref, gn_ref, gn_other_ref, mid_ref, cot_ref, t_ref, *refs):
    o_refs, w_refs, outs = refs[:4], refs[4:8], refs[8:]
    gm_ref, go_refs, grad_ref, s_ref, total = outs[0], outs[1:5], outs[5], outs[6], outs[7]
    step = pl.program_id(0)

    @pl.when(step == 0)
    def _():
        s_ref[...] = jnp.zeros_like(s_ref)
        total[...] = jnp.zeros_like(total)

    grad_two = gn_ref[...] + gn_other_ref[...]
    cot = cot_ref[...].astype(F32)
    unit, scale = norm_parts(mid_ref[...])
    grad_middle = cot + norm_back(unit, scale, grad_two, t_ref[6:7])
    gm_ref[...] = grad_middle
    grad_attn = grad_middle.astype(BF)
    s_ref[0:1] += column_sums(grad_attn.astype(F32))
    s_ref[1:2] += column_sums(grad_two * unit)
    s_ref[2:3] += column_sums(grad_two)
    s_ref[3:4] += column_sums(cot)
    for mask, o_ref, w_ref, go_ref in zip(MASK, o_refs, w_refs, go_refs):
        go_ref[...] = dot(grad_attn, w_ref[...], NT).astype(BF)
        start = pl.multiple_of((place_ref[0] ^ mask) * GROUP, GROUP)
        total[pl.ds(start, GROUP)] += dot(o_ref[...], grad_attn, TN)

    @pl.when(step == pl.num_programs(0) - 1)
    def _():
        grad_ref[...] = total[...].astype(BF)


def middle_back(place, gn, gn_other, mid, cot, vectors, mixed, weight, rows=256):
    count = mid.shape[0]
    full = pl.BlockSpec((rows, D), lambda i, p: (i, 0))
    part = pl.BlockSpec((rows, GROUP), lambda i, p: (i, 0))

    def whole(*dims):
        return pl.BlockSpec(dims, lambda i, p: (0, 0))

    return pl.pallas_call(
        middle_back_kernel,
        grid_spec=pltpu.PrefetchScalarGridSpec(
            num_scalar_prefetch=1,
            grid=(count // rows,),
            in_specs=[full, full, full, full, whole(16, D)]
            + mixed_specs(count, rows)
            + group_specs(),
            out_specs=[full] + [part] * 4 + [whole(D, D), whole(8, D)],
            scratch_shapes=[pltpu.VMEM((D, D), F32)],
        ),
        out_shape=[shape((count, D), F32)]
        + [shape((count, GROUP), BF)] * 4
        + [shape((D, D), BF), shape((8, D), F32)],
        name="middle_back",
        **params(),
    )(place, gn, gn_other, mid, cot, vectors, *mixed, mixed[2], *([weight] * 4))


def project_back_kernel(
    place_ref, n_ref, x_ref, w_ref, gq_ref, gk_ref, gv_ref, *refs, last, shard, four
):
    if last:
        late_ref, up_ref, squares_ref, ends_ref, total_start, sums_start, gn_ref, grad_ref, total, sums = refs
    else:
        gn_ref, total, sums = refs
    step = pl.program_id(0)

    @pl.when(step == 0)
    def _():
        if last:
            total[...] = total_start[...]
            sums[...] = sums_start[...]
        else:
            total[...] = jnp.zeros_like(total)
            sums[...] = jnp.zeros_like(sums)

    joined = jnp.concatenate([gq_ref[...], gk_ref[...], gv_ref[...]], axis=1)
    width = 3 * GROUP
    grad = dot(joined, w_ref[:, :width], NT)
    gn_ref[...] = grad.astype(BF)
    total[...] += dot(n_ref[...], joined, TN)
    unit, _ = norm_parts(x_ref[...].astype(F32))
    sums[0:1] += column_sums(grad * unit)
    sums[1:2] += column_sums(grad)
    sums[2:3, :width] += column_sums(joined.astype(F32))

    if last:

        @pl.when(step == pl.num_programs(0) - 1)
        def _():
            hot, part = bias_places(place_ref[0], shard)
            bias = sums[2:3, :width]
            spread = [
                dot(jnp.broadcast_to(jnp.where(part == j, bias, 0.0), (8, width)).astype(BF), hot, NT)
                for j in range(3)
            ]
            rows = [sums[0:1], sums[1:2], *[part[0:1] for part in spread]]
            rows += [late_ref[0:1], late_ref[1:2], late_ref[2:3]]
            wide = up_ref.shape[1]
            tall = 2 * wide * shard // D
            column = lax.broadcasted_iota(jnp.int32, (1, wide), 1)
            source = (column // tall * 2 + place_ref[0] % 2) * shard + column % shard
            which = column % tall // shard
            hot = lax.broadcasted_iota(jnp.int32, (D, wide), 0) == source
            ups = jnp.concatenate(
                [jnp.where(which == j, up_ref[0:1], 0.0) for j in range(tall // shard)]
                + [jnp.zeros((8 - tall // shard, wide), F32)],
                axis=0,
            )
            ups = dot(ups.astype(BF), jnp.where(hot, 1.0, 0.0).astype(BF), NT)
            rows += [ups[j : j + 1] for j in range(tall // shard)]
            rows += [late_ref[3:4]]
            for ref, j in ((squares_ref, 0), (squares_ref, 1), (squares_ref, 2), (ends_ref, 0), (ends_ref, 1)):
                rows += [jnp.broadcast_to(jnp.sum(ref[j : j + 1], axis=1, keepdims=True), (1, D))]
            rows += [jnp.zeros((128 - len(rows), D), F32)]
            vectors = jnp.concatenate(rows, axis=0).T.astype(BF)
            height = D // 8 if four else D
            for block in range(D // height):
                start = 0
                if four:
                    flip = block // 2 ^ place_ref[3]
                    start = pl.multiple_of(
                        (level_of(flip) * 2 + (block % 2 ^ place_ref[2])) * height, height
                    )
                here = slice(block * height, (block + 1) * height)
                grad_ref[pl.ds(start, height), :width] = total[here].astype(BF)
                grad_ref[pl.ds(start, height), width:] = vectors[here]


def project_back(
    place, normed, values, weight, parts, side, shard, four, before=None, rows=512
):
    count = normed.shape[0]
    half = count // 2
    width = 3 * GROUP
    last = before is not None

    def row_block(cols):
        return pl.BlockSpec((rows, cols), lambda i, p: (2 * i + side, 0))

    def whole(*dims):
        return pl.BlockSpec(dims, lambda i, p: (0, 0))

    in_specs = [row_block(D), row_block(D), whole(*weight.shape)] + [row_block(GROUP)] * 3
    operands = [normed, values, weight, *parts]
    out_specs, out_shape = [pl.BlockSpec((rows, D), lambda i, p: (i, 0))], [shape((half, D), BF)]
    totals = [whole(D, width), whole(8, D)]
    if last:
        in_specs += [whole(8, D), whole(8, before[1].shape[1]), whole(8, D), whole(8, D), *totals]
        operands += list(before)
        out_specs += [whole(*weight.shape)]
        out_shape += [shape(weight.shape, BF)]
        scratch = [pltpu.VMEM((D, width), F32), pltpu.VMEM((8, D), F32)]
    else:
        out_specs += totals
        out_shape += [shape((D, width), F32), shape((8, D), F32)]
        scratch = []
    return pl.pallas_call(
        functools.partial(project_back_kernel, last=last, shard=shard, four=four),
        grid_spec=pltpu.PrefetchScalarGridSpec(
            num_scalar_prefetch=1,
            grid=(half // rows,),
            in_specs=in_specs,
            out_specs=out_specs,
            scratch_shapes=scratch,
        ),
        out_shape=out_shape,
        name="project_back",
        **params(),
    )(place, *operands)


def first_back_kernel(x_ref, gm_ref, t_ref, a_ref, b_ref, c_ref, out_ref):
    grad = a_ref[...].astype(F32) + b_ref[...].astype(F32) + c_ref[...].astype(F32)
    unit, scale = norm_parts(x_ref[...].astype(F32))
    out_ref[...] = gm_ref[...] + norm_back(unit, scale, grad, t_ref[0:1])


def first_back(tokens, grad_middle, vectors, parts, rows=256):
    full = pl.BlockSpec((rows, D), lambda i: (i, 0))
    return pl.pallas_call(
        first_back_kernel,
        grid=(tokens.shape[0] // rows,),
        in_specs=[full, full, pl.BlockSpec((16, D), lambda i: (0, 0)), full, full, full],
        out_specs=full,
        out_shape=shape(tokens.shape, F32),
        name="first_back",
        **params(),
    )(tokens, grad_middle, vectors, *parts)


def per_device(
    tokens,
    positions,
    ln1_gain,
    ln1_shift,
    qkv_weight,
    qkv_bias,
    out_weight,
    out_bias,
    ln2_gain,
    ln2_shift,
    up_weight,
    up_bias,
    down_weight,
    down_bias,
    cotangent,
):
    rows = tokens.shape[0]
    outer = lax.axis_size("o")
    o, y, x, c = (lax.axis_index(name) for name in ALL)
    ctx = 2 * x + c
    four = outer == 4
    place = jnp.stack([ctx, 2 * y + x, y, o]).astype(jnp.int32)
    shard = ln1_gain.shape[0]
    blocks = D // shard
    half_blocks = blocks // 2
    tall = up_bias.shape[0]
    ff_half = tall * half_blocks

    vector_parts = (
        ln1_gain,
        ln1_shift,
        qkv_bias,
        out_bias,
        ln2_gain,
        ln2_shift,
        up_bias,
        down_bias,
    )
    n_vectors = sum(part.shape[0] for part in vector_parts) // shard
    packed = pack(qkv_weight, [part.reshape(1, -1) for part in vector_parts])
    packed, down_weight, out_weight, up_weight = tie(packed, down_weight, out_weight, up_weight)
    packed = lax.all_to_all(packed, ("x", "c"), 0, 0, tiled=True).reshape(4 * shard, -1)

    up_parts = up_weight.reshape(shard, half_blocks, 2, tall)

    def column_half(which):
        return lax.dynamic_index_in_dim(up_parts, which, 2, keepdims=False).reshape(shard, -1)

    upper = jnp.concatenate(by_place(c, column_half(c), swap(column_half(1 - c), "c")), axis=0)

    packed, tokens, positions, upper, out_weight = tie(
        packed, tokens, positions, upper, out_weight
    )
    packed_far = far_half(packed)
    place_rows = jnp.zeros((16, D), BF).at[:3, :rows].set(positions.astype(BF))
    sent = jnp.concatenate([tokens, place_rows], axis=0)
    from_x = swap(sent, "x")
    out_far = far_half(out_weight)
    packed_far, out_far, packed, down_weight, out_weight = tie(
        packed_far, out_far, packed, down_weight, out_weight
    )
    lower_far = far_half(down_weight)
    out = near_half(out_weight, out_far)
    packed_pair, packed_near = near_half(packed, packed_far)
    packed_y = swap(packed_pair, "y")
    packed_near, packed_y, from_x, upper, lower_far, out = tie(
        packed_near, packed_y, from_x, upper, lower_far, out
    )
    out = all_blocks(out)
    out_x = swap(out, "x")
    if four:
        pieces = (packed_pair, packed_y, packed_near, swap(packed_near, "y"))
    else:
        pieces = (jnp.stack(by_place(y, packed_pair, packed_y), axis=1).reshape(1, D, -1),)
    lower = near_half(down_weight, lower_far)
    upper_far = far_half(upper)
    from_c = swap(jnp.stack([sent, from_x]), "c")
    clip_rows = jnp.concatenate(
        [tokens, from_x[:rows], from_c[0, :rows], from_c[1, :rows]], axis=0
    )
    places = jnp.concatenate(
        [
            positions.astype(F32),
            from_x[rows : rows + 3, :rows].astype(F32),
            from_c[0, rows : rows + 3, :rows].astype(F32),
            from_c[1, rows : rows + 3, :rows].astype(F32),
        ],
        axis=1,
    )
    cosine, sine = rotary_tables(places, PAIR)
    pieces, lower, out_x, upper, upper_far, clip_rows, cosine, sine = tie(
        pieces, lower, out_x, upper, upper_far, clip_rows, cosine, sine
    )
    lower = all_blocks(lower)
    out_y = swap(jnp.stack([out, out_x]), "y")
    lower_x, lower_y = swap(lower, "x"), swap(lower, "y")
    upper = near_half(upper, upper_far)
    normed, q, k, v, vectors, gathered = project(place, clip_rows, pieces, cosine, sine, shard)

    q, upper, out_y = tie(q, upper, out_y)
    upper = all_blocks(upper)
    upper_x, upper_y = swap(upper, "x"), swap(upper, "y")
    cotangent_other = swap(cotangent, "c")
    mixed_far, wide_far, logs_far = attend(q, k, v, 1)
    if four:
        out_own = jnp.stack([out, out_x, out_y[0], out_y[1]])
        out_sources = (out_own, swap(out_own, "c"))
    else:
        out_half = jnp.stack(place_four(y, x, (out, out_x, out_y[0], out_y[1])), axis=1)
        out_half = out_half.reshape(half_blocks, shard, D)
        out_half = jnp.stack(by_place(c, out_half, swap(out_half, "c")), axis=1)
        out_sources = (out_half.reshape(1, 1, D, D), out_half.reshape(1, 1, D, D))
    mixed_far, lower_x, lower_y, out_sources, cotangent_other, q = tie(
        mixed_far, lower_x, lower_y, out_sources, cotangent_other, q
    )
    came_x = swap(mixed_far, "x")
    lower_xy = swap(lower_x, "y")
    mixed_near, wide_near, logs_near = attend(q, k, v, 0)
    mixed_near, came_x, upper_y, upper_x = tie(mixed_near, came_x, upper_y, upper_x)
    upper_xy = swap(upper_y, "x")
    came_c = swap(jnp.concatenate([mixed_near[rows:], came_x[rows:]], axis=0), "c")
    mixed = (mixed_near, came_x, came_c)
    mid, normed_two, squares, out_full = middle(place, tokens, vectors, mixed, out_sources, four)

    normed_other = swap(normed_two, "c")
    if four:
        up_pieces = (upper, upper_x, upper_y, upper_xy)
        down_pieces = (lower, lower_x, lower_y, lower_xy)
    else:
        upper = jnp.stack(place_four(y, x, (upper, upper_x, upper_y, upper_xy)), axis=1)
        up_pieces = (upper.reshape(1, D, ff_half),)
        lower = jnp.stack(place_four(y, x, (lower, lower_x, lower_y, lower_xy)), axis=1)
        down_pieces = (lower.reshape(1, ff_half, D),)
    active, grad_up, up_bias_grad, gn, gn_sent, mlp, mlp_sent = hidden(
        place,
        vectors,
        normed_two,
        normed_other,
        cotangent,
        cotangent_other,
        up_pieces,
        down_pieces,
        shard,
        tall,
    )
    gn_came = swap(gn_sent, "c")
    mlp_came = swap(mlp_sent, "c")

    def quarter(values, flip):
        parts = values.reshape(outer, 4, -1, values.shape[-1])
        return lax.dynamic_index_in_dim(parts, (2 * y + x) ^ flip, 1, keepdims=False)

    if four:
        ups = tuple(up_quarters(place, normed_two, normed_other, grad_up))
    else:
        normed_pair = jnp.concatenate([normed_two, normed_other], axis=0)
        up_grad = dot(normed_pair, grad_up, TN).astype(BF)
        ups = tuple(quarter(up_grad, flip) for flip in range(4))
    gn_came, ups = tie(gn_came, ups)
    upper_passed = swap(ups[3], "y")
    grad_middle, go_own, go_x, go_c, go_xc, out_grad, sums = middle_back(
        place, gn, gn_came, mid, cotangent, vectors, mixed, out_full
    )
    go_came_c = swap(jnp.concatenate([go_c, go_xc], axis=0), "c")
    out_grad = out_grad.reshape(half_blocks, 2, shard, D)
    out_sent = lax.dynamic_index_in_dim(out_grad, 1 - c, 1, keepdims=False)
    out_kept = lax.dynamic_index_in_dim(out_grad, c, 1, keepdims=False)
    out_came = swap(out_sent, "c")
    mlp_came, out_sent = tie(mlp_came, out_sent)
    final_low, ends = finish(mid, mlp, mlp_came, vectors, n_vectors - 1)
    go_came_c, out_came, final_low, active = tie(go_came_c, out_came, final_low, active)
    go_came_x = swap(jnp.concatenate([go_x, go_came_c[rows:]], axis=0), "x")
    out_sums = (out_kept + out_came).reshape(outer, 4, shard, D)
    if four:
        downs = tuple(down_quarters(place, cotangent, cotangent_other, active, out_sums))
    else:
        cotangent_pair = jnp.concatenate([cotangent, cotangent_other], axis=0)
        down_grad = dot(active, cotangent_pair, TN).astype(BF)
        lower_grad = jnp.concatenate(
            [down_grad.reshape(outer * 4, tall, D), out_sums.reshape(outer * 4, shard, D)], axis=1
        )
        downs = tuple(quarter(lower_grad, flip) for flip in range(4))

    downs, go_came_x, go_own, go_came_c, upper_passed, ups = tie(
        downs, go_came_x, go_own, go_came_c, upper_passed, ups
    )
    lower_passed = swap(downs[3], "x")
    upper_kept = swap(ups[2], "y")
    first = attend_back(
        q, k, v, go_own, go_came_c, 0, wide_near, logs_near, cosine, sine, 0
    )
    lower_passed, upper_kept, first, downs, ups = tie(lower_passed, upper_kept, first, downs, ups)
    upper_second = swap(ups[1] + upper_passed, "x")
    lower_second = swap(downs[2] + lower_passed, "y")
    parts = attend_back(
        q, k, v, go_came_x, go_came_x, 1, wide_far, logs_far, cosine, sine, 1, before=first
    )
    upper_second, lower_second, parts, downs = tie(upper_second, lower_second, parts, downs)
    lower_kept = swap(downs[1], "x")
    upper_sum = near_sums(ups[0], upper_second, upper_kept)

    gn_far, total, totals = project_back(
        place, normed, clip_rows, gathered, parts, 1, shard, four
    )
    gn_far, upper_sum, normed = tie(gn_far, upper_sum, normed)
    gn_far_came = swap(gn_far[rows:], "c")
    upper_grad = far_sums(upper_sum).astype(BF).reshape(2, shard, -1)
    gn_near, last = project_back(
        place,
        normed,
        clip_rows,
        gathered,
        parts,
        0,
        shard,
        four,
        before=(sums, up_bias_grad, squares, ends, total, totals),
    )
    gn_far_came, gn_near, last, lower_kept, upper_grad = tie(
        gn_far_came, gn_near, last, lower_kept, upper_grad
    )

    cut = 512
    last = last.reshape(outer, 2, 4 * shard, -1)

    def over_y(values):
        axis = values.ndim - 3
        if four:
            kept, sent = (lax.index_in_dim(values, i, axis, keepdims=False) for i in (0, 1))
        else:
            kept = lax.dynamic_index_in_dim(values, y, axis, keepdims=False)
            sent = lax.dynamic_index_in_dim(values, 1 - y, axis, keepdims=False)
        return kept.astype(F32) + swap(sent.astype(BF), "y").astype(F32)

    high = near_sums(last[..., cut:])
    low = over_y(last[..., :cut]).astype(BF)
    gn_x = swap(gn_far[:rows] + gn_far_came, "x")
    gn_near_came = swap(gn_near[rows:], "c")
    low, high, downs, lower_second, lower_kept = tie(low, high, downs, lower_second, lower_kept)
    low = near_sums(low)
    high = far_sums(high)
    lower_sum = near_sums(downs[0], lower_second, lower_kept)
    low, high = tie(low, high)
    low = far_sums(low)
    high = over_y(high)
    upper_kept = lax.dynamic_index_in_dim(upper_grad, c, 0, keepdims=False)
    upper_came = swap(lax.dynamic_index_in_dim(upper_grad, 1 - c, 0, keepdims=False), "c")
    low, high, lower_sum = tie(low, high, lower_sum)
    lower_grad = far_sums(lower_sum)
    last = jnp.concatenate([low.astype(BF), high.astype(BF)], axis=1)
    last = lax.all_to_all(last.reshape(4, shard, -1), ("x", "c"), 0, 0, tiled=True)
    input_grad = first_back(
        tokens, grad_middle, vectors, (gn_near[:rows], gn_near_came, gn_x)
    )
    upper_pair = by_place(c, upper_kept, upper_came)
    up_weight_grad = jnp.stack(
        [part.reshape(shard, half_blocks, tall) for part in upper_pair], axis=2
    )
    last = last.astype(F32)
    qkv_weight_grad = last[:, :, : 3 * GROUP].reshape(4, shard, 3, GROUP).transpose(1, 2, 0, 3)
    vector_grads = jnp.sum(last[:, :, 3 * GROUP : 3 * GROUP + n_vectors + 5], axis=0).T
    entry_count = rows * lax.axis_size(ALL) * D
    norm_stats = jnp.sqrt(vector_grads[n_vectors:, 0] / entry_count)

    return (
        final_low,
        input_grad,
        vector_grads[0],
        vector_grads[1],
        qkv_weight_grad.reshape(shard, 3 * D),
        vector_grads[2:5].reshape(-1),
        lower_grad[tall:],
        vector_grads[5],
        vector_grads[6],
        vector_grads[7],
        up_weight_grad.reshape(shard, -1).astype(F32),
        vector_grads[8 : n_vectors - 1].reshape(-1),
        lower_grad[:tall],
        vector_grads[n_vectors - 1],
        norm_stats,
    )


def solution(mesh):
    fine = Mesh(mesh.devices.reshape(-1, 2, 2, 2), ALL)
    rows, vector, whole = P(ALL, None), P(ALL), P()
    in_specs = (
        rows,
        P(None, ALL),
        vector,
        vector,
        rows,
        vector,
        rows,
        vector,
        vector,
        vector,
        rows,
        vector,
        rows,
        vector,
        rows,
    )
    out_specs = (
        rows,
        rows,
        vector,
        vector,
        rows,
        vector,
        rows,
        vector,
        vector,
        vector,
        rows,
        vector,
        rows,
        vector,
        whole,
    )
    return jax.shard_map(
        per_device, mesh=fine, in_specs=in_specs, out_specs=out_specs, check_vma=False
    )
```

```python
import functools
import math

import jax
import jax.numpy as jnp
from jax import lax
from jax.experimental import pallas as pl
from jax.experimental.pallas import tpu as pltpu
from jax.sharding import Mesh
from jax.sharding import PartitionSpec as P

D = 1024
HD = 64
GAP = HD // 6
PAIR = 2 * HD
GROUP = D // 4
EPSILON = 1e-06
BF = jnp.bfloat16
F32 = jnp.float32
ALL = ("o", "y", "x", "c")
SWAP = ((0, 1), (1, 0))
DIAGONAL = ((0, 3), (1, 2), (2, 1), (3, 0))
NT = (((1,), (1,)), ((), ()))
NN = (((1,), (0,)), ((), ()))
TN = (((0,), (0,)), ((), ()))
VMEM_LIMIT = 58 * 2**20
VMEM_MOST = 63 * 2**20
SMALL = pl.CostEstimate(flops=10**6, bytes_accessed=2**16, transcendentals=0)
MASK = (0, 2, 1, 3)


def dot(left, right, dims=NN):
    return lax.dot_general(left, right, dims, preferred_element_type=F32)


def swap(values, axis):
    return lax.ppermute(values, axis, SWAP)


def tie(*values):
    return lax.optimization_barrier(values)


def by_place(flag, own, other):
    return jnp.where(flag == 0, own, other), jnp.where(flag == 0, other, own)


def place_four(high, low, parts):
    first = by_place(low, parts[0], parts[1])
    second = by_place(low, parts[2], parts[3])
    even = by_place(high, first[0], second[0])
    odd = by_place(high, first[1], second[1])
    return even[0], odd[0], even[1], odd[1]


def far(values):
    return lax.ppermute(values, "o", [(i, i ^ 2) for i in range(4)])


def near(values):
    return lax.ppermute(values, "o", [(i, i ^ 1) for i in range(4)])


def level_place(own, level):
    return own ^ (level % 2 * 2 + level // 2)


def far_half(values):
    if lax.axis_size("o") != 4:
        return lax.all_gather(values, "o", axis=0, tiled=False)
    return far(values)


def near_half(values, came):
    if lax.axis_size("o") != 4:
        return came, came
    pair = jnp.stack([values, came])
    return pair, near(pair)


def all_blocks(halves):
    if lax.axis_size("o") != 4:
        return halves[0]
    return jnp.concatenate(halves, axis=0)


def near_sums(*terms):
    if lax.axis_size("o") != 4:
        return sum(terms)
    kept = sum(term[:2].astype(F32) for term in terms)
    return kept, near(sum(term[2:].astype(F32) for term in terms).astype(BF))


def far_sums(values, *earlier):
    if lax.axis_size("o") != 4:
        return lax.psum_scatter(values, "o", scatter_dimension=0, tiled=False).astype(F32)
    kept, came = values
    sums = kept + came.astype(F32)
    came = far(sums[1].astype(BF))
    if earlier:
        came = tie(came, *earlier)[0]
    return sums[0] + came.astype(F32)


def norm_parts(values):
    average = jnp.mean(values, axis=-1, keepdims=True)
    centred = values - average
    spread = jnp.mean(centred * centred, axis=-1, keepdims=True)
    scale = lax.rsqrt(spread + EPSILON)
    return centred * scale, scale


def norm_back(unit, scale, grad, gain):
    scaled = grad * gain
    return scale * (
        scaled
        - jnp.mean(scaled, axis=-1, keepdims=True)
        - unit * jnp.mean(scaled * unit, axis=-1, keepdims=True)
    )


def rotary_tables(places, width):
    column = jnp.arange(width) % HD
    segment = column // (2 * GAP)
    within = column % (2 * GAP)
    freq_index = (within % GAP).astype(F32)
    frequency = jnp.power(10000.0, -freq_index / GAP)
    angles = jnp.zeros((places.shape[1], width), F32)
    for axis_num in range(3):
        angles = (
            angles
            + places[axis_num][:, None] * jnp.where(segment == axis_num, frequency, 0.0)[None, :]
        )
    rotated = segment < 3
    return jnp.where(rotated, jnp.cos(angles), 1.0), jnp.where(rotated, jnp.sin(angles), 0.0)


def shifted(values, leading):
    ahead = pltpu.roll(values, PAIR - GAP, 1)
    behind = pltpu.roll(values, GAP, 1)
    return jnp.where(leading, -ahead, behind)


def leading_lanes():
    lane = lax.broadcasted_iota(jnp.int32, (1, PAIR), 1)
    return lane % HD % (2 * GAP) < GAP


def column_sums(values):
    return jnp.sum(values, axis=0, keepdims=True)


def params(aliases=None, limit=VMEM_LIMIT):
    return dict(
        compiler_params=pltpu.CompilerParams(vmem_limit_bytes=limit),
        cost_estimate=SMALL,
        input_output_aliases=aliases or {},
    )


def shape(dims, kind):
    return jax.ShapeDtypeStruct(dims, kind)


def pack_kernel(w_ref, *refs):
    vectors, out_ref = refs[:-1], refs[-1]
    shard = w_ref.shape[0]
    rows = []
    for ref in vectors:
        values = ref[...].astype(F32)
        rows += [values[:, low : low + shard] for low in range(0, values.shape[1], shard)]
    columns = jnp.concatenate(rows + [jnp.zeros((128 - len(rows), shard), F32)], axis=0).T
    for place in range(4):
        for part in range(3):
            start = part * D + place * GROUP
            out_ref[place, :, part * GROUP : (part + 1) * GROUP] = w_ref[:, start : start + GROUP]
        out_ref[place, :, 3 * GROUP :] = columns.astype(BF)


def pack(weight, vectors):
    return pl.pallas_call(
        pack_kernel,
        out_shape=shape((4, weight.shape[0], 3 * GROUP + 128), BF),
        name="pack",
        **params(),
    )(weight, *vectors)


def bias_places(place, shard):
    column = lax.broadcasted_iota(jnp.int32, (1, 3 * GROUP), 1)
    target = column // GROUP * D + place * GROUP + column % GROUP
    source = target // (3 * shard) * shard + target % shard
    hot = lax.broadcasted_iota(jnp.int32, (D, 3 * GROUP), 0) == source
    return jnp.where(hot, 1.0, 0.0).astype(BF), target % (3 * shard) // shard


def load_blocks(sources, target, semaphores):
    found = []
    for source, index, place in sources:
        block = source if isinstance(index, slice) else source.at[index]
        height = block.shape[0]
        start = pl.multiple_of(place * height, height)
        found.append(
            pltpu.make_async_copy(
                block, target.at[pl.ds(start, height)], semaphores.at[len(found)]
            )
        )
    return found


def piece_blocks(arrays, place):
    if len(arrays) == 1:
        return [(arrays[0], 0, 0)]
    return [
        (source, level, level_place(place[3], level) * 4 + (place[1] ^ flip))
        for flip, source in enumerate(arrays)
        for level in range(4)
    ]


def project_kernel(place_ref, x_ref, cos_ref, sin_ref, *refs, shard, pieces):
    sources, refs = refs[:pieces], refs[pieces:]
    n_ref, q_ref, k_ref, v_ref, t_ref, w_ref, b_ref, semaphores = refs

    @pl.when(pl.program_id(0) == 0)
    def _():
        if pieces == 1:
            blocks = [(sources[0], 0, 0)]
        else:
            blocks = [
                (
                    source,
                    level,
                    (level_place(place_ref[3], level) ^ (piece // 2)) * 2
                    + (place_ref[2] ^ (piece % 2)),
                )
                for piece, source in enumerate(sources)
                for level in range(2)
            ]
        copies = load_blocks(blocks, w_ref, semaphores)
        for copy in copies:
            copy.start()
        for copy in copies:
            copy.wait()
        t_ref[...] = w_ref[:, 3 * GROUP :].astype(F32).T[: t_ref.shape[0]]
        hot, part = bias_places(place_ref[0], shard)
        found = dot(t_ref[...].astype(BF), hot)
        bias = jnp.where(part == 0, found[2:3], jnp.where(part == 1, found[3:4], found[4:5]))
        b_ref[...] = jnp.broadcast_to(bias, b_ref.shape)

    unit, _ = norm_parts(x_ref[...].astype(F32))
    normed = (unit * t_ref[0:1] + t_ref[1:2]).astype(BF)
    n_ref[...] = normed
    joined = dot(normed, w_ref[:, : 3 * GROUP]) + b_ref[0:1]
    cosine, sine, leading = cos_ref[...], sin_ref[...], leading_lanes()
    for ref, start, factor in ((q_ref, 0, 1.0 / math.sqrt(HD)), (k_ref, GROUP, 1.0)):
        for low in range(0, GROUP, PAIR):
            part = joined[:, start + low : start + low + PAIR]
            turned = part * cosine + shifted(part, leading) * sine
            ref[:, low : low + PAIR] = (turned * factor).astype(BF)
    v_ref[...] = joined[:, 2 * GROUP :].astype(BF)


def project(place, values, pieces, cosine, sine, shard, rows=512):
    count = values.shape[0]
    width = pieces[0].shape[-1]

    def part(cols):
        return pl.BlockSpec((rows, cols), lambda i, p: (i, 0))

    def whole(*dims):
        return pl.BlockSpec(dims, lambda i, p: (0, 0))

    return pl.pallas_call(
        functools.partial(project_kernel, shard=shard, pieces=len(pieces)),
        grid_spec=pltpu.PrefetchScalarGridSpec(
            num_scalar_prefetch=1,
            grid=(count // rows,),
            in_specs=[part(D), part(PAIR), part(PAIR)]
            + [pl.BlockSpec(memory_space=pl.ANY)] * len(pieces),
            out_specs=[part(D), part(GROUP), part(GROUP), part(GROUP), whole(16, D), whole(D, width)],
            scratch_shapes=[
                pltpu.VMEM((8, 3 * GROUP), F32),
                pltpu.SemaphoreType.DMA((len(pieces) * pieces[0].shape[0],)),
            ],
        ),
        out_shape=[
            shape((count, D), BF),
            shape((count, GROUP), BF),
            shape((count, GROUP), BF),
            shape((count, GROUP), BF),
            shape((16, D), F32),
            shape((D, width), BF),
        ],
        name="project",
        **params(),
    )(place, values, cosine, sine, *pieces)


def attend_kernel(q_ref, k_ref, v_ref, *refs):
    o_ref, wide_ref, lse_ref = refs[-3:]
    q, k, v = q_ref[...], k_ref[...], v_ref[...]
    lane = lax.broadcasted_iota(jnp.int32, (1, PAIR), 1)
    mixed, logs = [], []
    for head in range(2):
        mine = (lane < HD) if head == 0 else (lane >= HD)
        scores = dot(jnp.where(mine, q, 0), k, NT)
        top = jnp.max(scores, axis=1, keepdims=True)
        weight = jnp.exp(scores - top)
        total = jnp.sum(weight, axis=1, keepdims=True)
        mixed.append(dot(weight.astype(BF), v) / total)
        logs.append(top + jnp.log(total))
    out = jnp.where(lane < HD, mixed[0], mixed[1])
    o_ref[...] = out.astype(BF)
    wide_ref[...] = out
    lse_ref[...] = jnp.where(lane < HD, logs[0], logs[1])


def attend(q, k, v, side, pair=None, before=None, rows=256):
    count = q.shape[0]
    half = count // 2
    per = count // 4 // rows
    pairs = GROUP // PAIR if pair is None else 1
    first = 0 if pair is None else pair

    def block(i):
        return i // per * 2 * per + side * per + i % per

    full = pl.BlockSpec((count, PAIR), lambda j, i: (0, first + j))
    out = pl.BlockSpec((rows, PAIR), lambda j, i: (i, first + j))
    before = list(before or ())
    return pl.pallas_call(
        attend_kernel,
        grid=(pairs, half // rows),
        in_specs=[pl.BlockSpec((rows, PAIR), lambda j, i: (block(i), first + j)), full, full]
        + [pl.BlockSpec(memory_space=pl.ANY)] * len(before),
        out_specs=[out, out, out],
        out_shape=[shape((half, GROUP), BF), shape((half, GROUP), F32), shape((half, GROUP), F32)],
        name="attend",
        **params({3: 0, 4: 1, 5: 2} if before else None),
    )(q, k, v, *before)


def attend_back_kernel(
    q_ref, go_ref, go_other_ref, wide_ref, lse_ref, k_ref, v_ref, cos_ref, sin_ref, *refs, last, block
):
    step, rows = pl.program_id(1), q_ref.shape[0]
    if last:
        k_start, v_start, _, gq_ref, gk_ref, gv_ref, k_sum, v_sum = refs
    else:
        gq_ref, k_sum, v_sum = refs

    @pl.when(step == 0)
    def _():
        if last:
            k_sum[...] = k_start[...]
            v_sum[...] = v_start[...]
        else:
            k_sum[...] = jnp.zeros_like(k_sum)
            v_sum[...] = jnp.zeros_like(v_sum)

    q, k, v, lse = q_ref[...], k_ref[...], v_ref[...], lse_ref[...]
    go = jnp.where(step < pl.num_programs(1) // 2, go_ref[...], go_other_ref[...])
    lane = lax.broadcasted_iota(jnp.int32, (1, PAIR), 1)
    leading = leading_lanes()
    product = go.astype(F32) * wide_ref[...]
    grads = []
    for head in range(2):
        mine = (lane < HD) if head == 0 else (lane >= HD)
        q_head, go_head = jnp.where(mine, q, 0), jnp.where(mine, go, 0)
        inner = jnp.sum(jnp.where(mine, product, 0.0), axis=1, keepdims=True)
        weight = jnp.exp(dot(q_head, k, NT) - lse[:, HD * head : HD * head + 1])
        pull = (weight * (dot(go_head, v, NT) - inner)).astype(BF)
        grads.append(dot(pull, k))
        k_sum[...] += dot(q_head.T, pull)
        v_sum[...] += dot(go_head.T, weight.astype(BF))
    grad = jnp.where(lane < HD, grads[0], grads[1])
    here = pl.ds(pl.multiple_of(block(step) * rows, rows), rows)
    grad = grad * cos_ref[here] - shifted(grad * sin_ref[here], leading)
    gq_ref[...] = (grad * (1.0 / math.sqrt(HD))).astype(BF)

    if last:

        @pl.when(step == pl.num_programs(1) - 1)
        def _():
            grad = k_sum[...].T
            grad = grad * cos_ref[...] - shifted(grad * sin_ref[...], leading)
            gk_ref[...] = grad.astype(BF)
            gv_ref[...] = v_sum[...].T.astype(BF)


def attend_back(q, k, v, go, go_other, wide, lse, cosine, sine, side, before=None, rows=256):
    count = q.shape[0]
    half = count // 2
    per = count // 4 // rows
    last = before is not None

    def block(i):
        return i // per * 2 * per + side * per + i % per

    part = pl.BlockSpec((rows, PAIR), lambda pair, i: (block(i), pair))
    own = pl.BlockSpec((rows, PAIR), lambda pair, i: (i, pair))
    full = pl.BlockSpec((count, PAIR), lambda pair, i: (0, pair))
    table = pl.BlockSpec((count, PAIR), lambda pair, i: (0, 0))
    turned = pl.BlockSpec((PAIR, count), lambda pair, i: (pair, 0))
    sums = shape((GROUP, count), F32)
    grad = shape((count, GROUP), BF)
    low = pl.BlockSpec((rows, PAIR), lambda pair, i: (jnp.minimum(i, per - 1), pair))
    high = pl.BlockSpec((rows, PAIR), lambda pair, i: (jnp.maximum(i - per, 0), pair))
    in_specs = [part, low, high, own, own, full, full, table, table]
    operands = [q, go, go_other, wide, lse, k, v, cosine, sine]
    if last:
        in_specs += [turned, turned, pl.BlockSpec(memory_space=pl.ANY)]
        operands += [before[1], before[2], before[0]]
        out_specs, out_shape = [part, full, full], [grad, grad, grad]
        scratch = [pltpu.VMEM((PAIR, count), F32)] * 2
    else:
        out_specs, out_shape, scratch = [part, turned, turned], [grad, sums, sums], []
    return pl.pallas_call(
        functools.partial(attend_back_kernel, last=last, block=block),
        grid=(GROUP // PAIR, half // rows),
        in_specs=in_specs,
        out_specs=out_specs,
        out_shape=out_shape,
        scratch_shapes=scratch,
        name="attend_back",
        **params({11: 0} if last else None),
    )(*operands)


def middle_kernel(place_ref, x_ref, t_ref, *refs, four):
    o_refs, sources, refs = refs[:4], refs[4:6], refs[6:]
    mid_ref, n_ref, s_ref, w_ref, semaphores = refs

    @pl.when(pl.program_id(0) == 0)
    def _():
        s_ref[...] = jnp.zeros_like(s_ref)
        if four:
            blocks = [
                (
                    source.at[flip],
                    level,
                    (level_place(place_ref[3], level) * 4 + (place_ref[1] ^ flip)) * 2
                    + (place_ref[0] % 2 ^ other),
                )
                for other, source in enumerate(sources)
                for flip in range(4)
                for level in range(4)
            ]
        else:
            blocks = [(sources[0].at[0], 0, 0)]
        copies = load_blocks(blocks, w_ref, semaphores)
        for copy in copies:
            copy.start()
        for copy in copies:
            copy.wait()

    x = x_ref[...].astype(F32)
    attn = t_ref[5:6]
    for mask, o_ref in zip(MASK, o_refs):
        start = pl.multiple_of((place_ref[0] ^ mask) * GROUP, GROUP)
        attn = attn + dot(o_ref[...], w_ref[pl.ds(start, GROUP)])
    mid = x + attn
    mid_ref[...] = mid
    unit, _ = norm_parts(mid)
    n_ref[...] = (unit * t_ref[6:7] + t_ref[7:8]).astype(BF)
    s_ref[0:1] += column_sums(x * x)
    s_ref[1:2] += column_sums(attn * attn)
    s_ref[2:3] += column_sums(mid * mid)


def group_specs():
    return [
        pl.BlockSpec((GROUP, D), lambda i, p, mask=mask: (p[0] ^ mask, 0)) for mask in MASK
    ]


def mixed_specs(count, rows):
    first = pl.BlockSpec((rows, GROUP), lambda i, p: (i, 0))
    second = pl.BlockSpec((rows, GROUP), lambda i, p: (i + count // rows, 0))
    return [first, first, first, second]


def middle(place, tokens, vectors, mixed, sources, four, rows=256):
    count = tokens.shape[0]
    full = pl.BlockSpec((rows, D), lambda i, p: (i, 0))

    def whole(*dims):
        return pl.BlockSpec(dims, lambda i, p: (0, 0))

    return pl.pallas_call(
        functools.partial(middle_kernel, four=four),
        grid_spec=pltpu.PrefetchScalarGridSpec(
            num_scalar_prefetch=1,
            grid=(count // rows,),
            in_specs=[full, whole(16, D)]
            + mixed_specs(count, rows)
            + [pl.BlockSpec(memory_space=pl.ANY)] * 2,
            out_specs=[full, full, whole(8, D), whole(D, D)],
            scratch_shapes=[pltpu.SemaphoreType.DMA((32,))],
        ),
        out_shape=[
            shape((count, D), F32),
            shape((count, D), BF),
            shape((8, D), F32),
            shape((D, D), BF),
        ],
        name="middle",
        **params(),
    )(place, tokens, vectors, *mixed, mixed[2], *sources)


def hidden_bias_kernel(place_ref, t_ref, out_ref, *, shard, tall):
    chunk = out_ref.shape[1]
    column = lax.broadcasted_iota(jnp.int32, (1, chunk), 1) + pl.program_id(0) * chunk
    source = (column // tall * 2 + place_ref[0] % 2) * shard + column % shard
    which = column % tall // shard
    hot = lax.broadcasted_iota(jnp.int32, (D, chunk), 0) == source
    found = dot(t_ref[...].astype(BF), jnp.where(hot, 1.0, 0.0).astype(BF))
    bias = jnp.zeros((1, chunk), F32)
    for row in range(tall // shard):
        bias = jnp.where(which == row, found[8 + row : 9 + row], bias)
    out_ref[...] = jnp.broadcast_to(bias, out_ref.shape)


def hidden_bias(place, vectors, width, shard, tall, chunk=512):
    return pl.pallas_call(
        functools.partial(hidden_bias_kernel, shard=shard, tall=tall),
        grid_spec=pltpu.PrefetchScalarGridSpec(
            num_scalar_prefetch=1,
            grid=(width // chunk,),
            in_specs=[pl.BlockSpec((16, D), lambda i, p: (0, 0))],
            out_specs=pl.BlockSpec((8, chunk), lambda i, p: (0, i)),
        ),
        out_shape=shape((8, width), F32),
        name="hidden_bias",
        **params(),
    )(place, vectors)


def hidden_kernel(place_ref, bias_ref, *refs, pieces):
    rows_in, refs = refs[:4], refs[4:]
    up_pieces, down_pieces, refs = refs[:pieces], refs[pieces : 2 * pieces], refs[2 * pieces :]
    b_ref, gn_ref, gn_other_ref, mlp_ref, mlp_other_ref = refs[:5]
    up_outs, down_outs = refs[5 : 5 + pieces], refs[5 + pieces : 5 + 2 * pieces]
    up, down, normed, cot, gn_sum, mlp_sum, up_total, down_total, *semaphores = refs[5 + 2 * pieces :]
    step = pl.program_id(0)
    chunk = bias_ref.shape[1]
    rows = gn_ref.shape[0]
    up_sem, down_sem, normed_sem, cot_sem = semaphores

    @pl.when(step == 0)
    def _():
        copies = load_blocks([(ref, slice(None), i) for i, ref in enumerate(rows_in[:2])], normed, normed_sem)
        copies += load_blocks(piece_blocks(up_pieces, place_ref), up, up_sem)
        copies += load_blocks([(ref, slice(None), i) for i, ref in enumerate(rows_in[2:])], cot, cot_sem)
        copies += load_blocks(piece_blocks(down_pieces, place_ref), down, down_sem)
        for copy in copies:
            copy.start()
        gn_sum[...] = jnp.zeros_like(gn_sum)
        mlp_sum[...] = jnp.zeros_like(mlp_sum)
        for copy in copies:
            copy.wait()

    here = pl.ds(pl.multiple_of(step * chunk, chunk), chunk)
    up_part, down_part = up[:, here], down[here, :]
    upward = dot(normed[...], up_part) + bias_ref[0:1]
    grad_active = dot(cot[...], down_part, NT)
    bell = 0.5 * (1.0 + lax.erf(upward * 0.7071067811865476))
    active = (upward * bell).astype(BF)
    slope = bell + upward * jnp.exp(-0.5 * upward * upward) * (1.0 / math.sqrt(2.0 * math.pi))
    grad_up = (grad_active * slope).astype(BF)
    b_ref[...] = jnp.broadcast_to(column_sums(grad_up.astype(F32)), b_ref.shape)
    gn_sum[...] += dot(grad_up, up_part, NT)
    mlp_sum[...] += dot(active, down_part)
    up_grad = dot(normed[...], grad_up, TN)
    down_grad = dot(active, cot[...], TN)
    if pieces == 1:
        up_outs[0][...] = up_grad.astype(BF)
        down_outs[0][...] = down_grad.astype(BF)
    else:
        up_total[...] = up_grad
        down_total[...] = down_grad
        for flip in range(4):
            for place in range(4):
                start = pl.multiple_of((place * 4 + (place_ref[1] ^ flip)) * (D // 16), D // 16)
                level = level_of(place ^ place_ref[3])
                up_outs[flip][level] = up_total[pl.ds(start, D // 16)].astype(BF)
            start = pl.multiple_of((place_ref[1] ^ flip) * (chunk // 4), chunk // 4)
            down_outs[flip][0] = down_total[pl.ds(start, chunk // 4)].astype(BF)

    @pl.when(step == pl.num_programs(0) - 1)
    def _():
        gn_ref[...] = gn_sum[:rows]
        mlp_ref[...] = mlp_sum[:rows]
        gn_other_ref[...] = gn_sum[rows:].astype(BF)
        mlp_other_ref[...] = mlp_sum[rows:].astype(BF)


def hidden(place, bias, own, other, cot, cot_other, up_pieces, down_pieces, extra):
    rows = own.shape[0]
    width = up_pieces[0].shape[-1]
    pieces = len(up_pieces)
    blocks = pieces * up_pieces[0].shape[0]
    chunk = width // 4

    def whole(*dims):
        return pl.BlockSpec(dims, lambda i, p: (0, 0))

    if pieces == 1:
        grad_specs = [
            pl.BlockSpec((D, chunk), lambda i, p: (0, i)),
            pl.BlockSpec((chunk, D), lambda i, p: (i, 0)),
        ]
        grad_shapes = [shape((D, width), BF), shape((width, D), BF)]
    else:
        grad_specs = [pl.BlockSpec((4, D // 16, chunk), lambda i, p: (0, 0, i))] * 4
        grad_specs += [
            pl.BlockSpec((1, chunk // 4, D), lambda i, p: (level_of(i ^ p[3]), 0, 0))
        ] * 4
        grad_shapes = [shape((4, D // 16, width), BF)] * 4
        grad_shapes += [shape((4, chunk // 4 + extra, D), BF)] * 4
    wide, low = shape((rows, D), F32), shape((rows, D), BF)
    lane_part = pl.BlockSpec((8, chunk), lambda i, p: (0, i))
    return pl.pallas_call(
        functools.partial(hidden_kernel, pieces=pieces),
        grid_spec=pltpu.PrefetchScalarGridSpec(
            num_scalar_prefetch=1,
            grid=(4,),
            in_specs=[lane_part] + [pl.BlockSpec(memory_space=pl.ANY)] * (4 + 2 * pieces),
            out_specs=[lane_part] + [whole(rows, D)] * 4 + grad_specs,
            scratch_shapes=[
                pltpu.VMEM((D, width), BF),
                pltpu.VMEM((width, D), BF),
                pltpu.VMEM((2 * rows, D), BF),
                pltpu.VMEM((2 * rows, D), BF),
                pltpu.VMEM((2 * rows, D), F32),
                pltpu.VMEM((2 * rows, D), F32),
                pltpu.VMEM((D, chunk), F32),
                pltpu.VMEM((chunk, D), F32),
                pltpu.SemaphoreType.DMA((blocks,)),
                pltpu.SemaphoreType.DMA((blocks,)),
                pltpu.SemaphoreType.DMA((2,)),
                pltpu.SemaphoreType.DMA((2,)),
            ],
        ),
        out_shape=[shape((8, width), F32), wide, low, wide, low] + grad_shapes,
        name="hidden",
        **params(limit=VMEM_MOST),
    )(place, bias, own, other, cot, cot_other, *up_pieces, *down_pieces)


def finish_kernel(mid_ref, mlp_ref, came_ref, t_ref, out_ref, s_ref, *, row):
    @pl.when(pl.program_id(0) == 0)
    def _():
        s_ref[...] = jnp.zeros_like(s_ref)

    mlp = mlp_ref[...] + came_ref[...].astype(F32) + t_ref[row : row + 1]
    final = mid_ref[...] + mlp
    out_ref[...] = final.astype(BF)
    s_ref[0:1] += column_sums(mlp * mlp)
    s_ref[1:2] += column_sums(final * final)


def finish(mid, mlp, came, vectors, row, rows=256):
    full = pl.BlockSpec((rows, D), lambda i: (i, 0))
    return pl.pallas_call(
        functools.partial(finish_kernel, row=row),
        grid=(mid.shape[0] // rows,),
        in_specs=[full, full, full, pl.BlockSpec((16, D), lambda i: (0, 0))],
        out_specs=[full, pl.BlockSpec((8, D), lambda i: (0, 0))],
        out_shape=[shape(mid.shape, BF), shape((8, D), F32)],
        name="finish",
        **params(),
    )(mid, mlp, came, vectors)


def append_kernel(place_ref, *refs):
    kept_ref, came_ref, outs = refs[0], refs[1], refs[-4:]
    for flip, out in enumerate(outs):
        for place in range(4):
            row = place_ref[1] ^ flip
            out[level_of(place ^ place_ref[3])] = kept_ref[place, row] + came_ref[place, row]


def append(place, kept, came, quarters):
    shard = kept.shape[2]
    spot = (quarters[0].shape[1] - shard) // shard
    part = pl.BlockSpec((4, 4, shard, D), lambda i, p: (0, 0, 0, 0))
    out = pl.BlockSpec((4, shard, D), lambda i, p: (0, spot, 0))
    return pl.pallas_call(
        append_kernel,
        grid_spec=pltpu.PrefetchScalarGridSpec(
            num_scalar_prefetch=1,
            grid=(1,),
            in_specs=[part, part] + [pl.BlockSpec(memory_space=pl.ANY)] * 4,
            out_specs=[out] * 4,
        ),
        out_shape=[shape(quarter.shape, BF) for quarter in quarters],
        name="append",
        **params({3: 0, 4: 1, 5: 2, 6: 3}),
    )(place, kept, came, *quarters)


def level_of(flip):
    return flip % 2 * 2 + flip // 2


def middle_back_kernel(place_ref, gn_ref, gn_other_ref, mid_ref, cot_ref, t_ref, *refs, four):
    o_refs, w_refs, outs = refs[:4], refs[4:8], refs[8:]
    gm_ref, go_refs, kept_ref, sent_ref, s_ref, total = outs[0], outs[1:5], *outs[5:9]
    step = pl.program_id(0)

    @pl.when(step == 0)
    def _():
        s_ref[...] = jnp.zeros_like(s_ref)
        total[...] = jnp.zeros_like(total)

    grad_two = gn_ref[...] + gn_other_ref[...].astype(F32)
    cot = cot_ref[...].astype(F32)
    unit, scale = norm_parts(mid_ref[...])
    grad_middle = cot + norm_back(unit, scale, grad_two, t_ref[6:7])
    gm_ref[...] = grad_middle
    grad_attn = grad_middle.astype(BF)
    s_ref[0:1] += column_sums(grad_attn.astype(F32))
    s_ref[1:2] += column_sums(grad_two * unit)
    s_ref[2:3] += column_sums(grad_two)
    s_ref[3:4] += column_sums(cot)
    for mask, o_ref, w_ref, go_ref in zip(MASK, o_refs, w_refs, go_refs):
        go_ref[...] = dot(grad_attn, w_ref[...], NT).astype(BF)
        start = pl.multiple_of((place_ref[0] ^ mask) * GROUP, GROUP)
        total[pl.ds(start, GROUP)] += dot(o_ref[...], grad_attn, TN)

    @pl.when(step == pl.num_programs(0) - 1)
    def _():
        if not four:
            kept_ref[...] = total[...].astype(BF)
            sent_ref[...] = jnp.zeros_like(sent_ref)
            return
        blocks, shard = kept_ref.shape[:2]
        for other, ref in enumerate((kept_ref, sent_ref)):
            for block in range(blocks):
                start = pl.multiple_of((2 * block + (place_ref[0] % 2 ^ other)) * shard, shard)
                ref[block] = total[pl.ds(start, shard)].astype(BF)


def middle_back(place, gn, gn_other, mid, cot, vectors, mixed, weight, shard, four, rows=256):
    count = mid.shape[0]
    full = pl.BlockSpec((rows, D), lambda i, p: (i, 0))
    part = pl.BlockSpec((rows, GROUP), lambda i, p: (i, 0))

    def whole(*dims):
        return pl.BlockSpec(dims, lambda i, p: (0, 0))

    if four:
        half = (D // (2 * shard), shard, D)
        out_specs = [pl.BlockSpec(half, lambda i, p: (0, 0, 0))] * 2
        out_shapes = [shape(half, BF)] * 2
    else:
        out_specs = [whole(D, D), whole(8, D)]
        out_shapes = [shape((D, D), BF), shape((8, D), BF)]
    return pl.pallas_call(
        functools.partial(middle_back_kernel, four=four),
        grid_spec=pltpu.PrefetchScalarGridSpec(
            num_scalar_prefetch=1,
            grid=(count // rows,),
            in_specs=[full, full, full, full, whole(16, D)]
            + mixed_specs(count, rows)
            + group_specs(),
            out_specs=[full] + [part] * 4 + out_specs + [whole(8, D)],
            scratch_shapes=[pltpu.VMEM((D, D), F32)],
        ),
        out_shape=[shape((count, D), F32)]
        + [shape((count, GROUP), BF)] * 4
        + out_shapes
        + [shape((8, D), F32)],
        name="middle_back",
        **params(),
    )(place, gn, gn_other, mid, cot, vectors, *mixed, mixed[2], *([weight] * 4))


def project_back_kernel(
    place_ref, n_ref, x_ref, w_ref, gq_ref, gk_ref, gv_ref, late_ref, up_ref, squares_ref, ends_ref,
    own_ref, other_ref, grad_ref, total, sums, *, shard, four
):
    step = pl.program_id(0)

    @pl.when(step == 0)
    def _():
        total[...] = jnp.zeros_like(total)
        sums[...] = jnp.zeros_like(sums)

    joined = jnp.concatenate([gq_ref[...], gk_ref[...], gv_ref[...]], axis=1)
    width = 3 * GROUP
    grad = dot(joined, w_ref[:, :width], NT)

    @pl.when(step < 2)
    def _():
        own_ref[...] = grad.astype(BF)

    @pl.when(step >= 2)
    def _():
        other_ref[...] = grad.astype(BF)

    total[...] += dot(n_ref[...], joined, TN)
    unit, _ = norm_parts(x_ref[...].astype(F32))
    sums[0:1] += column_sums(grad * unit)
    sums[1:2] += column_sums(grad)
    sums[2:3, :width] += column_sums(joined.astype(F32))

    @pl.when(step == pl.num_programs(0) - 1)
    def _():
        hot, part = bias_places(place_ref[0], shard)
        bias = sums[2:3, :width]
        spread = [
            dot(jnp.broadcast_to(jnp.where(part == j, bias, 0.0), (8, width)).astype(BF), hot, NT)
            for j in range(3)
        ]
        rows = [sums[0:1], sums[1:2], *[part[0:1] for part in spread]]
        rows += [late_ref[0:1], late_ref[1:2], late_ref[2:3]]
        wide = up_ref.shape[1]
        tall = 2 * wide * shard // D
        column = lax.broadcasted_iota(jnp.int32, (1, wide), 1)
        source = (column // tall * 2 + place_ref[0] % 2) * shard + column % shard
        which = column % tall // shard
        hot = lax.broadcasted_iota(jnp.int32, (D, wide), 0) == source
        ups = jnp.concatenate(
            [jnp.where(which == j, up_ref[0:1], 0.0) for j in range(tall // shard)]
            + [jnp.zeros((8 - tall // shard, wide), F32)],
            axis=0,
        )
        ups = dot(ups.astype(BF), jnp.where(hot, 1.0, 0.0).astype(BF), NT)
        rows += [ups[j : j + 1] for j in range(tall // shard)]
        rows += [late_ref[3:4]]
        for ref, j in ((squares_ref, 0), (squares_ref, 1), (squares_ref, 2), (ends_ref, 0), (ends_ref, 1)):
            rows += [jnp.broadcast_to(jnp.sum(ref[j : j + 1], axis=1, keepdims=True), (1, D))]
        rows += [jnp.zeros((128 - len(rows), D), F32)]
        vectors = jnp.concatenate(rows, axis=0).T.astype(BF)
        height = D // 8 if four else D
        for block in range(D // height):
            start = 0
            if four:
                flip = block // 2 ^ place_ref[3]
                start = pl.multiple_of(
                    (level_of(flip) * 2 + (block % 2 ^ place_ref[2])) * height, height
                )
            here = slice(block * height, (block + 1) * height)
            grad_ref[pl.ds(start, height), :width] = total[here].astype(BF)
            grad_ref[pl.ds(start, height), width:] = vectors[here]


def project_back(place, normed, values, weight, parts, late, shard, four, rows=512):
    count = normed.shape[0]
    width = 3 * GROUP

    def row_block(cols):
        return pl.BlockSpec((rows, cols), lambda i, p: (i, 0))

    def whole(*dims):
        return pl.BlockSpec(dims, lambda i, p: (0, 0))

    half = shape((count // 2, D), BF)
    return pl.pallas_call(
        functools.partial(project_back_kernel, shard=shard, four=four),
        grid_spec=pltpu.PrefetchScalarGridSpec(
            num_scalar_prefetch=1,
            grid=(count // rows,),
            in_specs=[row_block(D), row_block(D), whole(*weight.shape)]
            + [row_block(GROUP)] * 3
            + [whole(*part.shape) for part in late],
            out_specs=[
                pl.BlockSpec((rows, D), lambda i, p: (jnp.minimum(i, 1), 0)),
                pl.BlockSpec((rows, D), lambda i, p: (jnp.maximum(i - 2, 0), 0)),
                whole(*weight.shape),
            ],
            scratch_shapes=[pltpu.VMEM((D, width), F32), pltpu.VMEM((8, D), F32)],
        ),
        out_shape=[half, half, shape(weight.shape, BF)],
        name="project_back",
        **params(),
    )(place, normed, values, weight, *parts, *late)


def first_back_kernel(x_ref, gm_ref, t_ref, a_ref, b_ref, c_ref, out_ref):
    grad = a_ref[...].astype(F32) + b_ref[...].astype(F32) + c_ref[...].astype(F32)
    unit, scale = norm_parts(x_ref[...].astype(F32))
    out_ref[...] = gm_ref[...] + norm_back(unit, scale, grad, t_ref[0:1])


def first_back(tokens, grad_middle, vectors, parts, rows=256):
    full = pl.BlockSpec((rows, D), lambda i: (i, 0))
    return pl.pallas_call(
        first_back_kernel,
        grid=(tokens.shape[0] // rows,),
        in_specs=[full, full, pl.BlockSpec((16, D), lambda i: (0, 0)), full, full, full],
        out_specs=full,
        out_shape=shape(tokens.shape, F32),
        name="first_back",
        **params(),
    )(tokens, grad_middle, vectors, *parts)


def per_device(
    tokens,
    positions,
    ln1_gain,
    ln1_shift,
    qkv_weight,
    qkv_bias,
    out_weight,
    out_bias,
    ln2_gain,
    ln2_shift,
    up_weight,
    up_bias,
    down_weight,
    down_bias,
    cotangent,
):
    rows = tokens.shape[0]
    outer = lax.axis_size("o")
    o, y, x, c = (lax.axis_index(name) for name in ALL)
    ctx = 2 * x + c
    four = outer == 4
    place = jnp.stack([ctx, 2 * y + x, y, o]).astype(jnp.int32)
    shard = ln1_gain.shape[0]
    blocks = D // shard
    half_blocks = blocks // 2
    tall = up_bias.shape[0]
    ff_half = tall * half_blocks

    vector_parts = (
        ln1_gain,
        ln1_shift,
        qkv_bias,
        out_bias,
        ln2_gain,
        ln2_shift,
        up_bias,
        down_bias,
    )
    n_vectors = sum(part.shape[0] for part in vector_parts) // shard
    packed = pack(qkv_weight, [part.reshape(1, -1) for part in vector_parts])
    packed, down_weight, out_weight, up_weight = tie(packed, down_weight, out_weight, up_weight)
    packed = lax.all_to_all(packed, ("x", "c"), 0, 0, tiled=True).reshape(4 * shard, -1)

    up_parts = up_weight.reshape(shard, half_blocks, 2, tall)

    def column_half(which):
        return lax.dynamic_index_in_dim(up_parts, which, 2, keepdims=False).reshape(shard, -1)

    upper = jnp.concatenate(by_place(c, column_half(c), swap(column_half(1 - c), "c")), axis=0)

    packed, tokens, positions, upper, out_weight = tie(
        packed, tokens, positions, upper, out_weight
    )
    packed_far = far_half(packed)
    place_rows = jnp.zeros((16, D), BF).at[:3, :rows].set(positions.astype(BF))
    sent = jnp.concatenate([tokens, place_rows], axis=0)
    from_x = swap(sent, "x")
    out_far = far_half(out_weight)
    packed_far, out_far, packed, down_weight, out_weight = tie(
        packed_far, out_far, packed, down_weight, out_weight
    )
    lower_far = far_half(down_weight)
    out = near_half(out_weight, out_far)
    packed_pair, packed_near = near_half(packed, packed_far)
    packed_y = swap(packed_pair, "y")
    packed_near, packed_y, from_x, upper, lower_far, out = tie(
        packed_near, packed_y, from_x, upper, lower_far, out
    )
    out = all_blocks(out)
    out_x = swap(out, "x")
    if four:
        pieces = (packed_pair, packed_y, packed_near, swap(packed_near, "y"))
    else:
        pieces = (jnp.stack(by_place(y, packed_pair, packed_y), axis=1).reshape(1, D, -1),)
    lower = near_half(down_weight, lower_far)
    upper_far = far_half(upper)
    from_c = swap(jnp.stack([sent, from_x]), "c")
    clip_rows = jnp.concatenate(
        [tokens, from_x[:rows], from_c[0, :rows], from_c[1, :rows]], axis=0
    )
    places = jnp.concatenate(
        [
            positions.astype(F32),
            from_x[rows : rows + 3, :rows].astype(F32),
            from_c[0, rows : rows + 3, :rows].astype(F32),
            from_c[1, rows : rows + 3, :rows].astype(F32),
        ],
        axis=1,
    )
    cosine, sine = rotary_tables(places, PAIR)
    pieces, lower, out_x, upper, upper_far, clip_rows, cosine, sine = tie(
        pieces, lower, out_x, upper, upper_far, clip_rows, cosine, sine
    )
    lower = all_blocks(lower)
    out_y = swap(jnp.stack([out, out_x]), "y")
    lower_x, lower_y = swap(lower, "x"), swap(lower, "y")
    upper = near_half(upper, upper_far)
    normed, q, k, v, vectors, gathered = project(place, clip_rows, pieces, cosine, sine, shard)

    q, upper, out_y = tie(q, upper, out_y)
    upper = all_blocks(upper)
    upper_x, upper_y = swap(upper, "x"), swap(upper, "y")
    cotangent_other = swap(cotangent, "c")
    mixed_far, wide_far, logs_far = attend(q, k, v, 1)
    if four:
        out_own = jnp.stack([out, out_x, out_y[0], out_y[1]])
        out_sources = (out_own, swap(out_own, "c"))
    else:
        out_half = jnp.stack(place_four(y, x, (out, out_x, out_y[0], out_y[1])), axis=1)
        out_half = out_half.reshape(half_blocks, shard, D)
        out_half = jnp.stack(by_place(c, out_half, swap(out_half, "c")), axis=1)
        out_sources = (out_half.reshape(1, 1, D, D), out_half.reshape(1, 1, D, D))
    mixed_far, lower_x, lower_y, out_sources, cotangent_other, q = tie(
        mixed_far, lower_x, lower_y, out_sources, cotangent_other, q
    )
    came_x = swap(mixed_far, "x")
    lower_xy = swap(lower_x, "y")
    mixed_near, wide_near, logs_near = attend(q, k, v, 0)
    mixed_near, came_x, upper_y, upper_x = tie(mixed_near, came_x, upper_y, upper_x)
    upper_xy = swap(upper_y, "x")
    came_c = swap(jnp.concatenate([mixed_near[rows:], came_x[rows:]], axis=0), "c")
    mixed = (mixed_near, came_x, came_c)
    mid, normed_two, squares, out_full = middle(place, tokens, vectors, mixed, out_sources, four)

    normed_other = swap(normed_two, "c")
    if four:
        up_pieces = (upper, upper_x, upper_y, upper_xy)
        down_pieces = (lower, lower_x, lower_y, lower_xy)
    else:
        upper = jnp.stack(place_four(y, x, (upper, upper_x, upper_y, upper_xy)), axis=1)
        up_pieces = (upper.reshape(1, D, ff_half),)
        lower = jnp.stack(place_four(y, x, (lower, lower_x, lower_y, lower_xy)), axis=1)
        down_pieces = (lower.reshape(1, ff_half, D),)
    normed_two, bias_up = tie(normed_two, hidden_bias(place, vectors, ff_half, shard, tall))
    results = hidden(
        place,
        bias_up,
        normed_two,
        normed_other,
        cotangent,
        cotangent_other,
        up_pieces,
        down_pieces,
        shard,
    )
    up_bias_grad, gn, gn_sent, mlp, mlp_sent = results[:5]
    gn_came = swap(gn_sent, "c")
    mlp_came = swap(mlp_sent, "c")

    def quarter(values, flip):
        parts = values.reshape(outer, 4, -1, values.shape[-1])
        return lax.dynamic_index_in_dim(parts, (2 * y + x) ^ flip, 1, keepdims=False)

    if four:
        ups, downs = tuple(results[5:9]), tuple(results[9:])
    else:
        ups = tuple(quarter(results[5], flip) for flip in range(4))
        downs = ()
    grad_middle, go_own, go_x, go_c, go_xc, out_kept, out_sent, sums = middle_back(
        place, gn, gn_came, mid, cotangent, vectors, mixed, out_full, shard, four
    )
    go_c, ups = tie(go_c, ups)
    upper_passed = swap(ups[3], "y")
    go_came_c = swap(go_c, "c")
    go_came_x = swap(go_x, "x")
    go_came_xc = lax.ppermute(go_xc, ("x", "c"), DIAGONAL)
    if not four:
        out_grad = out_kept.reshape(half_blocks, 2, shard, D)
        out_sent = lax.dynamic_index_in_dim(out_grad, 1 - c, 1, keepdims=False)
        out_kept = lax.dynamic_index_in_dim(out_grad, c, 1, keepdims=False)
    out_came = swap(out_sent, "c")
    mlp_came, out_sent = tie(mlp_came, out_sent)
    final_low, ends = finish(mid, mlp, mlp_came, vectors, n_vectors - 1)
    go_came_c, out_came, final_low = tie(go_came_c, out_came, final_low)
    if four:
        downs = append(
            place,
            out_kept.reshape(4, 4, shard, D),
            out_came.reshape(4, 4, shard, D),
            downs,
        )
    else:
        out_sums = (out_kept + out_came).reshape(outer * 4, shard, D)
        lower_grad = results[6].reshape(outer * 4, tall, D)
        lower_grad = jnp.concatenate([lower_grad, out_sums], axis=1)
        downs = tuple(quarter(lower_grad, flip) for flip in range(4))

    downs, go_own, go_came_c, go_came_x, go_came_xc, ups, upper_passed = tie(
        downs, go_own, go_came_c, go_came_x, go_came_xc, ups, upper_passed
    )
    lower_passed = swap(downs[3], "x")
    upper_kept = swap(ups[2], "y")
    first = attend_back(
        q, k, v, go_own, go_came_c, wide_near, logs_near, cosine, sine, 0
    )
    lower_passed, upper_kept, first, downs, ups = tie(lower_passed, upper_kept, first, downs, ups)
    upper_second = swap(ups[1] + upper_passed, "x")
    lower_second = swap(downs[2] + lower_passed, "y")
    parts = attend_back(
        q, k, v, go_came_x, go_came_xc, wide_far, logs_far, cosine, sine, 1, before=first
    )
    upper_second, lower_second, parts, downs = tie(upper_second, lower_second, parts, downs)
    lower_kept = swap(downs[1], "x")
    upper_sum = near_sums(ups[0], upper_second, upper_kept)

    gn_low, gn_high, last = project_back(
        place,
        normed,
        clip_rows,
        gathered,
        parts,
        (sums, up_bias_grad, squares, ends),
        shard,
        four,
    )
    gn_low, gn_high, last, upper_sum, lower_kept = tie(
        gn_low, gn_high, last, upper_sum, lower_kept
    )
    gn_came = swap(gn_high, "c")

    cut = 512
    last = last.reshape(outer, 2, 4 * shard, -1)

    def over_y(values):
        axis = values.ndim - 3
        if four:
            kept, sent = (lax.index_in_dim(values, i, axis, keepdims=False) for i in (0, 1))
        else:
            kept = lax.dynamic_index_in_dim(values, y, axis, keepdims=False)
            sent = lax.dynamic_index_in_dim(values, 1 - y, axis, keepdims=False)
        return kept.astype(F32) + swap(sent.astype(BF), "y").astype(F32)

    high = near_sums(last[..., cut:])
    low = over_y(last[..., :cut]).astype(BF)
    gn_came, low, high, upper_sum, lower_kept = tie(gn_came, low, high, upper_sum, lower_kept)
    low = near_sums(low)
    high = far_sums(high)
    gn_x = swap(gn_low[rows:] + gn_came[rows:], "x")
    upper_grad = far_sums(upper_sum).astype(BF).reshape(2, shard, -1)
    lower_sum = near_sums(downs[0], lower_second, lower_kept)
    low, high = tie(low, high)
    low = far_sums(low)
    high = over_y(high)
    low, high, lower_sum, upper_grad = tie(low, high, lower_sum, upper_grad)
    upper_kept = lax.dynamic_index_in_dim(upper_grad, c, 0, keepdims=False)
    upper_came = swap(lax.dynamic_index_in_dim(upper_grad, 1 - c, 0, keepdims=False), "c")
    last = jnp.concatenate([low.astype(BF), high.astype(BF)], axis=1)
    last, tokens = tie(last, tokens)
    input_grad = first_back(tokens, grad_middle, vectors, (gn_low, gn_came, gn_x))
    last = lax.all_to_all(last.reshape(4, shard, -1), ("x", "c"), 0, 0, tiled=True)
    lower_grad = far_sums(lower_sum, last, input_grad)
    upper_pair = by_place(c, upper_kept, upper_came)
    up_weight_grad = jnp.stack(
        [part.reshape(shard, half_blocks, tall) for part in upper_pair], axis=2
    )
    last = last.astype(F32)
    qkv_weight_grad = last[:, :, : 3 * GROUP].reshape(4, shard, 3, GROUP).transpose(1, 2, 0, 3)
    vector_grads = jnp.sum(last[:, :, 3 * GROUP : 3 * GROUP + n_vectors + 5], axis=0).T
    entry_count = rows * lax.axis_size(ALL) * D
    norm_stats = jnp.sqrt(vector_grads[n_vectors:, 0] / entry_count)

    return (
        final_low,
        input_grad,
        vector_grads[0],
        vector_grads[1],
        qkv_weight_grad.reshape(shard, 3 * D),
        vector_grads[2:5].reshape(-1),
        lower_grad[tall:],
        vector_grads[5],
        vector_grads[6],
        vector_grads[7],
        up_weight_grad.reshape(shard, -1).astype(F32),
        vector_grads[8 : n_vectors - 1].reshape(-1),
        lower_grad[:tall],
        vector_grads[n_vectors - 1],
        norm_stats,
    )


def solution(mesh):
    fine = Mesh(mesh.devices.reshape(-1, 2, 2, 2), ALL)
    rows, vector, whole = P(ALL, None), P(ALL), P()
    in_specs = (
        rows,
        P(None, ALL),
        vector,
        vector,
        rows,
        vector,
        rows,
        vector,
        vector,
        vector,
        rows,
        vector,
        rows,
        vector,
        rows,
    )
    out_specs = (
        rows,
        rows,
        vector,
        vector,
        rows,
        vector,
        rows,
        vector,
        vector,
        vector,
        rows,
        vector,
        rows,
        vector,
        whole,
    )
    return jax.shard_map(
        per_device, mesh=fine, in_specs=in_specs, out_specs=out_specs, check_vma=False
    )
```

```python
import functools
import math

import jax
import jax.numpy as jnp
from jax import lax
from jax.experimental import pallas as pl
from jax.experimental.pallas import tpu as pltpu
from jax.sharding import Mesh
from jax.sharding import PartitionSpec as P

D = 1024
HD = 64
GAP = HD // 6
PAIR = 2 * HD
GROUP = D // 4
EPSILON = 1e-06
BF = jnp.bfloat16
F32 = jnp.float32
ALL = ("o", "y", "x", "c")
SWAP = ((0, 1), (1, 0))
DIAGONAL = ((0, 3), (1, 2), (2, 1), (3, 0))
NT = (((1,), (1,)), ((), ()))
NN = (((1,), (0,)), ((), ()))
TN = (((0,), (0,)), ((), ()))
VMEM_LIMIT = 58 * 2**20
VMEM_MOST = 63 * 2**20
SMALL = pl.CostEstimate(flops=10**6, bytes_accessed=2**16, transcendentals=0)
MASK = (0, 2, 1, 3)


def dot(left, right, dims=NN):
    return lax.dot_general(left, right, dims, preferred_element_type=F32)


def swap(values, axis):
    return lax.ppermute(values, axis, SWAP)


def tie(*values):
    return lax.optimization_barrier(values)


def by_place(flag, own, other):
    return jnp.where(flag == 0, own, other), jnp.where(flag == 0, other, own)


def place_four(high, low, parts):
    first = by_place(low, parts[0], parts[1])
    second = by_place(low, parts[2], parts[3])
    even = by_place(high, first[0], second[0])
    odd = by_place(high, first[1], second[1])
    return even[0], odd[0], even[1], odd[1]


def far(values):
    return lax.ppermute(values, "o", [(i, i ^ 2) for i in range(4)])


def near(values):
    return lax.ppermute(values, "o", [(i, i ^ 1) for i in range(4)])


def level_place(own, level):
    return own ^ (level % 2 * 2 + level // 2)


def far_half(values):
    if lax.axis_size("o") != 4:
        return lax.all_gather(values, "o", axis=0, tiled=False)
    return far(values)


def near_half(values, came):
    if lax.axis_size("o") != 4:
        return came, came
    pair = jnp.stack([values, came])
    return pair, near(pair)


def all_blocks(halves):
    if lax.axis_size("o") != 4:
        return halves[0]
    return jnp.concatenate(halves, axis=0)


def near_sums(*terms):
    if lax.axis_size("o") != 4:
        return sum(terms)
    kept = sum(term[:2].astype(F32) for term in terms)
    return kept, near(sum(term[2:].astype(F32) for term in terms).astype(BF))


def far_sums(values, *earlier):
    if lax.axis_size("o") != 4:
        return lax.psum_scatter(values, "o", scatter_dimension=0, tiled=False).astype(F32)
    kept, came = values
    sums = kept + came.astype(F32)
    came = far(sums[1].astype(BF))
    if earlier:
        came = tie(came, *earlier)[0]
    return sums[0] + came.astype(F32)


def norm_parts(values):
    average = jnp.mean(values, axis=-1, keepdims=True)
    centred = values - average
    spread = jnp.mean(centred * centred, axis=-1, keepdims=True)
    scale = lax.rsqrt(spread + EPSILON)
    return centred * scale, scale


def norm_back(unit, scale, grad, gain):
    scaled = grad * gain
    return scale * (
        scaled
        - jnp.mean(scaled, axis=-1, keepdims=True)
        - unit * jnp.mean(scaled * unit, axis=-1, keepdims=True)
    )


def rotary_tables(places, width):
    column = jnp.arange(width) % HD
    segment = column // (2 * GAP)
    within = column % (2 * GAP)
    freq_index = (within % GAP).astype(F32)
    frequency = jnp.power(10000.0, -freq_index / GAP)
    angles = jnp.zeros((places.shape[1], width), F32)
    for axis_num in range(3):
        angles = (
            angles
            + places[axis_num][:, None] * jnp.where(segment == axis_num, frequency, 0.0)[None, :]
        )
    rotated = segment < 3
    return jnp.where(rotated, jnp.cos(angles), 1.0), jnp.where(rotated, jnp.sin(angles), 0.0)


def shifted(values, leading):
    ahead = pltpu.roll(values, PAIR - GAP, 1)
    behind = pltpu.roll(values, GAP, 1)
    return jnp.where(leading, -ahead, behind)


def leading_lanes():
    lane = lax.broadcasted_iota(jnp.int32, (1, PAIR), 1)
    return lane % HD % (2 * GAP) < GAP


def column_sums(values):
    return jnp.sum(values, axis=0, keepdims=True)


def params(aliases=None, limit=VMEM_LIMIT):
    return dict(
        compiler_params=pltpu.CompilerParams(vmem_limit_bytes=limit),
        cost_estimate=SMALL,
        input_output_aliases=aliases or {},
    )


def shape(dims, kind):
    return jax.ShapeDtypeStruct(dims, kind)


def pack_kernel(w_ref, *refs):
    vectors, out_ref = refs[:-1], refs[-1]
    shard = w_ref.shape[0]
    rows = []
    for ref in vectors:
        values = ref[...].astype(F32)
        rows += [values[:, low : low + shard] for low in range(0, values.shape[1], shard)]
    columns = jnp.concatenate(rows + [jnp.zeros((128 - len(rows), shard), F32)], axis=0).T
    for place in range(4):
        for part in range(3):
            start = part * D + place * GROUP
            out_ref[place, :, part * GROUP : (part + 1) * GROUP] = w_ref[:, start : start + GROUP]
        out_ref[place, :, 3 * GROUP :] = columns.astype(BF)


def pack(weight, vectors):
    return pl.pallas_call(
        pack_kernel,
        out_shape=shape((4, weight.shape[0], 3 * GROUP + 128), BF),
        name="pack",
        **params(),
    )(weight, *vectors)


def bias_places(place, shard):
    column = lax.broadcasted_iota(jnp.int32, (1, 3 * GROUP), 1)
    target = column // GROUP * D + place * GROUP + column % GROUP
    source = target // (3 * shard) * shard + target % shard
    hot = lax.broadcasted_iota(jnp.int32, (D, 3 * GROUP), 0) == source
    return jnp.where(hot, 1.0, 0.0).astype(BF), target % (3 * shard) // shard


def load_blocks(sources, target, semaphores):
    found = []
    for source, index, place in sources:
        block = source if isinstance(index, slice) else source.at[index]
        height = block.shape[0]
        start = pl.multiple_of(place * height, height)
        found.append(
            pltpu.make_async_copy(
                block, target.at[pl.ds(start, height)], semaphores.at[len(found)]
            )
        )
    return found


def piece_blocks(arrays, place):
    if len(arrays) == 1:
        return [(arrays[0], 0, 0)]
    return [
        (source, level, level_place(place[3], level) * 4 + (place[1] ^ flip))
        for flip, source in enumerate(arrays)
        for level in range(4)
    ]


def project_kernel(place_ref, x_ref, cos_ref, sin_ref, *refs, shard, pieces):
    sources, refs = refs[:pieces], refs[pieces:]
    n_ref, q_ref, k_ref, v_ref, t_ref, w_ref, b_ref, semaphores = refs

    @pl.when(pl.program_id(0) == 0)
    def _():
        if pieces == 1:
            blocks = [(sources[0], 0, 0)]
        else:
            blocks = [
                (
                    source,
                    level,
                    (level_place(place_ref[3], level) ^ (piece // 2)) * 2
                    + (place_ref[2] ^ (piece % 2)),
                )
                for piece, source in enumerate(sources)
                for level in range(2)
            ]
        copies = load_blocks(blocks, w_ref, semaphores)
        for copy in copies:
            copy.start()
        for copy in copies:
            copy.wait()
        t_ref[...] = w_ref[:, 3 * GROUP :].astype(F32).T[: t_ref.shape[0]]
        hot, part = bias_places(place_ref[0], shard)
        found = dot(t_ref[...].astype(BF), hot)
        bias = jnp.where(part == 0, found[2:3], jnp.where(part == 1, found[3:4], found[4:5]))
        b_ref[...] = jnp.broadcast_to(bias, b_ref.shape)

    unit, _ = norm_parts(x_ref[...].astype(F32))
    normed = (unit * t_ref[0:1] + t_ref[1:2]).astype(BF)
    n_ref[...] = normed
    joined = dot(normed, w_ref[:, : 3 * GROUP]) + b_ref[0:1]
    cosine, sine, leading = cos_ref[...], sin_ref[...], leading_lanes()
    for ref, start, factor in ((q_ref, 0, 1.0 / math.sqrt(HD)), (k_ref, GROUP, 1.0)):
        for low in range(0, GROUP, PAIR):
            part = joined[:, start + low : start + low + PAIR]
            turned = part * cosine + shifted(part, leading) * sine
            ref[:, low : low + PAIR] = (turned * factor).astype(BF)
    v_ref[...] = joined[:, 2 * GROUP :].astype(BF)


def project(place, values, pieces, cosine, sine, shard, rows=512):
    count = values.shape[0]
    width = pieces[0].shape[-1]

    def part(cols):
        return pl.BlockSpec((rows, cols), lambda i, p: (i, 0))

    def whole(*dims):
        return pl.BlockSpec(dims, lambda i, p: (0, 0))

    return pl.pallas_call(
        functools.partial(project_kernel, shard=shard, pieces=len(pieces)),
        grid_spec=pltpu.PrefetchScalarGridSpec(
            num_scalar_prefetch=1,
            grid=(count // rows,),
            in_specs=[part(D), part(PAIR), part(PAIR)]
            + [pl.BlockSpec(memory_space=pl.ANY)] * len(pieces),
            out_specs=[part(D), part(GROUP), part(GROUP), part(GROUP), whole(16, D), whole(D, width)],
            scratch_shapes=[
                pltpu.VMEM((8, 3 * GROUP), F32),
                pltpu.SemaphoreType.DMA((len(pieces) * pieces[0].shape[0],)),
            ],
        ),
        out_shape=[
            shape((count, D), BF),
            shape((count, GROUP), BF),
            shape((count, GROUP), BF),
            shape((count, GROUP), BF),
            shape((16, D), F32),
            shape((D, width), BF),
        ],
        name="project",
        **params(),
    )(place, values, cosine, sine, *pieces)


def attend_kernel(q_ref, k_ref, v_ref, *refs):
    o_ref, wide_ref, lse_ref = refs[-3:]
    q, k, v = q_ref[...], k_ref[...], v_ref[...]
    lane = lax.broadcasted_iota(jnp.int32, (1, PAIR), 1)
    weights, totals, logs = [], [], []
    for scores in [dot(jnp.where(mine, q, 0), k, NT) for mine in (lane < HD, lane >= HD)]:
        top = jnp.max(scores, axis=1, keepdims=True)
        weight = jnp.exp(scores - top)
        total = jnp.sum(weight, axis=1, keepdims=True)
        weights.append(weight.astype(BF))
        totals.append(total)
        logs.append(top + jnp.log(total))
    mixed = [dot(weight, v) / total for weight, total in zip(weights, totals)]
    out = jnp.where(lane < HD, mixed[0], mixed[1])
    o_ref[...] = out.astype(BF)
    wide_ref[...] = out
    lse_ref[...] = jnp.where(lane < HD, logs[0], logs[1])


def attend(q, k, v, side, pair=None, before=None, rows=256):
    count = q.shape[0]
    half = count // 2
    per = count // 4 // rows
    pairs = GROUP // PAIR if pair is None else 1
    first = 0 if pair is None else pair

    def block(i):
        return i // per * 2 * per + side * per + i % per

    full = pl.BlockSpec((count, PAIR), lambda j, i: (0, first + j))
    out = pl.BlockSpec((rows, PAIR), lambda j, i: (i, first + j))
    before = list(before or ())
    return pl.pallas_call(
        attend_kernel,
        grid=(pairs, half // rows),
        in_specs=[pl.BlockSpec((rows, PAIR), lambda j, i: (block(i), first + j)), full, full]
        + [pl.BlockSpec(memory_space=pl.ANY)] * len(before),
        out_specs=[out, out, out],
        out_shape=[shape((half, GROUP), BF), shape((half, GROUP), F32), shape((half, GROUP), F32)],
        name="attend",
        **params({3: 0, 4: 1, 5: 2} if before else None),
    )(q, k, v, *before)


def attend_back_kernel(
    q_ref, go_ref, go_other_ref, wide_ref, lse_ref, k_ref, v_ref, cos_ref, sin_ref, *refs, last, block
):
    step, rows = pl.program_id(1), q_ref.shape[0]
    if last:
        k_start, v_start, _, gq_ref, gk_ref, gv_ref, k_sum, v_sum = refs
    else:
        gq_ref, k_sum, v_sum = refs

    @pl.when(step == 0)
    def _():
        if last:
            k_sum[...] = k_start[...]
            v_sum[...] = v_start[...]
        else:
            k_sum[...] = jnp.zeros_like(k_sum)
            v_sum[...] = jnp.zeros_like(v_sum)

    q, k, v, lse = q_ref[...], k_ref[...], v_ref[...], lse_ref[...]
    go = jnp.where(step < pl.num_programs(1) // 2, go_ref[...], go_other_ref[...])
    lane = lax.broadcasted_iota(jnp.int32, (1, PAIR), 1)
    leading = leading_lanes()
    product = go.astype(F32) * wide_ref[...]
    grads = []
    for head in range(2):
        mine = (lane < HD) if head == 0 else (lane >= HD)
        q_head, go_head = jnp.where(mine, q, 0), jnp.where(mine, go, 0)
        inner = jnp.sum(jnp.where(mine, product, 0.0), axis=1, keepdims=True)
        weight = jnp.exp(dot(q_head, k, NT) - lse[:, HD * head : HD * head + 1])
        pull = (weight * (dot(go_head, v, NT) - inner)).astype(BF)
        grads.append(dot(pull, k))
        k_sum[...] += dot(q_head.T, pull)
        v_sum[...] += dot(go_head.T, weight.astype(BF))
    grad = jnp.where(lane < HD, grads[0], grads[1])
    here = pl.ds(pl.multiple_of(block(step) * rows, rows), rows)
    grad = grad * cos_ref[here] - shifted(grad * sin_ref[here], leading)
    gq_ref[...] = (grad * (1.0 / math.sqrt(HD))).astype(BF)

    if last:

        @pl.when(step == pl.num_programs(1) - 1)
        def _():
            grad = k_sum[...].T
            grad = grad * cos_ref[...] - shifted(grad * sin_ref[...], leading)
            gk_ref[...] = grad.astype(BF)
            gv_ref[...] = v_sum[...].T.astype(BF)


def attend_back(q, k, v, go, go_other, wide, lse, cosine, sine, side, before=None, rows=256):
    count = q.shape[0]
    half = count // 2
    per = count // 4 // rows
    last = before is not None

    def block(i):
        return i // per * 2 * per + side * per + i % per

    part = pl.BlockSpec((rows, PAIR), lambda pair, i: (block(i), pair))
    own = pl.BlockSpec((rows, PAIR), lambda pair, i: (i, pair))
    full = pl.BlockSpec((count, PAIR), lambda pair, i: (0, pair))
    table = pl.BlockSpec((count, PAIR), lambda pair, i: (0, 0))
    turned = pl.BlockSpec((PAIR, count), lambda pair, i: (pair, 0))
    sums = shape((GROUP, count), F32)
    grad = shape((count, GROUP), BF)
    low = pl.BlockSpec((rows, PAIR), lambda pair, i: (jnp.minimum(i, per - 1), pair))
    high = pl.BlockSpec((rows, PAIR), lambda pair, i: (jnp.maximum(i - per, 0), pair))
    in_specs = [part, low, high, own, own, full, full, table, table]
    operands = [q, go, go_other, wide, lse, k, v, cosine, sine]
    if last:
        in_specs += [turned, turned, pl.BlockSpec(memory_space=pl.ANY)]
        operands += [before[1], before[2], before[0]]
        out_specs, out_shape = [part, full, full], [grad, grad, grad]
        scratch = [pltpu.VMEM((PAIR, count), F32)] * 2
    else:
        out_specs, out_shape, scratch = [part, turned, turned], [grad, sums, sums], []
    return pl.pallas_call(
        functools.partial(attend_back_kernel, last=last, block=block),
        grid=(GROUP // PAIR, half // rows),
        in_specs=in_specs,
        out_specs=out_specs,
        out_shape=out_shape,
        scratch_shapes=scratch,
        name="attend_back",
        **params({11: 0} if last else None),
    )(*operands)


def middle_kernel(place_ref, x_ref, t_ref, *refs, four):
    o_refs, sources, refs = refs[:4], refs[4:6], refs[6:]
    mid_ref, n_ref, s_ref, w_ref, semaphores = refs

    @pl.when(pl.program_id(0) == 0)
    def _():
        s_ref[...] = jnp.zeros_like(s_ref)
        if four:
            blocks = [
                (
                    source.at[flip],
                    level,
                    (level_place(place_ref[3], level) * 4 + (place_ref[1] ^ flip)) * 2
                    + (place_ref[0] % 2 ^ other),
                )
                for other, source in enumerate(sources)
                for flip in range(4)
                for level in range(4)
            ]
        else:
            blocks = [(sources[0].at[0], 0, 0)]
        copies = load_blocks(blocks, w_ref, semaphores)
        for copy in copies:
            copy.start()
        for copy in copies:
            copy.wait()

    x = x_ref[...].astype(F32)
    attn = t_ref[5:6]
    for mask, o_ref in zip(MASK, o_refs):
        start = pl.multiple_of((place_ref[0] ^ mask) * GROUP, GROUP)
        attn = attn + dot(o_ref[...], w_ref[pl.ds(start, GROUP)])
    mid = x + attn
    mid_ref[...] = mid
    unit, _ = norm_parts(mid)
    n_ref[...] = (unit * t_ref[6:7] + t_ref[7:8]).astype(BF)
    s_ref[0:1] += column_sums(x * x)
    s_ref[1:2] += column_sums(attn * attn)
    s_ref[2:3] += column_sums(mid * mid)


def group_specs():
    return [
        pl.BlockSpec((GROUP, D), lambda i, p, mask=mask: (p[0] ^ mask, 0)) for mask in MASK
    ]


def mixed_specs(count, rows):
    first = pl.BlockSpec((rows, GROUP), lambda i, p: (i, 0))
    second = pl.BlockSpec((rows, GROUP), lambda i, p: (i + count // rows, 0))
    return [first, first, first, second]


def middle(place, tokens, vectors, mixed, sources, four, rows=256):
    count = tokens.shape[0]
    full = pl.BlockSpec((rows, D), lambda i, p: (i, 0))

    def whole(*dims):
        return pl.BlockSpec(dims, lambda i, p: (0, 0))

    return pl.pallas_call(
        functools.partial(middle_kernel, four=four),
        grid_spec=pltpu.PrefetchScalarGridSpec(
            num_scalar_prefetch=1,
            grid=(count // rows,),
            in_specs=[full, whole(16, D)]
            + mixed_specs(count, rows)
            + [pl.BlockSpec(memory_space=pl.ANY)] * 2,
            out_specs=[full, full, whole(8, D), whole(D, D)],
            scratch_shapes=[pltpu.SemaphoreType.DMA((32,))],
        ),
        out_shape=[
            shape((count, D), F32),
            shape((count, D), BF),
            shape((8, D), F32),
            shape((D, D), BF),
        ],
        name="middle",
        **params(),
    )(place, tokens, vectors, *mixed, mixed[2], *sources)


def hidden_bias_kernel(place_ref, t_ref, out_ref, *, shard, tall):
    chunk = out_ref.shape[1]
    column = lax.broadcasted_iota(jnp.int32, (1, chunk), 1) + pl.program_id(0) * chunk
    source = (column // tall * 2 + place_ref[0] % 2) * shard + column % shard
    which = column % tall // shard
    hot = lax.broadcasted_iota(jnp.int32, (D, chunk), 0) == source
    found = dot(t_ref[...].astype(BF), jnp.where(hot, 1.0, 0.0).astype(BF))
    bias = jnp.zeros((1, chunk), F32)
    for row in range(tall // shard):
        bias = jnp.where(which == row, found[8 + row : 9 + row], bias)
    out_ref[...] = jnp.broadcast_to(bias, out_ref.shape)


def hidden_bias(place, vectors, width, shard, tall, chunk=512):
    return pl.pallas_call(
        functools.partial(hidden_bias_kernel, shard=shard, tall=tall),
        grid_spec=pltpu.PrefetchScalarGridSpec(
            num_scalar_prefetch=1,
            grid=(width // chunk,),
            in_specs=[pl.BlockSpec((16, D), lambda i, p: (0, 0))],
            out_specs=pl.BlockSpec((8, chunk), lambda i, p: (0, i)),
        ),
        out_shape=shape((8, width), F32),
        name="hidden_bias",
        **params(),
    )(place, vectors)


def hidden_kernel(place_ref, bias_ref, *refs, pieces):
    rows_in, refs = refs[:4], refs[4:]
    up_pieces, down_pieces, refs = refs[:pieces], refs[pieces : 2 * pieces], refs[2 * pieces :]
    b_ref, gn_ref, gn_other_ref, mlp_ref, mlp_other_ref = refs[:5]
    up_outs, down_outs = refs[5 : 5 + pieces], refs[5 + pieces : 5 + 2 * pieces]
    up, down, normed, cot, gn_sum, mlp_sum, up_total, down_total, *semaphores = refs[5 + 2 * pieces :]
    step = pl.program_id(0)
    chunk = bias_ref.shape[1]
    rows = gn_ref.shape[0]
    up_sem, down_sem, normed_sem, cot_sem = semaphores

    @pl.when(step == 0)
    def _():
        copies = load_blocks([(ref, slice(None), i) for i, ref in enumerate(rows_in[:2])], normed, normed_sem)
        copies += load_blocks(piece_blocks(up_pieces, place_ref), up, up_sem)
        copies += load_blocks([(ref, slice(None), i) for i, ref in enumerate(rows_in[2:])], cot, cot_sem)
        copies += load_blocks(piece_blocks(down_pieces, place_ref), down, down_sem)
        for copy in copies:
            copy.start()
        gn_sum[...] = jnp.zeros_like(gn_sum)
        mlp_sum[...] = jnp.zeros_like(mlp_sum)
        for copy in copies:
            copy.wait()

    here = pl.ds(pl.multiple_of(step * chunk, chunk), chunk)
    up_part, down_part = up[:, here], down[here, :]
    upward = dot(normed[...], up_part) + bias_ref[0:1]
    grad_active = dot(cot[...], down_part, NT)
    bell = 0.5 * (1.0 + lax.erf(upward * 0.7071067811865476))
    active = (upward * bell).astype(BF)
    slope = bell + upward * jnp.exp(-0.5 * upward * upward) * (1.0 / math.sqrt(2.0 * math.pi))
    grad_up = (grad_active * slope).astype(BF)
    b_ref[...] = jnp.broadcast_to(column_sums(grad_up.astype(F32)), b_ref.shape)
    gn_sum[...] += dot(grad_up, up_part, NT)
    mlp_sum[...] += dot(active, down_part)
    up_grad = dot(normed[...], grad_up, TN)
    down_grad = dot(active, cot[...], TN)
    if pieces == 1:
        up_outs[0][...] = up_grad.astype(BF)
        down_outs[0][...] = down_grad.astype(BF)
    else:
        up_total[...] = up_grad
        down_total[...] = down_grad
        for flip in range(4):
            for place in range(4):
                start = pl.multiple_of((place * 4 + (place_ref[1] ^ flip)) * (D // 16), D // 16)
                level = level_of(place ^ place_ref[3])
                up_outs[flip][level] = up_total[pl.ds(start, D // 16)].astype(BF)
            start = pl.multiple_of((place_ref[1] ^ flip) * (chunk // 4), chunk // 4)
            down_outs[flip][0] = down_total[pl.ds(start, chunk // 4)].astype(BF)

    @pl.when(step == pl.num_programs(0) - 1)
    def _():
        gn_ref[...] = gn_sum[:rows]
        mlp_ref[...] = mlp_sum[:rows]
        gn_other_ref[...] = gn_sum[rows:].astype(BF)
        mlp_other_ref[...] = mlp_sum[rows:].astype(BF)


def hidden(place, bias, own, other, cot, cot_other, up_pieces, down_pieces, extra):
    rows = own.shape[0]
    width = up_pieces[0].shape[-1]
    pieces = len(up_pieces)
    blocks = pieces * up_pieces[0].shape[0]
    chunk = width // 4

    def whole(*dims):
        return pl.BlockSpec(dims, lambda i, p: (0, 0))

    if pieces == 1:
        grad_specs = [
            pl.BlockSpec((D, chunk), lambda i, p: (0, i)),
            pl.BlockSpec((chunk, D), lambda i, p: (i, 0)),
        ]
        grad_shapes = [shape((D, width), BF), shape((width, D), BF)]
    else:
        grad_specs = [pl.BlockSpec((4, D // 16, chunk), lambda i, p: (0, 0, i))] * 4
        grad_specs += [
            pl.BlockSpec((1, chunk // 4, D), lambda i, p: (level_of(i ^ p[3]), 0, 0))
        ] * 4
        grad_shapes = [shape((4, D // 16, width), BF)] * 4
        grad_shapes += [shape((4, chunk // 4 + extra, D), BF)] * 4
    wide, low = shape((rows, D), F32), shape((rows, D), BF)
    lane_part = pl.BlockSpec((8, chunk), lambda i, p: (0, i))
    return pl.pallas_call(
        functools.partial(hidden_kernel, pieces=pieces),
        grid_spec=pltpu.PrefetchScalarGridSpec(
            num_scalar_prefetch=1,
            grid=(4,),
            in_specs=[lane_part] + [pl.BlockSpec(memory_space=pl.ANY)] * (4 + 2 * pieces),
            out_specs=[lane_part] + [whole(rows, D)] * 4 + grad_specs,
            scratch_shapes=[
                pltpu.VMEM((D, width), BF),
                pltpu.VMEM((width, D), BF),
                pltpu.VMEM((2 * rows, D), BF),
                pltpu.VMEM((2 * rows, D), BF),
                pltpu.VMEM((2 * rows, D), F32),
                pltpu.VMEM((2 * rows, D), F32),
                pltpu.VMEM((D, chunk), F32),
                pltpu.VMEM((chunk, D), F32),
                pltpu.SemaphoreType.DMA((blocks,)),
                pltpu.SemaphoreType.DMA((blocks,)),
                pltpu.SemaphoreType.DMA((2,)),
                pltpu.SemaphoreType.DMA((2,)),
            ],
        ),
        out_shape=[shape((8, width), F32), wide, low, wide, low] + grad_shapes,
        name="hidden",
        **params(limit=VMEM_MOST),
    )(place, bias, own, other, cot, cot_other, *up_pieces, *down_pieces)


def finish_kernel(mid_ref, mlp_ref, came_ref, t_ref, out_ref, s_ref, *, row):
    @pl.when(pl.program_id(0) == 0)
    def _():
        s_ref[...] = jnp.zeros_like(s_ref)

    mlp = mlp_ref[...] + came_ref[...].astype(F32) + t_ref[row : row + 1]
    final = mid_ref[...] + mlp
    out_ref[...] = final.astype(BF)
    s_ref[0:1] += column_sums(mlp * mlp)
    s_ref[1:2] += column_sums(final * final)


def finish(mid, mlp, came, vectors, row, rows=256):
    full = pl.BlockSpec((rows, D), lambda i: (i, 0))
    return pl.pallas_call(
        functools.partial(finish_kernel, row=row),
        grid=(mid.shape[0] // rows,),
        in_specs=[full, full, full, pl.BlockSpec((16, D), lambda i: (0, 0))],
        out_specs=[full, pl.BlockSpec((8, D), lambda i: (0, 0))],
        out_shape=[shape(mid.shape, BF), shape((8, D), F32)],
        name="finish",
        **params(),
    )(mid, mlp, came, vectors)


def append_kernel(place_ref, *refs):
    kept_ref, came_ref, outs = refs[0], refs[1], refs[-4:]
    for flip, out in enumerate(outs):
        for place in range(4):
            row = place_ref[1] ^ flip
            out[level_of(place ^ place_ref[3])] = kept_ref[place, row] + came_ref[place, row]


def append(place, kept, came, quarters):
    shard = kept.shape[2]
    spot = (quarters[0].shape[1] - shard) // shard
    part = pl.BlockSpec((4, 4, shard, D), lambda i, p: (0, 0, 0, 0))
    out = pl.BlockSpec((4, shard, D), lambda i, p: (0, spot, 0))
    return pl.pallas_call(
        append_kernel,
        grid_spec=pltpu.PrefetchScalarGridSpec(
            num_scalar_prefetch=1,
            grid=(1,),
            in_specs=[part, part] + [pl.BlockSpec(memory_space=pl.ANY)] * 4,
            out_specs=[out] * 4,
        ),
        out_shape=[shape(quarter.shape, BF) for quarter in quarters],
        name="append",
        **params({3: 0, 4: 1, 5: 2, 6: 3}),
    )(place, kept, came, *quarters)


def level_of(flip):
    return flip % 2 * 2 + flip // 2


def middle_back_kernel(place_ref, gn_ref, gn_other_ref, mid_ref, cot_ref, t_ref, *refs, four):
    o_refs, w_refs, outs = refs[:4], refs[4:8], refs[8:]
    gm_ref, go_refs, kept_ref, sent_ref, s_ref, total = outs[0], outs[1:5], *outs[5:9]
    step = pl.program_id(0)

    @pl.when(step == 0)
    def _():
        s_ref[...] = jnp.zeros_like(s_ref)
        total[...] = jnp.zeros_like(total)

    grad_two = gn_ref[...] + gn_other_ref[...].astype(F32)
    cot = cot_ref[...].astype(F32)
    unit, scale = norm_parts(mid_ref[...])
    grad_middle = cot + norm_back(unit, scale, grad_two, t_ref[6:7])
    gm_ref[...] = grad_middle
    grad_attn = grad_middle.astype(BF)
    s_ref[0:1] += column_sums(grad_attn.astype(F32))
    s_ref[1:2] += column_sums(grad_two * unit)
    s_ref[2:3] += column_sums(grad_two)
    s_ref[3:4] += column_sums(cot)
    for mask, o_ref, w_ref, go_ref in zip(MASK, o_refs, w_refs, go_refs):
        go_ref[...] = dot(grad_attn, w_ref[...], NT).astype(BF)
        start = pl.multiple_of((place_ref[0] ^ mask) * GROUP, GROUP)
        total[pl.ds(start, GROUP)] += dot(o_ref[...], grad_attn, TN)

    @pl.when(step == pl.num_programs(0) - 1)
    def _():
        if not four:
            kept_ref[...] = total[...].astype(BF)
            sent_ref[...] = jnp.zeros_like(sent_ref)
            return
        blocks, shard = kept_ref.shape[:2]
        for other, ref in enumerate((kept_ref, sent_ref)):
            for block in range(blocks):
                start = pl.multiple_of((2 * block + (place_ref[0] % 2 ^ other)) * shard, shard)
                ref[block] = total[pl.ds(start, shard)].astype(BF)


def middle_back(place, gn, gn_other, mid, cot, vectors, mixed, weight, shard, four, rows=256):
    count = mid.shape[0]
    full = pl.BlockSpec((rows, D), lambda i, p: (i, 0))
    part = pl.BlockSpec((rows, GROUP), lambda i, p: (i, 0))

    def whole(*dims):
        return pl.BlockSpec(dims, lambda i, p: (0, 0))

    if four:
        half = (D // (2 * shard), shard, D)
        out_specs = [pl.BlockSpec(half, lambda i, p: (0, 0, 0))] * 2
        out_shapes = [shape(half, BF)] * 2
    else:
        out_specs = [whole(D, D), whole(8, D)]
        out_shapes = [shape((D, D), BF), shape((8, D), BF)]
    return pl.pallas_call(
        functools.partial(middle_back_kernel, four=four),
        grid_spec=pltpu.PrefetchScalarGridSpec(
            num_scalar_prefetch=1,
            grid=(count // rows,),
            in_specs=[full, full, full, full, whole(16, D)]
            + mixed_specs(count, rows)
            + group_specs(),
            out_specs=[full] + [part] * 4 + out_specs + [whole(8, D)],
            scratch_shapes=[pltpu.VMEM((D, D), F32)],
        ),
        out_shape=[shape((count, D), F32)]
        + [shape((count, GROUP), BF)] * 4
        + out_shapes
        + [shape((8, D), F32)],
        name="middle_back",
        **params(),
    )(place, gn, gn_other, mid, cot, vectors, *mixed, mixed[2], *([weight] * 4))


def project_back_kernel(
    place_ref, n_ref, x_ref, w_ref, gq_ref, gk_ref, gv_ref, late_ref, up_ref, squares_ref, ends_ref,
    own_ref, other_ref, grad_ref, total, sums, *, shard, four
):
    step = pl.program_id(0)

    @pl.when(step == 0)
    def _():
        total[...] = jnp.zeros_like(total)
        sums[...] = jnp.zeros_like(sums)

    joined = jnp.concatenate([gq_ref[...], gk_ref[...], gv_ref[...]], axis=1)
    width = 3 * GROUP
    grad = dot(joined, w_ref[:, :width], NT)

    @pl.when(step < 2)
    def _():
        own_ref[...] = grad.astype(BF)

    @pl.when(step >= 2)
    def _():
        other_ref[...] = grad.astype(BF)

    total[...] += dot(n_ref[...], joined, TN)
    unit, _ = norm_parts(x_ref[...].astype(F32))
    sums[0:1] += column_sums(grad * unit)
    sums[1:2] += column_sums(grad)
    sums[2:3, :width] += column_sums(joined.astype(F32))

    @pl.when(step == pl.num_programs(0) - 1)
    def _():
        hot, part = bias_places(place_ref[0], shard)
        bias = sums[2:3, :width]
        spread = [
            dot(jnp.broadcast_to(jnp.where(part == j, bias, 0.0), (8, width)).astype(BF), hot, NT)
            for j in range(3)
        ]
        rows = [sums[0:1], sums[1:2], *[part[0:1] for part in spread]]
        rows += [late_ref[0:1], late_ref[1:2], late_ref[2:3]]
        wide = up_ref.shape[1]
        tall = 2 * wide * shard // D
        column = lax.broadcasted_iota(jnp.int32, (1, wide), 1)
        source = (column // tall * 2 + place_ref[0] % 2) * shard + column % shard
        which = column % tall // shard
        hot = lax.broadcasted_iota(jnp.int32, (D, wide), 0) == source
        ups = jnp.concatenate(
            [jnp.where(which == j, up_ref[0:1], 0.0) for j in range(tall // shard)]
            + [jnp.zeros((8 - tall // shard, wide), F32)],
            axis=0,
        )
        ups = dot(ups.astype(BF), jnp.where(hot, 1.0, 0.0).astype(BF), NT)
        rows += [ups[j : j + 1] for j in range(tall // shard)]
        rows += [late_ref[3:4]]
        for ref, j in ((squares_ref, 0), (squares_ref, 1), (squares_ref, 2), (ends_ref, 0), (ends_ref, 1)):
            rows += [jnp.broadcast_to(jnp.sum(ref[j : j + 1], axis=1, keepdims=True), (1, D))]
        rows += [jnp.zeros((128 - len(rows), D), F32)]
        vectors = jnp.concatenate(rows, axis=0).T.astype(BF)
        height = D // 8 if four else D
        for block in range(D // height):
            start = 0
            if four:
                flip = block // 2 ^ place_ref[3]
                start = pl.multiple_of(
                    (level_of(flip) * 2 + (block % 2 ^ place_ref[2])) * height, height
                )
            here = slice(block * height, (block + 1) * height)
            grad_ref[pl.ds(start, height), :width] = total[here].astype(BF)
            grad_ref[pl.ds(start, height), width:] = vectors[here]


def project_back(place, normed, values, weight, parts, late, shard, four, rows=512):
    count = normed.shape[0]
    width = 3 * GROUP

    def row_block(cols):
        return pl.BlockSpec((rows, cols), lambda i, p: (i, 0))

    def whole(*dims):
        return pl.BlockSpec(dims, lambda i, p: (0, 0))

    half = shape((count // 2, D), BF)
    return pl.pallas_call(
        functools.partial(project_back_kernel, shard=shard, four=four),
        grid_spec=pltpu.PrefetchScalarGridSpec(
            num_scalar_prefetch=1,
            grid=(count // rows,),
            in_specs=[row_block(D), row_block(D), whole(*weight.shape)]
            + [row_block(GROUP)] * 3
            + [whole(*part.shape) for part in late],
            out_specs=[
                pl.BlockSpec((rows, D), lambda i, p: (jnp.minimum(i, 1), 0)),
                pl.BlockSpec((rows, D), lambda i, p: (jnp.maximum(i - 2, 0), 0)),
                whole(*weight.shape),
            ],
            scratch_shapes=[pltpu.VMEM((D, width), F32), pltpu.VMEM((8, D), F32)],
        ),
        out_shape=[half, half, shape(weight.shape, BF)],
        name="project_back",
        **params(),
    )(place, normed, values, weight, *parts, *late)


def first_back_kernel(x_ref, gm_ref, t_ref, a_ref, b_ref, c_ref, out_ref):
    grad = a_ref[...].astype(F32) + b_ref[...].astype(F32) + c_ref[...].astype(F32)
    unit, scale = norm_parts(x_ref[...].astype(F32))
    out_ref[...] = gm_ref[...] + norm_back(unit, scale, grad, t_ref[0:1])


def first_back(tokens, grad_middle, vectors, parts, rows=256):
    full = pl.BlockSpec((rows, D), lambda i: (i, 0))
    return pl.pallas_call(
        first_back_kernel,
        grid=(tokens.shape[0] // rows,),
        in_specs=[full, full, pl.BlockSpec((16, D), lambda i: (0, 0)), full, full, full],
        out_specs=full,
        out_shape=shape(tokens.shape, F32),
        name="first_back",
        **params(),
    )(tokens, grad_middle, vectors, *parts)


def per_device(
    tokens,
    positions,
    ln1_gain,
    ln1_shift,
    qkv_weight,
    qkv_bias,
    out_weight,
    out_bias,
    ln2_gain,
    ln2_shift,
    up_weight,
    up_bias,
    down_weight,
    down_bias,
    cotangent,
):
    rows = tokens.shape[0]
    outer = lax.axis_size("o")
    o, y, x, c = (lax.axis_index(name) for name in ALL)
    ctx = 2 * x + c
    four = outer == 4
    place = jnp.stack([ctx, 2 * y + x, y, o]).astype(jnp.int32)
    shard = ln1_gain.shape[0]
    blocks = D // shard
    half_blocks = blocks // 2
    tall = up_bias.shape[0]
    ff_half = tall * half_blocks

    vector_parts = (
        ln1_gain,
        ln1_shift,
        qkv_bias,
        out_bias,
        ln2_gain,
        ln2_shift,
        up_bias,
        down_bias,
    )
    n_vectors = sum(part.shape[0] for part in vector_parts) // shard
    packed = pack(qkv_weight, [part.reshape(1, -1) for part in vector_parts])
    packed, down_weight, out_weight, up_weight = tie(packed, down_weight, out_weight, up_weight)
    packed = lax.all_to_all(packed, ("x", "c"), 0, 0, tiled=True).reshape(4 * shard, -1)

    up_parts = up_weight.reshape(shard, half_blocks, 2, tall)

    def column_half(which):
        return lax.dynamic_index_in_dim(up_parts, which, 2, keepdims=False).reshape(shard, -1)

    upper = jnp.concatenate(by_place(c, column_half(c), swap(column_half(1 - c), "c")), axis=0)

    packed, tokens, positions, upper, out_weight = tie(
        packed, tokens, positions, upper, out_weight
    )
    packed_far = far_half(packed)
    place_rows = jnp.zeros((16, D), BF).at[:3, :rows].set(positions.astype(BF))
    sent = jnp.concatenate([tokens, place_rows], axis=0)
    from_x = swap(sent, "x")
    out_far = far_half(out_weight)
    packed_far, out_far, packed, down_weight, out_weight = tie(
        packed_far, out_far, packed, down_weight, out_weight
    )
    lower_far = far_half(down_weight)
    out = near_half(out_weight, out_far)
    packed_pair, packed_near = near_half(packed, packed_far)
    packed_y = swap(packed_pair, "y")
    packed_near, packed_y, from_x, upper, lower_far, out = tie(
        packed_near, packed_y, from_x, upper, lower_far, out
    )
    out = all_blocks(out)
    out_x = swap(out, "x")
    if four:
        pieces = (packed_pair, packed_y, packed_near, swap(packed_near, "y"))
    else:
        pieces = (jnp.stack(by_place(y, packed_pair, packed_y), axis=1).reshape(1, D, -1),)
    lower = near_half(down_weight, lower_far)
    upper_far = far_half(upper)
    from_c = swap(jnp.stack([sent, from_x]), "c")
    clip_rows = jnp.concatenate(
        [tokens, from_x[:rows], from_c[0, :rows], from_c[1, :rows]], axis=0
    )
    places = jnp.concatenate(
        [
            positions.astype(F32),
            from_x[rows : rows + 3, :rows].astype(F32),
            from_c[0, rows : rows + 3, :rows].astype(F32),
            from_c[1, rows : rows + 3, :rows].astype(F32),
        ],
        axis=1,
    )
    cosine, sine = rotary_tables(places, PAIR)
    pieces, lower, out_x, upper, upper_far, clip_rows, cosine, sine = tie(
        pieces, lower, out_x, upper, upper_far, clip_rows, cosine, sine
    )
    lower = all_blocks(lower)
    out_y = swap(jnp.stack([out, out_x]), "y")
    lower_x, lower_y = swap(lower, "x"), swap(lower, "y")
    upper = near_half(upper, upper_far)
    normed, q, k, v, vectors, gathered = project(place, clip_rows, pieces, cosine, sine, shard)

    q, upper, out_y = tie(q, upper, out_y)
    upper = all_blocks(upper)
    upper_x, upper_y = swap(upper, "x"), swap(upper, "y")
    cotangent_other = swap(cotangent, "c")
    mixed_far, wide_far, logs_far = attend(q, k, v, 1)
    if four:
        out_own = jnp.stack([out, out_x, out_y[0], out_y[1]])
        out_sources = (out_own, swap(out_own, "c"))
    else:
        out_half = jnp.stack(place_four(y, x, (out, out_x, out_y[0], out_y[1])), axis=1)
        out_half = out_half.reshape(half_blocks, shard, D)
        out_half = jnp.stack(by_place(c, out_half, swap(out_half, "c")), axis=1)
        out_sources = (out_half.reshape(1, 1, D, D), out_half.reshape(1, 1, D, D))
    mixed_far, lower_x, lower_y, out_sources, cotangent_other, q = tie(
        mixed_far, lower_x, lower_y, out_sources, cotangent_other, q
    )
    came_x = swap(mixed_far, "x")
    mixed_near, wide_near, logs_near = attend(q, k, v, 0)
    mixed_near, came_x, upper_y, upper_x, lower_x = tie(
        mixed_near, came_x, upper_y, upper_x, lower_x
    )
    upper_xy = swap(upper_y, "x")
    lower_xy = swap(lower_x, "y")
    came_c = swap(jnp.concatenate([mixed_near[rows:], came_x[rows:]], axis=0), "c")
    mixed = (mixed_near, came_x, came_c)
    mid, normed_two, squares, out_full = middle(place, tokens, vectors, mixed, out_sources, four)

    normed_other = swap(normed_two, "c")
    if four:
        up_pieces = (upper, upper_x, upper_y, upper_xy)
        down_pieces = (lower, lower_x, lower_y, lower_xy)
    else:
        upper = jnp.stack(place_four(y, x, (upper, upper_x, upper_y, upper_xy)), axis=1)
        up_pieces = (upper.reshape(1, D, ff_half),)
        lower = jnp.stack(place_four(y, x, (lower, lower_x, lower_y, lower_xy)), axis=1)
        down_pieces = (lower.reshape(1, ff_half, D),)
    normed_two, bias_up = tie(normed_two, hidden_bias(place, vectors, ff_half, shard, tall))
    results = hidden(
        place,
        bias_up,
        normed_two,
        normed_other,
        cotangent,
        cotangent_other,
        up_pieces,
        down_pieces,
        shard,
    )
    up_bias_grad, gn, gn_sent, mlp, mlp_sent = results[:5]
    gn_came = swap(gn_sent, "c")
    mlp_came = swap(mlp_sent, "c")

    def quarter(values, flip):
        parts = values.reshape(outer, 4, -1, values.shape[-1])
        return lax.dynamic_index_in_dim(parts, (2 * y + x) ^ flip, 1, keepdims=False)

    if four:
        ups, downs = tuple(results[5:9]), tuple(results[9:])
    else:
        ups = tuple(quarter(results[5], flip) for flip in range(4))
        downs = ()
    grad_middle, go_own, go_x, go_c, go_xc, out_kept, out_sent, sums = middle_back(
        place, gn, gn_came, mid, cotangent, vectors, mixed, out_full, shard, four
    )
    go_c, ups = tie(go_c, ups)
    upper_passed = swap(ups[3], "y")
    go_came_c = swap(go_c, "c")
    go_came_x = swap(go_x, "x")
    go_came_xc = lax.ppermute(go_xc, ("x", "c"), DIAGONAL)
    if not four:
        out_grad = out_kept.reshape(half_blocks, 2, shard, D)
        out_sent = lax.dynamic_index_in_dim(out_grad, 1 - c, 1, keepdims=False)
        out_kept = lax.dynamic_index_in_dim(out_grad, c, 1, keepdims=False)
    out_came = swap(out_sent, "c")
    mlp_came, out_sent = tie(mlp_came, out_sent)
    final_low, ends = finish(mid, mlp, mlp_came, vectors, n_vectors - 1)
    go_came_c, out_came, final_low = tie(go_came_c, out_came, final_low)
    if four:
        downs = append(
            place,
            out_kept.reshape(4, 4, shard, D),
            out_came.reshape(4, 4, shard, D),
            downs,
        )
    else:
        out_sums = (out_kept + out_came).reshape(outer * 4, shard, D)
        lower_grad = results[6].reshape(outer * 4, tall, D)
        lower_grad = jnp.concatenate([lower_grad, out_sums], axis=1)
        downs = tuple(quarter(lower_grad, flip) for flip in range(4))

    downs, go_own, go_came_c, go_came_x, go_came_xc = tie(
        downs, go_own, go_came_c, go_came_x, go_came_xc
    )
    lower_passed = swap(downs[3], "x")
    first = attend_back(
        q, k, v, go_own, go_came_c, wide_near, logs_near, cosine, sine, 0
    )
    lower_passed, upper_passed, first, downs, ups = tie(
        lower_passed, upper_passed, first, downs, ups
    )
    upper_kept = swap(ups[2], "y")
    upper_second = swap(ups[1] + upper_passed, "x")
    lower_second = swap(downs[2] + lower_passed, "y")
    parts = attend_back(
        q, k, v, go_came_x, go_came_xc, wide_far, logs_far, cosine, sine, 1, before=first
    )
    upper_second, upper_kept, parts, downs = tie(upper_second, upper_kept, parts, downs)
    lower_kept = swap(downs[1], "x")
    upper_sum = near_sums(ups[0], upper_second, upper_kept)

    gn_low, gn_high, last = project_back(
        place,
        normed,
        clip_rows,
        gathered,
        parts,
        (sums, up_bias_grad, squares, ends),
        shard,
        four,
    )
    gn_low, gn_high, last, upper_sum, lower_kept, lower_second = tie(
        gn_low, gn_high, last, upper_sum, lower_kept, lower_second
    )
    gn_came = swap(gn_high, "c")

    cut = 512
    last = last.reshape(outer, 2, 4 * shard, -1)

    def over_y(values):
        axis = values.ndim - 3
        if four:
            kept, sent = (lax.index_in_dim(values, i, axis, keepdims=False) for i in (0, 1))
        else:
            kept = lax.dynamic_index_in_dim(values, y, axis, keepdims=False)
            sent = lax.dynamic_index_in_dim(values, 1 - y, axis, keepdims=False)
        return kept.astype(F32) + swap(sent.astype(BF), "y").astype(F32)

    high = near_sums(last[..., cut:])
    low = over_y(last[..., :cut]).astype(BF)
    gn_came, low, high, upper_sum, lower_kept = tie(gn_came, low, high, upper_sum, lower_kept)
    low = near_sums(low)
    high = far_sums(high)
    gn_x = swap(gn_low[rows:] + gn_came[rows:], "x")
    upper_grad = far_sums(upper_sum).astype(BF).reshape(2, shard, -1)
    lower_sum = near_sums(downs[0], lower_second, lower_kept)
    low, high = tie(low, high)
    low = far_sums(low)
    high = over_y(high)
    low, high, lower_sum, upper_grad = tie(low, high, lower_sum, upper_grad)
    upper_kept = lax.dynamic_index_in_dim(upper_grad, c, 0, keepdims=False)
    upper_came = swap(lax.dynamic_index_in_dim(upper_grad, 1 - c, 0, keepdims=False), "c")
    last = jnp.concatenate([low.astype(BF), high.astype(BF)], axis=1)
    last, tokens = tie(last, tokens)
    input_grad = first_back(tokens, grad_middle, vectors, (gn_low, gn_came, gn_x))
    last = lax.all_to_all(last.reshape(4, shard, -1), ("x", "c"), 0, 0, tiled=True)
    last, input_grad = tie(last, input_grad)
    lower_grad = far_sums(lower_sum, last)
    upper_pair = by_place(c, upper_kept, upper_came)
    up_weight_grad = jnp.stack(
        [part.reshape(shard, half_blocks, tall) for part in upper_pair], axis=2
    )
    last = last.astype(F32)
    qkv_weight_grad = last[:, :, : 3 * GROUP].reshape(4, shard, 3, GROUP).transpose(1, 2, 0, 3)
    vector_grads = jnp.sum(last[:, :, 3 * GROUP : 3 * GROUP + n_vectors + 5], axis=0).T
    entry_count = rows * lax.axis_size(ALL) * D
    norm_stats = jnp.sqrt(vector_grads[n_vectors:, 0] / entry_count)

    return (
        final_low,
        input_grad,
        vector_grads[0],
        vector_grads[1],
        qkv_weight_grad.reshape(shard, 3 * D),
        vector_grads[2:5].reshape(-1),
        lower_grad[tall:],
        vector_grads[5],
        vector_grads[6],
        vector_grads[7],
        up_weight_grad.reshape(shard, -1).astype(F32),
        vector_grads[8 : n_vectors - 1].reshape(-1),
        lower_grad[:tall],
        vector_grads[n_vectors - 1],
        norm_stats,
    )


def solution(mesh):
    fine = Mesh(mesh.devices.reshape(-1, 2, 2, 2), ALL)
    rows, vector, whole = P(ALL, None), P(ALL), P()
    in_specs = (
        rows,
        P(None, ALL),
        vector,
        vector,
        rows,
        vector,
        rows,
        vector,
        vector,
        vector,
        rows,
        vector,
        rows,
        vector,
        rows,
    )
    out_specs = (
        rows,
        rows,
        vector,
        vector,
        rows,
        vector,
        rows,
        vector,
        vector,
        vector,
        rows,
        vector,
        rows,
        vector,
        whole,
    )
    return jax.shard_map(
        per_device, mesh=fine, in_specs=in_specs, out_specs=out_specs, check_vma=False
    )
```

```python
import functools
import math

import jax
import jax.numpy as jnp
from jax import lax
from jax.experimental import pallas as pl
from jax.experimental.pallas import tpu as pltpu
from jax.sharding import Mesh
from jax.sharding import PartitionSpec as P

D = 1024
HD = 64
GAP = HD // 6
PAIR = 2 * HD
GROUP = D // 4
EPSILON = 1e-06
BF = jnp.bfloat16
F32 = jnp.float32
ALL = ("o", "y", "x", "c")
SWAP = ((0, 1), (1, 0))
DIAGONAL = ((0, 3), (1, 2), (2, 1), (3, 0))
NT = (((1,), (1,)), ((), ()))
NN = (((1,), (0,)), ((), ()))
TN = (((0,), (0,)), ((), ()))
VMEM_LIMIT = 58 * 2**20
VMEM_MOST = 63 * 2**20
SMALL = pl.CostEstimate(flops=10**6, bytes_accessed=2**16, transcendentals=0)
MASK = (0, 2, 1, 3)


def dot(left, right, dims=NN):
    return lax.dot_general(left, right, dims, preferred_element_type=F32)


def swap(values, axis):
    return lax.ppermute(values, axis, SWAP)


def tie(*values):
    return lax.optimization_barrier(values)


def by_place(flag, own, other):
    return jnp.where(flag == 0, own, other), jnp.where(flag == 0, other, own)


def place_four(high, low, parts):
    first = by_place(low, parts[0], parts[1])
    second = by_place(low, parts[2], parts[3])
    even = by_place(high, first[0], second[0])
    odd = by_place(high, first[1], second[1])
    return even[0], odd[0], even[1], odd[1]


def far(values):
    return lax.ppermute(values, "o", [(i, i ^ 2) for i in range(4)])


def near(values):
    return lax.ppermute(values, "o", [(i, i ^ 1) for i in range(4)])


def level_place(own, level):
    return own ^ (level % 2 * 2 + level // 2)


def far_half(values):
    if lax.axis_size("o") != 4:
        return lax.all_gather(values, "o", axis=0, tiled=False)
    return far(values)


def near_half(values, came):
    if lax.axis_size("o") != 4:
        return came, came
    pair = jnp.stack([values, came])
    return pair, near(pair)


def all_blocks(halves):
    if lax.axis_size("o") != 4:
        return halves[0]
    return jnp.concatenate(halves, axis=0)


def near_sums(*terms):
    if lax.axis_size("o") != 4:
        return sum(terms)
    kept = sum(term[:2].astype(F32) for term in terms)
    return kept, near(sum(term[2:].astype(F32) for term in terms).astype(BF))


def far_sums(values, *earlier):
    if lax.axis_size("o") != 4:
        return lax.psum_scatter(values, "o", scatter_dimension=0, tiled=False).astype(F32)
    kept, came = values
    sums = kept + came.astype(F32)
    came = far(sums[1].astype(BF))
    if earlier:
        came = tie(came, *earlier)[0]
    return sums[0] + came.astype(F32)


def norm_parts(values):
    average = jnp.mean(values, axis=-1, keepdims=True)
    centred = values - average
    spread = jnp.mean(centred * centred, axis=-1, keepdims=True)
    scale = lax.rsqrt(spread + EPSILON)
    return centred * scale, scale


def norm_back(unit, scale, grad, gain):
    scaled = grad * gain
    return scale * (
        scaled
        - jnp.mean(scaled, axis=-1, keepdims=True)
        - unit * jnp.mean(scaled * unit, axis=-1, keepdims=True)
    )


def rotary_tables(places, width):
    column = jnp.arange(width) % HD
    segment = column // (2 * GAP)
    within = column % (2 * GAP)
    freq_index = (within % GAP).astype(F32)
    frequency = jnp.power(10000.0, -freq_index / GAP)
    angles = jnp.zeros((places.shape[1], width), F32)
    for axis_num in range(3):
        angles = (
            angles
            + places[axis_num][:, None] * jnp.where(segment == axis_num, frequency, 0.0)[None, :]
        )
    rotated = segment < 3
    return jnp.where(rotated, jnp.cos(angles), 1.0), jnp.where(rotated, jnp.sin(angles), 0.0)


def shifted(values, leading):
    ahead = pltpu.roll(values, PAIR - GAP, 1)
    behind = pltpu.roll(values, GAP, 1)
    return jnp.where(leading, -ahead, behind)


def leading_lanes():
    lane = lax.broadcasted_iota(jnp.int32, (1, PAIR), 1)
    return lane % HD % (2 * GAP) < GAP


def column_sums(values):
    return jnp.sum(values, axis=0, keepdims=True)


def params(aliases=None, limit=VMEM_LIMIT):
    return dict(
        compiler_params=pltpu.CompilerParams(vmem_limit_bytes=limit),
        cost_estimate=SMALL,
        input_output_aliases=aliases or {},
    )


def shape(dims, kind):
    return jax.ShapeDtypeStruct(dims, kind)


def pack_kernel(w_ref, *refs):
    vectors, out_ref = refs[:-1], refs[-1]
    shard = w_ref.shape[0]
    rows = []
    for ref in vectors:
        values = ref[...].astype(F32)
        rows += [values[:, low : low + shard] for low in range(0, values.shape[1], shard)]
    columns = jnp.concatenate(rows + [jnp.zeros((128 - len(rows), shard), F32)], axis=0).T
    for place in range(4):
        for part in range(3):
            start = part * D + place * GROUP
            out_ref[place, :, part * GROUP : (part + 1) * GROUP] = w_ref[:, start : start + GROUP]
        out_ref[place, :, 3 * GROUP :] = columns.astype(BF)


def pack(weight, vectors):
    return pl.pallas_call(
        pack_kernel,
        out_shape=shape((4, weight.shape[0], 3 * GROUP + 128), BF),
        name="pack",
        **params(),
    )(weight, *vectors)


def bias_places(place, shard):
    column = lax.broadcasted_iota(jnp.int32, (1, 3 * GROUP), 1)
    target = column // GROUP * D + place * GROUP + column % GROUP
    source = target // (3 * shard) * shard + target % shard
    hot = lax.broadcasted_iota(jnp.int32, (D, 3 * GROUP), 0) == source
    return jnp.where(hot, 1.0, 0.0).astype(BF), target % (3 * shard) // shard


def load_blocks(sources, target, semaphores):
    found = []
    for source, index, place in sources:
        block = source if isinstance(index, slice) else source.at[index]
        height = block.shape[0]
        start = pl.multiple_of(place * height, height)
        found.append(
            pltpu.make_async_copy(
                block, target.at[pl.ds(start, height)], semaphores.at[len(found)]
            )
        )
    return found


def piece_blocks(arrays, place):
    if len(arrays) == 1:
        return [(arrays[0], 0, 0)]
    return [
        (source, level, level_place(place[3], level) * 4 + (place[1] ^ flip))
        for flip, source in enumerate(arrays)
        for level in range(4)
    ]


def project_kernel(place_ref, x_ref, cos_ref, sin_ref, *refs, shard, pieces):
    sources, refs = refs[:pieces], refs[pieces:]
    n_ref, q_ref, k_ref, v_ref, t_ref, w_ref, b_ref, semaphores = refs

    @pl.when(pl.program_id(0) == 0)
    def _():
        if pieces == 1:
            blocks = [(sources[0], 0, 0)]
        else:
            blocks = [
                (
                    source,
                    level,
                    (level_place(place_ref[3], level) ^ (piece // 2)) * 2
                    + (place_ref[2] ^ (piece % 2)),
                )
                for piece, source in enumerate(sources)
                for level in range(2)
            ]
        copies = load_blocks(blocks, w_ref, semaphores)
        for copy in copies:
            copy.start()
        for copy in copies:
            copy.wait()
        t_ref[...] = w_ref[:, 3 * GROUP :].astype(F32).T[: t_ref.shape[0]]
        hot, part = bias_places(place_ref[0], shard)
        found = dot(t_ref[...].astype(BF), hot)
        bias = jnp.where(part == 0, found[2:3], jnp.where(part == 1, found[3:4], found[4:5]))
        b_ref[...] = jnp.broadcast_to(bias, b_ref.shape)

    unit, _ = norm_parts(x_ref[...].astype(F32))
    normed = (unit * t_ref[0:1] + t_ref[1:2]).astype(BF)
    n_ref[...] = normed
    joined = dot(normed, w_ref[:, : 3 * GROUP]) + b_ref[0:1]
    cosine, sine, leading = cos_ref[...], sin_ref[...], leading_lanes()
    for ref, start, factor in ((q_ref, 0, 1.0 / math.sqrt(HD)), (k_ref, GROUP, 1.0)):
        for low in range(0, GROUP, PAIR):
            part = joined[:, start + low : start + low + PAIR]
            turned = part * cosine + shifted(part, leading) * sine
            ref[:, low : low + PAIR] = (turned * factor).astype(BF)
    v_ref[...] = joined[:, 2 * GROUP :].astype(BF)


def project(place, values, pieces, cosine, sine, shard, rows=512):
    count = values.shape[0]
    width = pieces[0].shape[-1]

    def part(cols):
        return pl.BlockSpec((rows, cols), lambda i, p: (i, 0))

    def whole(*dims):
        return pl.BlockSpec(dims, lambda i, p: (0, 0))

    return pl.pallas_call(
        functools.partial(project_kernel, shard=shard, pieces=len(pieces)),
        grid_spec=pltpu.PrefetchScalarGridSpec(
            num_scalar_prefetch=1,
            grid=(count // rows,),
            in_specs=[part(D), part(PAIR), part(PAIR)]
            + [pl.BlockSpec(memory_space=pl.ANY)] * len(pieces),
            out_specs=[part(D), part(GROUP), part(GROUP), part(GROUP), whole(16, D), whole(D, width)],
            scratch_shapes=[
                pltpu.VMEM((8, 3 * GROUP), F32),
                pltpu.SemaphoreType.DMA((len(pieces) * pieces[0].shape[0],)),
            ],
        ),
        out_shape=[
            shape((count, D), BF),
            shape((count, GROUP), BF),
            shape((count, GROUP), BF),
            shape((count, GROUP), BF),
            shape((16, D), F32),
            shape((D, width), BF),
        ],
        name="project",
        **params(),
    )(place, values, cosine, sine, *pieces)


def attend_kernel(q_ref, k_ref, v_ref, *refs):
    o_ref, wide_ref, lse_ref = refs[-3:]
    q, k, v = q_ref[...], k_ref[...], v_ref[...]
    lane = lax.broadcasted_iota(jnp.int32, (1, PAIR), 1)
    weights, totals, logs = [], [], []
    for scores in [dot(jnp.where(mine, q, 0), k, NT) for mine in (lane < HD, lane >= HD)]:
        top = jnp.max(scores, axis=1, keepdims=True)
        weight = jnp.exp(scores - top)
        total = jnp.sum(weight, axis=1, keepdims=True)
        weights.append(weight.astype(BF))
        totals.append(total)
        logs.append(top + jnp.log(total))
    mixed = [dot(weight, v) / total for weight, total in zip(weights, totals)]
    out = jnp.where(lane < HD, mixed[0], mixed[1])
    o_ref[...] = out.astype(BF)
    wide_ref[...] = out
    lse_ref[...] = jnp.where(lane < HD, logs[0], logs[1])


def attend(q, k, v, side, pair=None, before=None, rows=256):
    count = q.shape[0]
    half = count // 2
    per = count // 4 // rows
    pairs = GROUP // PAIR if pair is None else 1
    first = 0 if pair is None else pair

    def block(i):
        return i // per * 2 * per + side * per + i % per

    full = pl.BlockSpec((count, PAIR), lambda j, i: (0, first + j))
    out = pl.BlockSpec((rows, PAIR), lambda j, i: (i, first + j))
    before = list(before or ())
    return pl.pallas_call(
        attend_kernel,
        grid=(pairs, half // rows),
        in_specs=[pl.BlockSpec((rows, PAIR), lambda j, i: (block(i), first + j)), full, full]
        + [pl.BlockSpec(memory_space=pl.ANY)] * len(before),
        out_specs=[out, out, out],
        out_shape=[shape((half, GROUP), BF), shape((half, GROUP), F32), shape((half, GROUP), F32)],
        name="attend",
        **params({3: 0, 4: 1, 5: 2} if before else None),
    )(q, k, v, *before)


def attend_back_kernel(
    q_ref, go_ref, go_other_ref, wide_ref, lse_ref, k_ref, v_ref, cos_ref, sin_ref, *refs, last, block
):
    step, rows = pl.program_id(1), q_ref.shape[0]
    if last:
        k_start, v_start, _, gq_ref, gk_ref, gv_ref, k_sum, v_sum = refs
    else:
        gq_ref, k_sum, v_sum = refs

    @pl.when(step == 0)
    def _():
        if last:
            k_sum[...] = k_start[...]
            v_sum[...] = v_start[...]
        else:
            k_sum[...] = jnp.zeros_like(k_sum)
            v_sum[...] = jnp.zeros_like(v_sum)

    q, k, v, lse = q_ref[...], k_ref[...], v_ref[...], lse_ref[...]
    go = jnp.where(step < pl.num_programs(1) // 2, go_ref[...], go_other_ref[...])
    lane = lax.broadcasted_iota(jnp.int32, (1, PAIR), 1)
    leading = leading_lanes()
    product = go.astype(F32) * wide_ref[...]
    grads = []
    for head in range(2):
        mine = (lane < HD) if head == 0 else (lane >= HD)
        q_head, go_head = jnp.where(mine, q, 0), jnp.where(mine, go, 0)
        inner = jnp.sum(jnp.where(mine, product, 0.0), axis=1, keepdims=True)
        weight = jnp.exp(dot(q_head, k, NT) - lse[:, HD * head : HD * head + 1])
        pull = (weight * (dot(go_head, v, NT) - inner)).astype(BF)
        grads.append(dot(pull, k))
        k_sum[...] += dot(q_head.T, pull)
        v_sum[...] += dot(go_head.T, weight.astype(BF))
    grad = jnp.where(lane < HD, grads[0], grads[1])
    here = pl.ds(pl.multiple_of(block(step) * rows, rows), rows)
    grad = grad * cos_ref[here] - shifted(grad * sin_ref[here], leading)
    gq_ref[...] = (grad * (1.0 / math.sqrt(HD))).astype(BF)

    if last:

        @pl.when(step == pl.num_programs(1) - 1)
        def _():
            grad = k_sum[...].T
            grad = grad * cos_ref[...] - shifted(grad * sin_ref[...], leading)
            gk_ref[...] = grad.astype(BF)
            gv_ref[...] = v_sum[...].T.astype(BF)


def attend_back(q, k, v, go, go_other, wide, lse, cosine, sine, side, before=None, rows=256):
    count = q.shape[0]
    half = count // 2
    per = count // 4 // rows
    last = before is not None

    def block(i):
        return i // per * 2 * per + side * per + i % per

    part = pl.BlockSpec((rows, PAIR), lambda pair, i: (block(i), pair))
    own = pl.BlockSpec((rows, PAIR), lambda pair, i: (i, pair))
    full = pl.BlockSpec((count, PAIR), lambda pair, i: (0, pair))
    table = pl.BlockSpec((count, PAIR), lambda pair, i: (0, 0))
    turned = pl.BlockSpec((PAIR, count), lambda pair, i: (pair, 0))
    sums = shape((GROUP, count), F32)
    grad = shape((count, GROUP), BF)
    low = pl.BlockSpec((rows, PAIR), lambda pair, i: (jnp.minimum(i, per - 1), pair))
    high = pl.BlockSpec((rows, PAIR), lambda pair, i: (jnp.maximum(i - per, 0), pair))
    in_specs = [part, low, high, own, own, full, full, table, table]
    operands = [q, go, go_other, wide, lse, k, v, cosine, sine]
    if last:
        in_specs += [turned, turned, pl.BlockSpec(memory_space=pl.ANY)]
        operands += [before[1], before[2], before[0]]
        out_specs, out_shape = [part, full, full], [grad, grad, grad]
        scratch = [pltpu.VMEM((PAIR, count), F32)] * 2
    else:
        out_specs, out_shape, scratch = [part, turned, turned], [grad, sums, sums], []
    return pl.pallas_call(
        functools.partial(attend_back_kernel, last=last, block=block),
        grid=(GROUP // PAIR, half // rows),
        in_specs=in_specs,
        out_specs=out_specs,
        out_shape=out_shape,
        scratch_shapes=scratch,
        name="attend_back",
        **params({11: 0} if last else None),
    )(*operands)


def middle_kernel(place_ref, x_ref, t_ref, *refs, four):
    o_refs, sources, refs = refs[:4], refs[4:6], refs[6:]
    mid_ref, n_ref, s_ref, w_ref, semaphores = refs

    @pl.when(pl.program_id(0) == 0)
    def _():
        s_ref[...] = jnp.zeros_like(s_ref)
        if four:
            blocks = [
                (
                    source.at[flip],
                    level,
                    (level_place(place_ref[3], level) * 4 + (place_ref[1] ^ flip)) * 2
                    + (place_ref[0] % 2 ^ other),
                )
                for other, source in enumerate(sources)
                for flip in range(4)
                for level in range(4)
            ]
        else:
            blocks = [(sources[0].at[0], 0, 0)]
        copies = load_blocks(blocks, w_ref, semaphores)
        for copy in copies:
            copy.start()
        for copy in copies:
            copy.wait()

    x = x_ref[...].astype(F32)
    attn = t_ref[5:6]
    for mask, o_ref in zip(MASK, o_refs):
        start = pl.multiple_of((place_ref[0] ^ mask) * GROUP, GROUP)
        attn = attn + dot(o_ref[...], w_ref[pl.ds(start, GROUP)])
    mid = x + attn
    mid_ref[...] = mid
    unit, _ = norm_parts(mid)
    n_ref[...] = (unit * t_ref[6:7] + t_ref[7:8]).astype(BF)
    s_ref[0:1] += column_sums(x * x)
    s_ref[1:2] += column_sums(attn * attn)
    s_ref[2:3] += column_sums(mid * mid)


def group_specs():
    return [
        pl.BlockSpec((GROUP, D), lambda i, p, mask=mask: (p[0] ^ mask, 0)) for mask in MASK
    ]


def mixed_specs(count, rows):
    first = pl.BlockSpec((rows, GROUP), lambda i, p: (i, 0))
    second = pl.BlockSpec((rows, GROUP), lambda i, p: (i + count // rows, 0))
    return [first, first, first, second]


def middle(place, tokens, vectors, mixed, sources, four, rows=256):
    count = tokens.shape[0]
    full = pl.BlockSpec((rows, D), lambda i, p: (i, 0))

    def whole(*dims):
        return pl.BlockSpec(dims, lambda i, p: (0, 0))

    return pl.pallas_call(
        functools.partial(middle_kernel, four=four),
        grid_spec=pltpu.PrefetchScalarGridSpec(
            num_scalar_prefetch=1,
            grid=(count // rows,),
            in_specs=[full, whole(16, D)]
            + mixed_specs(count, rows)
            + [pl.BlockSpec(memory_space=pl.ANY)] * 2,
            out_specs=[full, full, whole(8, D), whole(D, D)],
            scratch_shapes=[pltpu.SemaphoreType.DMA((32,))],
        ),
        out_shape=[
            shape((count, D), F32),
            shape((count, D), BF),
            shape((8, D), F32),
            shape((D, D), BF),
        ],
        name="middle",
        **params(),
    )(place, tokens, vectors, *mixed, mixed[2], *sources)


def hidden_bias_kernel(place_ref, t_ref, out_ref, *, shard, tall):
    chunk = out_ref.shape[1]
    column = lax.broadcasted_iota(jnp.int32, (1, chunk), 1) + pl.program_id(0) * chunk
    source = (column // tall * 2 + place_ref[0] % 2) * shard + column % shard
    which = column % tall // shard
    hot = lax.broadcasted_iota(jnp.int32, (D, chunk), 0) == source
    found = dot(t_ref[...].astype(BF), jnp.where(hot, 1.0, 0.0).astype(BF))
    bias = jnp.zeros((1, chunk), F32)
    for row in range(tall // shard):
        bias = jnp.where(which == row, found[8 + row : 9 + row], bias)
    out_ref[...] = jnp.broadcast_to(bias, out_ref.shape)


def hidden_bias(place, vectors, width, shard, tall, chunk=512):
    return pl.pallas_call(
        functools.partial(hidden_bias_kernel, shard=shard, tall=tall),
        grid_spec=pltpu.PrefetchScalarGridSpec(
            num_scalar_prefetch=1,
            grid=(width // chunk,),
            in_specs=[pl.BlockSpec((16, D), lambda i, p: (0, 0))],
            out_specs=pl.BlockSpec((8, chunk), lambda i, p: (0, i)),
        ),
        out_shape=shape((8, width), F32),
        name="hidden_bias",
        **params(),
    )(place, vectors)


def hidden_kernel(place_ref, bias_ref, *refs, pieces):
    rows_in, refs = refs[:4], refs[4:]
    up_pieces, down_pieces, refs = refs[:pieces], refs[pieces : 2 * pieces], refs[2 * pieces :]
    b_ref, gn_ref, gn_other_ref, mlp_ref, mlp_other_ref = refs[:5]
    up_outs, down_outs = refs[5 : 5 + pieces], refs[5 + pieces : 5 + 2 * pieces]
    up, down, normed, cot, gn_sum, mlp_sum, up_total, down_total, *semaphores = refs[5 + 2 * pieces :]
    step = pl.program_id(0)
    chunk = bias_ref.shape[1]
    rows = gn_ref.shape[0]
    up_sem, down_sem, normed_sem, cot_sem = semaphores

    @pl.when(step == 0)
    def _():
        copies = load_blocks([(ref, slice(None), i) for i, ref in enumerate(rows_in[:2])], normed, normed_sem)
        copies += load_blocks(piece_blocks(up_pieces, place_ref), up, up_sem)
        copies += load_blocks([(ref, slice(None), i) for i, ref in enumerate(rows_in[2:])], cot, cot_sem)
        copies += load_blocks(piece_blocks(down_pieces, place_ref), down, down_sem)
        for copy in copies:
            copy.start()
        gn_sum[...] = jnp.zeros_like(gn_sum)
        mlp_sum[...] = jnp.zeros_like(mlp_sum)
        for copy in copies:
            copy.wait()

    here = pl.ds(pl.multiple_of(step * chunk, chunk), chunk)
    up_part, down_part = up[:, here], down[here, :]
    upward = dot(normed[...], up_part) + bias_ref[0:1]
    grad_active = dot(cot[...], down_part, NT)
    bell = 0.5 * (1.0 + lax.erf(upward * 0.7071067811865476))
    active = (upward * bell).astype(BF)
    slope = bell + upward * jnp.exp(-0.5 * upward * upward) * (1.0 / math.sqrt(2.0 * math.pi))
    grad_up = (grad_active * slope).astype(BF)
    b_ref[...] = jnp.broadcast_to(column_sums(grad_up.astype(F32)), b_ref.shape)
    gn_sum[...] += dot(grad_up, up_part, NT)
    mlp_sum[...] += dot(active, down_part)
    up_grad = dot(normed[...], grad_up, TN)
    down_grad = dot(active, cot[...], TN)
    if pieces == 1:
        up_outs[0][...] = up_grad.astype(BF)
        down_outs[0][...] = down_grad.astype(BF)
    else:
        up_total[...] = up_grad
        down_total[...] = down_grad
        for flip in range(4):
            for place in range(4):
                start = pl.multiple_of((place * 4 + (place_ref[1] ^ flip)) * (D // 16), D // 16)
                level = level_of(place ^ place_ref[3])
                up_outs[flip][level] = up_total[pl.ds(start, D // 16)].astype(BF)
            start = pl.multiple_of((place_ref[1] ^ flip) * (chunk // 4), chunk // 4)
            down_outs[flip][0] = down_total[pl.ds(start, chunk // 4)].astype(BF)

    @pl.when(step == pl.num_programs(0) - 1)
    def _():
        gn_ref[...] = gn_sum[:rows]
        mlp_ref[...] = mlp_sum[:rows]
        gn_other_ref[...] = gn_sum[rows:].astype(BF)
        mlp_other_ref[...] = mlp_sum[rows:].astype(BF)


def hidden(place, bias, own, other, cot, cot_other, up_pieces, down_pieces, extra):
    rows = own.shape[0]
    width = up_pieces[0].shape[-1]
    pieces = len(up_pieces)
    blocks = pieces * up_pieces[0].shape[0]
    chunk = width // 4

    def whole(*dims):
        return pl.BlockSpec(dims, lambda i, p: (0, 0))

    if pieces == 1:
        grad_specs = [
            pl.BlockSpec((D, chunk), lambda i, p: (0, i)),
            pl.BlockSpec((chunk, D), lambda i, p: (i, 0)),
        ]
        grad_shapes = [shape((D, width), BF), shape((width, D), BF)]
    else:
        grad_specs = [pl.BlockSpec((4, D // 16, chunk), lambda i, p: (0, 0, i))] * 4
        grad_specs += [
            pl.BlockSpec((1, chunk // 4, D), lambda i, p: (level_of(i ^ p[3]), 0, 0))
        ] * 4
        grad_shapes = [shape((4, D // 16, width), BF)] * 4
        grad_shapes += [shape((4, chunk // 4 + extra, D), BF)] * 4
    wide, low = shape((rows, D), F32), shape((rows, D), BF)
    lane_part = pl.BlockSpec((8, chunk), lambda i, p: (0, i))
    return pl.pallas_call(
        functools.partial(hidden_kernel, pieces=pieces),
        grid_spec=pltpu.PrefetchScalarGridSpec(
            num_scalar_prefetch=1,
            grid=(4,),
            in_specs=[lane_part] + [pl.BlockSpec(memory_space=pl.ANY)] * (4 + 2 * pieces),
            out_specs=[lane_part] + [whole(rows, D)] * 4 + grad_specs,
            scratch_shapes=[
                pltpu.VMEM((D, width), BF),
                pltpu.VMEM((width, D), BF),
                pltpu.VMEM((2 * rows, D), BF),
                pltpu.VMEM((2 * rows, D), BF),
                pltpu.VMEM((2 * rows, D), F32),
                pltpu.VMEM((2 * rows, D), F32),
                pltpu.VMEM((D, chunk), F32),
                pltpu.VMEM((chunk, D), F32),
                pltpu.SemaphoreType.DMA((blocks,)),
                pltpu.SemaphoreType.DMA((blocks,)),
                pltpu.SemaphoreType.DMA((2,)),
                pltpu.SemaphoreType.DMA((2,)),
            ],
        ),
        out_shape=[shape((8, width), F32), wide, low, wide, low] + grad_shapes,
        name="hidden",
        **params(limit=VMEM_MOST),
    )(place, bias, own, other, cot, cot_other, *up_pieces, *down_pieces)


def finish_kernel(mid_ref, mlp_ref, came_ref, t_ref, out_ref, s_ref, *, row):
    @pl.when(pl.program_id(0) == 0)
    def _():
        s_ref[...] = jnp.zeros_like(s_ref)

    mlp = mlp_ref[...] + came_ref[...].astype(F32) + t_ref[row : row + 1]
    final = mid_ref[...] + mlp
    out_ref[...] = final.astype(BF)
    s_ref[0:1] += column_sums(mlp * mlp)
    s_ref[1:2] += column_sums(final * final)


def finish(mid, mlp, came, vectors, row, rows=256):
    full = pl.BlockSpec((rows, D), lambda i: (i, 0))
    return pl.pallas_call(
        functools.partial(finish_kernel, row=row),
        grid=(mid.shape[0] // rows,),
        in_specs=[full, full, full, pl.BlockSpec((16, D), lambda i: (0, 0))],
        out_specs=[full, pl.BlockSpec((8, D), lambda i: (0, 0))],
        out_shape=[shape(mid.shape, BF), shape((8, D), F32)],
        name="finish",
        **params(),
    )(mid, mlp, came, vectors)


def append_kernel(place_ref, *refs):
    kept_ref, came_ref, outs = refs[0], refs[1], refs[-4:]
    for flip, out in enumerate(outs):
        for place in range(4):
            row = place_ref[1] ^ flip
            out[level_of(place ^ place_ref[3])] = kept_ref[place, row] + came_ref[place, row]


def append(place, kept, came, quarters):
    shard = kept.shape[2]
    spot = (quarters[0].shape[1] - shard) // shard
    part = pl.BlockSpec((4, 4, shard, D), lambda i, p: (0, 0, 0, 0))
    out = pl.BlockSpec((4, shard, D), lambda i, p: (0, spot, 0))
    return pl.pallas_call(
        append_kernel,
        grid_spec=pltpu.PrefetchScalarGridSpec(
            num_scalar_prefetch=1,
            grid=(1,),
            in_specs=[part, part] + [pl.BlockSpec(memory_space=pl.ANY)] * 4,
            out_specs=[out] * 4,
        ),
        out_shape=[shape(quarter.shape, BF) for quarter in quarters],
        name="append",
        **params({3: 0, 4: 1, 5: 2, 6: 3}),
    )(place, kept, came, *quarters)


def level_of(flip):
    return flip % 2 * 2 + flip // 2


def middle_back_kernel(place_ref, gn_ref, gn_other_ref, mid_ref, cot_ref, t_ref, *refs, four):
    o_refs, w_refs, outs = refs[:4], refs[4:8], refs[8:]
    gm_ref, go_refs, kept_ref, sent_ref, s_ref, total = outs[0], outs[1:5], *outs[5:9]
    step = pl.program_id(0)

    @pl.when(step == 0)
    def _():
        s_ref[...] = jnp.zeros_like(s_ref)
        total[...] = jnp.zeros_like(total)

    grad_two = gn_ref[...] + gn_other_ref[...].astype(F32)
    cot = cot_ref[...].astype(F32)
    unit, scale = norm_parts(mid_ref[...])
    grad_middle = cot + norm_back(unit, scale, grad_two, t_ref[6:7])
    gm_ref[...] = grad_middle
    grad_attn = grad_middle.astype(BF)
    s_ref[0:1] += column_sums(grad_attn.astype(F32))
    s_ref[1:2] += column_sums(grad_two * unit)
    s_ref[2:3] += column_sums(grad_two)
    s_ref[3:4] += column_sums(cot)
    for mask, o_ref, w_ref, go_ref in zip(MASK, o_refs, w_refs, go_refs):
        go_ref[...] = dot(grad_attn, w_ref[...], NT).astype(BF)
        start = pl.multiple_of((place_ref[0] ^ mask) * GROUP, GROUP)
        total[pl.ds(start, GROUP)] += dot(o_ref[...], grad_attn, TN)

    @pl.when(step == pl.num_programs(0) - 1)
    def _():
        if not four:
            kept_ref[...] = total[...].astype(BF)
            sent_ref[...] = jnp.zeros_like(sent_ref)
            return
        blocks, shard = kept_ref.shape[:2]
        for other, ref in enumerate((kept_ref, sent_ref)):
            for block in range(blocks):
                start = pl.multiple_of((2 * block + (place_ref[0] % 2 ^ other)) * shard, shard)
                ref[block] = total[pl.ds(start, shard)].astype(BF)


def middle_back(place, gn, gn_other, mid, cot, vectors, mixed, weight, shard, four, rows=256):
    count = mid.shape[0]
    full = pl.BlockSpec((rows, D), lambda i, p: (i, 0))
    part = pl.BlockSpec((rows, GROUP), lambda i, p: (i, 0))

    def whole(*dims):
        return pl.BlockSpec(dims, lambda i, p: (0, 0))

    if four:
        half = (D // (2 * shard), shard, D)
        out_specs = [pl.BlockSpec(half, lambda i, p: (0, 0, 0))] * 2
        out_shapes = [shape(half, BF)] * 2
    else:
        out_specs = [whole(D, D), whole(8, D)]
        out_shapes = [shape((D, D), BF), shape((8, D), BF)]
    return pl.pallas_call(
        functools.partial(middle_back_kernel, four=four),
        grid_spec=pltpu.PrefetchScalarGridSpec(
            num_scalar_prefetch=1,
            grid=(count // rows,),
            in_specs=[full, full, full, full, whole(16, D)]
            + mixed_specs(count, rows)
            + group_specs(),
            out_specs=[full] + [part] * 4 + out_specs + [whole(8, D)],
            scratch_shapes=[pltpu.VMEM((D, D), F32)],
        ),
        out_shape=[shape((count, D), F32)]
        + [shape((count, GROUP), BF)] * 4
        + out_shapes
        + [shape((8, D), F32)],
        name="middle_back",
        **params(),
    )(place, gn, gn_other, mid, cot, vectors, *mixed, mixed[2], *([weight] * 4))


def project_back_kernel(
    place_ref, n_ref, x_ref, w_ref, gq_ref, gk_ref, gv_ref, late_ref, up_ref, squares_ref, ends_ref,
    own_ref, other_ref, grad_ref, total, sums, *, shard, four
):
    step = pl.program_id(0)

    @pl.when(step == 0)
    def _():
        total[...] = jnp.zeros_like(total)
        sums[...] = jnp.zeros_like(sums)

    joined = jnp.concatenate([gq_ref[...], gk_ref[...], gv_ref[...]], axis=1)
    width = 3 * GROUP
    grad = dot(joined, w_ref[:, :width], NT)

    @pl.when(step < 2)
    def _():
        own_ref[...] = grad.astype(BF)

    @pl.when(step >= 2)
    def _():
        other_ref[...] = grad.astype(BF)

    total[...] += dot(n_ref[...], joined, TN)
    unit, _ = norm_parts(x_ref[...].astype(F32))
    sums[0:1] += column_sums(grad * unit)
    sums[1:2] += column_sums(grad)
    sums[2:3, :width] += column_sums(joined.astype(F32))

    @pl.when(step == pl.num_programs(0) - 1)
    def _():
        hot, part = bias_places(place_ref[0], shard)
        bias = sums[2:3, :width]
        spread = [
            dot(jnp.broadcast_to(jnp.where(part == j, bias, 0.0), (8, width)).astype(BF), hot, NT)
            for j in range(3)
        ]
        rows = [sums[0:1], sums[1:2], *[part[0:1] for part in spread]]
        rows += [late_ref[0:1], late_ref[1:2], late_ref[2:3]]
        wide = up_ref.shape[1]
        tall = 2 * wide * shard // D
        column = lax.broadcasted_iota(jnp.int32, (1, wide), 1)
        source = (column // tall * 2 + place_ref[0] % 2) * shard + column % shard
        which = column % tall // shard
        hot = lax.broadcasted_iota(jnp.int32, (D, wide), 0) == source
        ups = jnp.concatenate(
            [jnp.where(which == j, up_ref[0:1], 0.0) for j in range(tall // shard)]
            + [jnp.zeros((8 - tall // shard, wide), F32)],
            axis=0,
        )
        ups = dot(ups.astype(BF), jnp.where(hot, 1.0, 0.0).astype(BF), NT)
        rows += [ups[j : j + 1] for j in range(tall // shard)]
        rows += [late_ref[3:4]]
        for ref, j in ((squares_ref, 0), (squares_ref, 1), (squares_ref, 2), (ends_ref, 0), (ends_ref, 1)):
            rows += [jnp.broadcast_to(jnp.sum(ref[j : j + 1], axis=1, keepdims=True), (1, D))]
        rows += [jnp.zeros((128 - len(rows), D), F32)]
        vectors = jnp.concatenate(rows, axis=0).T.astype(BF)
        height = D // 8 if four else D
        for block in range(D // height):
            start = 0
            if four:
                flip = block // 2 ^ place_ref[3]
                start = pl.multiple_of(
                    (level_of(flip) * 2 + (block % 2 ^ place_ref[2])) * height, height
                )
            here = slice(block * height, (block + 1) * height)
            grad_ref[pl.ds(start, height), :width] = total[here].astype(BF)
            grad_ref[pl.ds(start, height), width:] = vectors[here]


def project_back(place, normed, values, weight, parts, late, shard, four, rows=512):
    count = normed.shape[0]
    width = 3 * GROUP

    def row_block(cols):
        return pl.BlockSpec((rows, cols), lambda i, p: (i, 0))

    def whole(*dims):
        return pl.BlockSpec(dims, lambda i, p: (0, 0))

    half = shape((count // 2, D), BF)
    return pl.pallas_call(
        functools.partial(project_back_kernel, shard=shard, four=four),
        grid_spec=pltpu.PrefetchScalarGridSpec(
            num_scalar_prefetch=1,
            grid=(count // rows,),
            in_specs=[row_block(D), row_block(D), whole(*weight.shape)]
            + [row_block(GROUP)] * 3
            + [whole(*part.shape) for part in late],
            out_specs=[
                pl.BlockSpec((rows, D), lambda i, p: (jnp.minimum(i, 1), 0)),
                pl.BlockSpec((rows, D), lambda i, p: (jnp.maximum(i - 2, 0), 0)),
                whole(*weight.shape),
            ],
            scratch_shapes=[pltpu.VMEM((D, width), F32), pltpu.VMEM((8, D), F32)],
        ),
        out_shape=[half, half, shape(weight.shape, BF)],
        name="project_back",
        **params(),
    )(place, normed, values, weight, *parts, *late)


def first_back_kernel(x_ref, gm_ref, t_ref, a_ref, b_ref, c_ref, out_ref):
    grad = a_ref[...].astype(F32) + b_ref[...].astype(F32) + c_ref[...].astype(F32)
    unit, scale = norm_parts(x_ref[...].astype(F32))
    out_ref[...] = gm_ref[...] + norm_back(unit, scale, grad, t_ref[0:1])


def first_back(tokens, grad_middle, vectors, parts, rows=256):
    full = pl.BlockSpec((rows, D), lambda i: (i, 0))
    return pl.pallas_call(
        first_back_kernel,
        grid=(tokens.shape[0] // rows,),
        in_specs=[full, full, pl.BlockSpec((16, D), lambda i: (0, 0)), full, full, full],
        out_specs=full,
        out_shape=shape(tokens.shape, F32),
        name="first_back",
        **params(),
    )(tokens, grad_middle, vectors, *parts)


def per_device(
    tokens,
    positions,
    ln1_gain,
    ln1_shift,
    qkv_weight,
    qkv_bias,
    out_weight,
    out_bias,
    ln2_gain,
    ln2_shift,
    up_weight,
    up_bias,
    down_weight,
    down_bias,
    cotangent,
):
    rows = tokens.shape[0]
    outer = lax.axis_size("o")
    o, y, x, c = (lax.axis_index(name) for name in ALL)
    ctx = 2 * x + c
    four = outer == 4
    place = jnp.stack([ctx, 2 * y + x, y, o]).astype(jnp.int32)
    shard = ln1_gain.shape[0]
    blocks = D // shard
    half_blocks = blocks // 2
    tall = up_bias.shape[0]
    ff_half = tall * half_blocks

    vector_parts = (
        ln1_gain,
        ln1_shift,
        qkv_bias,
        out_bias,
        ln2_gain,
        ln2_shift,
        up_bias,
        down_bias,
    )
    n_vectors = sum(part.shape[0] for part in vector_parts) // shard
    packed = pack(qkv_weight, [part.reshape(1, -1) for part in vector_parts])
    packed, down_weight, out_weight, up_weight = tie(packed, down_weight, out_weight, up_weight)
    packed = lax.all_to_all(packed, ("x", "c"), 0, 0, tiled=True).reshape(4 * shard, -1)

    up_parts = up_weight.reshape(shard, half_blocks, 2, tall)

    def column_half(which):
        return lax.dynamic_index_in_dim(up_parts, which, 2, keepdims=False).reshape(shard, -1)

    upper = jnp.concatenate(by_place(c, column_half(c), swap(column_half(1 - c), "c")), axis=0)

    packed, tokens, positions, upper, out_weight = tie(
        packed, tokens, positions, upper, out_weight
    )
    packed_far = far_half(packed)
    place_rows = jnp.zeros((16, D), BF).at[:3, :rows].set(positions.astype(BF))
    sent = jnp.concatenate([tokens, place_rows], axis=0)
    from_x = swap(sent, "x")
    out_far = far_half(out_weight)
    packed_far, out_far, packed, down_weight, out_weight = tie(
        packed_far, out_far, packed, down_weight, out_weight
    )
    lower_far = far_half(down_weight)
    out = near_half(out_weight, out_far)
    packed_pair, packed_near = near_half(packed, packed_far)
    packed_y = swap(packed_pair, "y")
    packed_near, packed_y, from_x, upper, lower_far, out = tie(
        packed_near, packed_y, from_x, upper, lower_far, out
    )
    out = all_blocks(out)
    out_x = swap(out, "x")
    if four:
        pieces = (packed_pair, packed_y, packed_near, swap(packed_near, "y"))
    else:
        pieces = (jnp.stack(by_place(y, packed_pair, packed_y), axis=1).reshape(1, D, -1),)
    lower = near_half(down_weight, lower_far)
    upper_far = far_half(upper)
    from_c = swap(jnp.stack([sent, from_x]), "c")
    clip_rows = jnp.concatenate(
        [tokens, from_x[:rows], from_c[0, :rows], from_c[1, :rows]], axis=0
    )
    places = jnp.concatenate(
        [
            positions.astype(F32),
            from_x[rows : rows + 3, :rows].astype(F32),
            from_c[0, rows : rows + 3, :rows].astype(F32),
            from_c[1, rows : rows + 3, :rows].astype(F32),
        ],
        axis=1,
    )
    cosine, sine = rotary_tables(places, PAIR)
    pieces, lower, out_x, upper, upper_far, clip_rows, cosine, sine = tie(
        pieces, lower, out_x, upper, upper_far, clip_rows, cosine, sine
    )
    lower = all_blocks(lower)
    out_y = swap(jnp.stack([out, out_x]), "y")
    lower_x, lower_y = swap(lower, "x"), swap(lower, "y")
    upper = near_half(upper, upper_far)
    normed, q, k, v, vectors, gathered = project(place, clip_rows, pieces, cosine, sine, shard)

    q, upper, out_y = tie(q, upper, out_y)
    upper = all_blocks(upper)
    upper_x, upper_y = swap(upper, "x"), swap(upper, "y")
    cotangent_other = swap(cotangent, "c")
    mixed_far, wide_far, logs_far = attend(q, k, v, 1)
    if four:
        out_own = jnp.stack([out, out_x, out_y[0], out_y[1]])
        out_sources = (out_own, swap(out_own, "c"))
    else:
        out_half = jnp.stack(place_four(y, x, (out, out_x, out_y[0], out_y[1])), axis=1)
        out_half = out_half.reshape(half_blocks, shard, D)
        out_half = jnp.stack(by_place(c, out_half, swap(out_half, "c")), axis=1)
        out_sources = (out_half.reshape(1, 1, D, D), out_half.reshape(1, 1, D, D))
    mixed_far, lower_x, lower_y, out_sources, cotangent_other, q = tie(
        mixed_far, lower_x, lower_y, out_sources, cotangent_other, q
    )
    came_x = swap(mixed_far, "x")
    mixed_near, wide_near, logs_near = attend(q, k, v, 0)
    mixed_near, came_x, upper_y, upper_x, lower_x = tie(
        mixed_near, came_x, upper_y, upper_x, lower_x
    )
    upper_xy = swap(upper_y, "x")
    lower_xy = swap(lower_x, "y")
    came_c = swap(jnp.concatenate([mixed_near[rows:], came_x[rows:]], axis=0), "c")
    mixed = (mixed_near, came_x, came_c)
    mid, normed_two, squares, out_full = middle(place, tokens, vectors, mixed, out_sources, four)

    normed_other = swap(normed_two, "c")
    if four:
        up_pieces = (upper, upper_x, upper_y, upper_xy)
        down_pieces = (lower, lower_x, lower_y, lower_xy)
    else:
        upper = jnp.stack(place_four(y, x, (upper, upper_x, upper_y, upper_xy)), axis=1)
        up_pieces = (upper.reshape(1, D, ff_half),)
        lower = jnp.stack(place_four(y, x, (lower, lower_x, lower_y, lower_xy)), axis=1)
        down_pieces = (lower.reshape(1, ff_half, D),)
    normed_two, bias_up = tie(normed_two, hidden_bias(place, vectors, ff_half, shard, tall))
    results = hidden(
        place,
        bias_up,
        normed_two,
        normed_other,
        cotangent,
        cotangent_other,
        up_pieces,
        down_pieces,
        shard,
    )
    up_bias_grad, gn, gn_sent, mlp, mlp_sent = results[:5]
    gn_came = swap(gn_sent, "c")
    mlp_came = swap(mlp_sent, "c")

    def quarter(values, flip):
        parts = values.reshape(outer, 4, -1, values.shape[-1])
        return lax.dynamic_index_in_dim(parts, (2 * y + x) ^ flip, 1, keepdims=False)

    if four:
        ups, downs = tuple(results[5:9]), tuple(results[9:])
    else:
        ups = tuple(quarter(results[5], flip) for flip in range(4))
        downs = ()
    grad_middle, go_own, go_x, go_c, go_xc, out_kept, out_sent, sums = middle_back(
        place, gn, gn_came, mid, cotangent, vectors, mixed, out_full, shard, four
    )
    go_c, ups = tie(go_c, ups)
    upper_passed = swap(ups[3], "y")
    go_came_c = swap(go_c, "c")
    go_came_x = swap(go_x, "x")
    go_came_xc = lax.ppermute(go_xc, ("x", "c"), DIAGONAL)
    if not four:
        out_grad = out_kept.reshape(half_blocks, 2, shard, D)
        out_sent = lax.dynamic_index_in_dim(out_grad, 1 - c, 1, keepdims=False)
        out_kept = lax.dynamic_index_in_dim(out_grad, c, 1, keepdims=False)
    out_came = swap(out_sent, "c")
    mlp_came, out_sent = tie(mlp_came, out_sent)
    final_low, ends = finish(mid, mlp, mlp_came, vectors, n_vectors - 1)
    go_came_c, out_came, final_low = tie(go_came_c, out_came, final_low)
    if four:
        downs = append(
            place,
            out_kept.reshape(4, 4, shard, D),
            out_came.reshape(4, 4, shard, D),
            downs,
        )
    else:
        out_sums = (out_kept + out_came).reshape(outer * 4, shard, D)
        lower_grad = results[6].reshape(outer * 4, tall, D)
        lower_grad = jnp.concatenate([lower_grad, out_sums], axis=1)
        downs = tuple(quarter(lower_grad, flip) for flip in range(4))

    downs, go_own, go_came_c, go_came_x, go_came_xc = tie(
        downs, go_own, go_came_c, go_came_x, go_came_xc
    )
    lower_passed = swap(downs[3], "x")
    first = attend_back(
        q, k, v, go_own, go_came_c, wide_near, logs_near, cosine, sine, 0
    )
    lower_passed, upper_passed, first, downs, ups = tie(
        lower_passed, upper_passed, first, downs, ups
    )
    upper_kept = swap(ups[2], "y")
    upper_second = swap(ups[1] + upper_passed, "x")
    lower_second = swap(downs[2] + lower_passed, "y")
    parts = attend_back(
        q, k, v, go_came_x, go_came_xc, wide_far, logs_far, cosine, sine, 1, before=first
    )
    upper_second, upper_kept, parts, downs = tie(upper_second, upper_kept, parts, downs)
    lower_kept = swap(downs[1], "x")
    upper_sum = near_sums(ups[0], upper_second, upper_kept)

    gn_low, gn_high, last = project_back(
        place,
        normed,
        clip_rows,
        gathered,
        parts,
        (sums, up_bias_grad, squares, ends),
        shard,
        four,
    )
    gn_low, gn_high, last, upper_sum, lower_kept, lower_second = tie(
        gn_low, gn_high, last, upper_sum, lower_kept, lower_second
    )
    gn_came = swap(gn_high, "c")

    cut = 512
    last = last.reshape(outer, 2, 4 * shard, -1)

    def over_y(values):
        axis = values.ndim - 3
        if four:
            kept, sent = (lax.index_in_dim(values, i, axis, keepdims=False) for i in (0, 1))
        else:
            kept = lax.dynamic_index_in_dim(values, y, axis, keepdims=False)
            sent = lax.dynamic_index_in_dim(values, 1 - y, axis, keepdims=False)
        return kept.astype(F32) + swap(sent.astype(BF), "y").astype(F32)

    high = near_sums(last[..., cut:])
    low = over_y(last[..., :cut]).astype(BF)
    gn_came, low, high, upper_sum, lower_kept = tie(gn_came, low, high, upper_sum, lower_kept)
    low = near_sums(low)
    high = far_sums(high)
    gn_x = swap(gn_low[rows:] + gn_came[rows:], "x")
    upper_grad = far_sums(upper_sum).astype(BF).reshape(2, shard, -1)
    lower_sum = near_sums(downs[0], lower_second, lower_kept)
    low, high = tie(low, high)
    low = far_sums(low)
    high = over_y(high)
    low, high, lower_sum, upper_grad = tie(low, high, lower_sum, upper_grad)
    upper_kept = lax.dynamic_index_in_dim(upper_grad, c, 0, keepdims=False)
    upper_came = swap(lax.dynamic_index_in_dim(upper_grad, 1 - c, 0, keepdims=False), "c")
    last = jnp.concatenate([low.astype(BF), high.astype(BF)], axis=1)
    last, tokens = tie(last, tokens)
    input_grad = first_back(tokens, grad_middle, vectors, (gn_low, gn_came, gn_x))
    last = lax.all_to_all(last.reshape(4, shard, -1), ("x", "c"), 0, 0, tiled=True)
    lower_grad = far_sums(lower_sum, last, input_grad)
    upper_pair = by_place(c, upper_kept, upper_came)
    up_weight_grad = jnp.stack(
        [part.reshape(shard, half_blocks, tall) for part in upper_pair], axis=2
    )
    last = last.astype(F32)
    qkv_weight_grad = last[:, :, : 3 * GROUP].reshape(4, shard, 3, GROUP).transpose(1, 2, 0, 3)
    vector_grads = jnp.sum(last[:, :, 3 * GROUP : 3 * GROUP + n_vectors + 5], axis=0).T
    entry_count = rows * lax.axis_size(ALL) * D
    norm_stats = jnp.sqrt(vector_grads[n_vectors:, 0] / entry_count)

    return (
        final_low,
        input_grad,
        vector_grads[0],
        vector_grads[1],
        qkv_weight_grad.reshape(shard, 3 * D),
        vector_grads[2:5].reshape(-1),
        lower_grad[tall:],
        vector_grads[5],
        vector_grads[6],
        vector_grads[7],
        up_weight_grad.reshape(shard, -1).astype(F32),
        vector_grads[8 : n_vectors - 1].reshape(-1),
        lower_grad[:tall],
        vector_grads[n_vectors - 1],
        norm_stats,
    )


def solution(mesh):
    fine = Mesh(mesh.devices.reshape(-1, 2, 2, 2), ALL)
    rows, vector, whole = P(ALL, None), P(ALL), P()
    in_specs = (
        rows,
        P(None, ALL),
        vector,
        vector,
        rows,
        vector,
        rows,
        vector,
        vector,
        vector,
        rows,
        vector,
        rows,
        vector,
        rows,
    )
    out_specs = (
        rows,
        rows,
        vector,
        vector,
        rows,
        vector,
        rows,
        vector,
        vector,
        vector,
        rows,
        vector,
        rows,
        vector,
        whole,
    )
    return jax.shard_map(
        per_device, mesh=fine, in_specs=in_specs, out_specs=out_specs, check_vma=False
    )
```

```python
import functools
import math

import jax
import jax.numpy as jnp
from jax import lax
from jax.experimental import pallas as pl
from jax.experimental.pallas import tpu as pltpu
from jax.sharding import Mesh
from jax.sharding import PartitionSpec as P

D = 1024
HD = 64
GAP = HD // 6
PAIR = 2 * HD
GROUP = D // 4
EPSILON = 1e-06
BF = jnp.bfloat16
F32 = jnp.float32
ALL = ("o", "y", "x", "c")
SWAP = ((0, 1), (1, 0))
DIAGONAL = ((0, 3), (1, 2), (2, 1), (3, 0))
NT = (((1,), (1,)), ((), ()))
NN = (((1,), (0,)), ((), ()))
TN = (((0,), (0,)), ((), ()))
VMEM_LIMIT = 58 * 2**20
VMEM_MOST = 63 * 2**20
SMALL = pl.CostEstimate(flops=10**6, bytes_accessed=2**16, transcendentals=0)
MASK = (0, 2, 1, 3)


def dot(left, right, dims=NN):
    return lax.dot_general(left, right, dims, preferred_element_type=F32)


def swap(values, axis):
    return lax.ppermute(values, axis, SWAP)


def tie(*values):
    return lax.optimization_barrier(values)


def by_place(flag, own, other):
    return jnp.where(flag == 0, own, other), jnp.where(flag == 0, other, own)


def place_four(high, low, parts):
    first = by_place(low, parts[0], parts[1])
    second = by_place(low, parts[2], parts[3])
    even = by_place(high, first[0], second[0])
    odd = by_place(high, first[1], second[1])
    return even[0], odd[0], even[1], odd[1]


def far(values):
    return lax.ppermute(values, "o", [(i, i ^ 2) for i in range(4)])


def near(values):
    return lax.ppermute(values, "o", [(i, i ^ 1) for i in range(4)])


def level_place(own, level):
    return own ^ (level % 2 * 2 + level // 2)


def far_half(values):
    if lax.axis_size("o") != 4:
        return lax.all_gather(values, "o", axis=0, tiled=False)
    return far(values)


def near_half(values, came):
    if lax.axis_size("o") != 4:
        return came, came
    pair = jnp.stack([values, came])
    return pair, near(pair)


def all_blocks(halves):
    if lax.axis_size("o") != 4:
        return halves[0]
    return jnp.concatenate(halves, axis=0)


def near_sums(*terms):
    if lax.axis_size("o") != 4:
        return sum(terms)
    kept = sum(term[:2].astype(F32) for term in terms)
    return kept, near(sum(term[2:].astype(F32) for term in terms).astype(BF))


def far_sums(values, *earlier):
    if lax.axis_size("o") != 4:
        return lax.psum_scatter(values, "o", scatter_dimension=0, tiled=False).astype(F32)
    kept, came = values
    sums = kept + came.astype(F32)
    came = far(sums[1].astype(BF))
    if earlier:
        came = tie(came, *earlier)[0]
    return sums[0] + came.astype(F32)


def norm_parts(values):
    average = jnp.mean(values, axis=-1, keepdims=True)
    centred = values - average
    spread = jnp.mean(centred * centred, axis=-1, keepdims=True)
    scale = lax.rsqrt(spread + EPSILON)
    return centred * scale, scale


def norm_back(unit, scale, grad, gain):
    scaled = grad * gain
    return scale * (
        scaled
        - jnp.mean(scaled, axis=-1, keepdims=True)
        - unit * jnp.mean(scaled * unit, axis=-1, keepdims=True)
    )


def rotary_tables(places, width):
    column = jnp.arange(width) % HD
    segment = column // (2 * GAP)
    within = column % (2 * GAP)
    freq_index = (within % GAP).astype(F32)
    frequency = jnp.power(10000.0, -freq_index / GAP)
    angles = jnp.zeros((places.shape[1], width), F32)
    for axis_num in range(3):
        angles = (
            angles
            + places[axis_num][:, None] * jnp.where(segment == axis_num, frequency, 0.0)[None, :]
        )
    rotated = segment < 3
    return jnp.where(rotated, jnp.cos(angles), 1.0), jnp.where(rotated, jnp.sin(angles), 0.0)


def shifted(values, leading):
    ahead = pltpu.roll(values, PAIR - GAP, 1)
    behind = pltpu.roll(values, GAP, 1)
    return jnp.where(leading, -ahead, behind)


def leading_lanes():
    lane = lax.broadcasted_iota(jnp.int32, (1, PAIR), 1)
    return lane % HD % (2 * GAP) < GAP


def column_sums(values):
    return jnp.sum(values, axis=0, keepdims=True)


def params(aliases=None, limit=VMEM_LIMIT):
    return dict(
        compiler_params=pltpu.CompilerParams(vmem_limit_bytes=limit),
        cost_estimate=SMALL,
        input_output_aliases=aliases or {},
    )


def shape(dims, kind):
    return jax.ShapeDtypeStruct(dims, kind)


def pack_kernel(w_ref, *refs):
    vectors, out_ref = refs[:-1], refs[-1]
    shard = w_ref.shape[0]
    rows = []
    for ref in vectors:
        values = ref[...].astype(F32)
        rows += [values[:, low : low + shard] for low in range(0, values.shape[1], shard)]
    columns = jnp.concatenate(rows + [jnp.zeros((128 - len(rows), shard), F32)], axis=0).T
    for place in range(4):
        for part in range(3):
            start = part * D + place * GROUP
            out_ref[place, :, part * GROUP : (part + 1) * GROUP] = w_ref[:, start : start + GROUP]
        out_ref[place, :, 3 * GROUP :] = columns.astype(BF)


def pack(weight, vectors):
    return pl.pallas_call(
        pack_kernel,
        out_shape=shape((4, weight.shape[0], 3 * GROUP + 128), BF),
        name="pack",
        **params(),
    )(weight, *vectors)


def bias_places(place, shard):
    column = lax.broadcasted_iota(jnp.int32, (1, 3 * GROUP), 1)
    target = column // GROUP * D + place * GROUP + column % GROUP
    source = target // (3 * shard) * shard + target % shard
    hot = lax.broadcasted_iota(jnp.int32, (D, 3 * GROUP), 0) == source
    return jnp.where(hot, 1.0, 0.0).astype(BF), target % (3 * shard) // shard


def load_blocks(sources, target, semaphores):
    found = []
    for source, index, place in sources:
        block = source if isinstance(index, slice) else source.at[index]
        height = block.shape[0]
        start = pl.multiple_of(place * height, height)
        found.append(
            pltpu.make_async_copy(
                block, target.at[pl.ds(start, height)], semaphores.at[len(found)]
            )
        )
    return found


def piece_blocks(arrays, place):
    if len(arrays) == 1:
        return [(arrays[0], 0, 0)]
    return [
        (source, level, level_place(place[3], level) * 4 + (place[1] ^ flip))
        for flip, source in enumerate(arrays)
        for level in range(4)
    ]


def project_kernel(place_ref, x_ref, cos_ref, sin_ref, *refs, shard, pieces):
    sources, refs = refs[:pieces], refs[pieces:]
    n_ref, q_ref, k_ref, v_ref, t_ref, w_ref, b_ref, semaphores = refs

    @pl.when(pl.program_id(0) == 0)
    def _():
        if pieces == 1:
            blocks = [(sources[0], 0, 0)]
        else:
            blocks = [
                (
                    source,
                    level,
                    (level_place(place_ref[3], level) ^ (piece // 2)) * 2
                    + (place_ref[2] ^ (piece % 2)),
                )
                for piece, source in enumerate(sources)
                for level in range(2)
            ]
        copies = load_blocks(blocks, w_ref, semaphores)
        for copy in copies:
            copy.start()
        for copy in copies:
            copy.wait()
        t_ref[...] = w_ref[:, 3 * GROUP :].astype(F32).T[: t_ref.shape[0]]
        hot, part = bias_places(place_ref[0], shard)
        found = dot(t_ref[...].astype(BF), hot)
        bias = jnp.where(part == 0, found[2:3], jnp.where(part == 1, found[3:4], found[4:5]))
        b_ref[...] = jnp.broadcast_to(bias, b_ref.shape)

    unit, _ = norm_parts(x_ref[...].astype(F32))
    normed = (unit * t_ref[0:1] + t_ref[1:2]).astype(BF)
    n_ref[...] = normed
    joined = dot(normed, w_ref[:, : 3 * GROUP]) + b_ref[0:1]
    cosine, sine, leading = cos_ref[...], sin_ref[...], leading_lanes()
    for ref, start, factor in ((q_ref, 0, 1.0 / math.sqrt(HD)), (k_ref, GROUP, 1.0)):
        for low in range(0, GROUP, PAIR):
            part = joined[:, start + low : start + low + PAIR]
            turned = part * cosine + shifted(part, leading) * sine
            ref[:, low : low + PAIR] = (turned * factor).astype(BF)
    v_ref[...] = joined[:, 2 * GROUP :].astype(BF)


def project(place, values, pieces, cosine, sine, shard, rows=512):
    count = values.shape[0]
    width = pieces[0].shape[-1]

    def part(cols):
        return pl.BlockSpec((rows, cols), lambda i, p: (i, 0))

    def whole(*dims):
        return pl.BlockSpec(dims, lambda i, p: (0, 0))

    return pl.pallas_call(
        functools.partial(project_kernel, shard=shard, pieces=len(pieces)),
        grid_spec=pltpu.PrefetchScalarGridSpec(
            num_scalar_prefetch=1,
            grid=(count // rows,),
            in_specs=[part(D), part(PAIR), part(PAIR)]
            + [pl.BlockSpec(memory_space=pl.ANY)] * len(pieces),
            out_specs=[part(D), part(GROUP), part(GROUP), part(GROUP), whole(16, D), whole(D, width)],
            scratch_shapes=[
                pltpu.VMEM((8, 3 * GROUP), F32),
                pltpu.SemaphoreType.DMA((len(pieces) * pieces[0].shape[0],)),
            ],
        ),
        out_shape=[
            shape((count, D), BF),
            shape((count, GROUP), BF),
            shape((count, GROUP), BF),
            shape((count, GROUP), BF),
            shape((16, D), F32),
            shape((D, width), BF),
        ],
        name="project",
        **params(),
    )(place, values, cosine, sine, *pieces)


def attend_kernel(q_ref, k_ref, v_ref, *refs):
    o_ref, wide_ref, lse_ref = refs[-3:]
    q, k, v = q_ref[...], k_ref[...], v_ref[...]
    lane = lax.broadcasted_iota(jnp.int32, (1, PAIR), 1)
    weights, totals, logs = [], [], []
    for scores in [dot(jnp.where(mine, q, 0), k, NT) for mine in (lane < HD, lane >= HD)]:
        top = jnp.max(scores, axis=1, keepdims=True)
        weight = jnp.exp(scores - top)
        total = jnp.sum(weight, axis=1, keepdims=True)
        weights.append(weight.astype(BF))
        totals.append(total)
        logs.append(top + jnp.log(total))
    mixed = [dot(weight, v) / total for weight, total in zip(weights, totals)]
    out = jnp.where(lane < HD, mixed[0], mixed[1])
    o_ref[...] = out.astype(BF)
    wide_ref[...] = out
    lse_ref[...] = jnp.where(lane < HD, logs[0], logs[1])


def attend(q, k, v, side, pair=None, before=None, rows=256):
    count = q.shape[0]
    half = count // 2
    per = count // 4 // rows
    pairs = GROUP // PAIR if pair is None else 1
    first = 0 if pair is None else pair

    def block(i):
        return i // per * 2 * per + side * per + i % per

    full = pl.BlockSpec((count, PAIR), lambda j, i: (0, first + j))
    out = pl.BlockSpec((rows, PAIR), lambda j, i: (i, first + j))
    before = list(before or ())
    return pl.pallas_call(
        attend_kernel,
        grid=(pairs, half // rows),
        in_specs=[pl.BlockSpec((rows, PAIR), lambda j, i: (block(i), first + j)), full, full]
        + [pl.BlockSpec(memory_space=pl.ANY)] * len(before),
        out_specs=[out, out, out],
        out_shape=[shape((half, GROUP), BF), shape((half, GROUP), F32), shape((half, GROUP), F32)],
        name="attend",
        **params({3: 0, 4: 1, 5: 2} if before else None),
    )(q, k, v, *before)


def attend_back_kernel(
    q_ref, go_ref, go_other_ref, wide_ref, lse_ref, k_ref, v_ref, cos_ref, sin_ref, *refs, last, block
):
    step, rows = pl.program_id(1), q_ref.shape[0]
    if last:
        k_start, v_start, _, gq_ref, gk_ref, gv_ref, k_sum, v_sum = refs
    else:
        gq_ref, k_sum, v_sum = refs

    @pl.when(step == 0)
    def _():
        if last:
            k_sum[...] = k_start[...]
            v_sum[...] = v_start[...]
        else:
            k_sum[...] = jnp.zeros_like(k_sum)
            v_sum[...] = jnp.zeros_like(v_sum)

    q, k, v, lse = q_ref[...], k_ref[...], v_ref[...], lse_ref[...]
    go = jnp.where(step < pl.num_programs(1) // 2, go_ref[...], go_other_ref[...])
    lane = lax.broadcasted_iota(jnp.int32, (1, PAIR), 1)
    leading = leading_lanes()
    product = go.astype(F32) * wide_ref[...]
    grads = []
    for head in range(2):
        mine = (lane < HD) if head == 0 else (lane >= HD)
        q_head, go_head = jnp.where(mine, q, 0), jnp.where(mine, go, 0)
        inner = jnp.sum(jnp.where(mine, product, 0.0), axis=1, keepdims=True)
        weight = jnp.exp(dot(q_head, k, NT) - lse[:, HD * head : HD * head + 1])
        pull = (weight * (dot(go_head, v, NT) - inner)).astype(BF)
        grads.append(dot(pull, k))
        k_sum[...] += dot(q_head.T, pull)
        v_sum[...] += dot(go_head.T, weight.astype(BF))
    grad = jnp.where(lane < HD, grads[0], grads[1])
    here = pl.ds(pl.multiple_of(block(step) * rows, rows), rows)
    grad = grad * cos_ref[here] - shifted(grad * sin_ref[here], leading)
    gq_ref[...] = (grad * (1.0 / math.sqrt(HD))).astype(BF)

    if last:

        @pl.when(step == pl.num_programs(1) - 1)
        def _():
            grad = k_sum[...].T
            grad = grad * cos_ref[...] - shifted(grad * sin_ref[...], leading)
            gk_ref[...] = grad.astype(BF)
            gv_ref[...] = v_sum[...].T.astype(BF)


def attend_back(q, k, v, go, go_other, wide, lse, cosine, sine, side, before=None, rows=512):
    count = q.shape[0]
    half = count // 2
    per = count // 4 // rows
    last = before is not None

    def block(i):
        return i // per * 2 * per + side * per + i % per

    part = pl.BlockSpec((rows, PAIR), lambda pair, i: (block(i), pair))
    own = pl.BlockSpec((rows, PAIR), lambda pair, i: (i, pair))
    full = pl.BlockSpec((count, PAIR), lambda pair, i: (0, pair))
    table = pl.BlockSpec((count, PAIR), lambda pair, i: (0, 0))
    turned = pl.BlockSpec((PAIR, count), lambda pair, i: (pair, 0))
    sums = shape((GROUP, count), F32)
    grad = shape((count, GROUP), BF)
    low = pl.BlockSpec((rows, PAIR), lambda pair, i: (jnp.minimum(i, per - 1), pair))
    high = pl.BlockSpec((rows, PAIR), lambda pair, i: (jnp.maximum(i - per, 0), pair))
    in_specs = [part, low, high, own, own, full, full, table, table]
    operands = [q, go, go_other, wide, lse, k, v, cosine, sine]
    if last:
        in_specs += [turned, turned, pl.BlockSpec(memory_space=pl.ANY)]
        operands += [before[1], before[2], before[0]]
        out_specs, out_shape = [part, full, full], [grad, grad, grad]
        scratch = [pltpu.VMEM((PAIR, count), F32)] * 2
    else:
        out_specs, out_shape, scratch = [part, turned, turned], [grad, sums, sums], []
    return pl.pallas_call(
        functools.partial(attend_back_kernel, last=last, block=block),
        grid=(GROUP // PAIR, half // rows),
        in_specs=in_specs,
        out_specs=out_specs,
        out_shape=out_shape,
        scratch_shapes=scratch,
        name="attend_back",
        **params({11: 0} if last else None),
    )(*operands)


def middle_kernel(place_ref, x_ref, t_ref, *refs, four):
    o_refs, sources, refs = refs[:4], refs[4:6], refs[6:]
    mid_ref, n_ref, s_ref, w_ref, semaphores = refs

    @pl.when(pl.program_id(0) == 0)
    def _():
        s_ref[...] = jnp.zeros_like(s_ref)
        if four:
            blocks = [
                (
                    source.at[flip],
                    level,
                    (level_place(place_ref[3], level) * 4 + (place_ref[1] ^ flip)) * 2
                    + (place_ref[0] % 2 ^ other),
                )
                for other, source in enumerate(sources)
                for flip in range(4)
                for level in range(4)
            ]
        else:
            blocks = [(sources[0].at[0], 0, 0)]
        copies = load_blocks(blocks, w_ref, semaphores)
        for copy in copies:
            copy.start()
        for copy in copies:
            copy.wait()

    x = x_ref[...].astype(F32)
    attn = t_ref[5:6]
    for mask, o_ref in zip(MASK, o_refs):
        start = pl.multiple_of((place_ref[0] ^ mask) * GROUP, GROUP)
        attn = attn + dot(o_ref[...], w_ref[pl.ds(start, GROUP)])
    mid = x + attn
    mid_ref[...] = mid
    unit, _ = norm_parts(mid)
    n_ref[...] = (unit * t_ref[6:7] + t_ref[7:8]).astype(BF)
    s_ref[0:1] += column_sums(x * x)
    s_ref[1:2] += column_sums(attn * attn)
    s_ref[2:3] += column_sums(mid * mid)


def group_specs():
    return [
        pl.BlockSpec((GROUP, D), lambda i, p, mask=mask: (p[0] ^ mask, 0)) for mask in MASK
    ]


def mixed_specs(count, rows):
    first = pl.BlockSpec((rows, GROUP), lambda i, p: (i, 0))
    second = pl.BlockSpec((rows, GROUP), lambda i, p: (i + count // rows, 0))
    return [first, first, first, second]


def middle(place, tokens, vectors, mixed, sources, four, rows=256):
    count = tokens.shape[0]
    full = pl.BlockSpec((rows, D), lambda i, p: (i, 0))

    def whole(*dims):
        return pl.BlockSpec(dims, lambda i, p: (0, 0))

    return pl.pallas_call(
        functools.partial(middle_kernel, four=four),
        grid_spec=pltpu.PrefetchScalarGridSpec(
            num_scalar_prefetch=1,
            grid=(count // rows,),
            in_specs=[full, whole(16, D)]
            + mixed_specs(count, rows)
            + [pl.BlockSpec(memory_space=pl.ANY)] * 2,
            out_specs=[full, full, whole(8, D), whole(D, D)],
            scratch_shapes=[pltpu.SemaphoreType.DMA((32,))],
        ),
        out_shape=[
            shape((count, D), F32),
            shape((count, D), BF),
            shape((8, D), F32),
            shape((D, D), BF),
        ],
        name="middle",
        **params(),
    )(place, tokens, vectors, *mixed, mixed[2], *sources)


def hidden_bias_kernel(place_ref, t_ref, out_ref, *, shard, tall):
    chunk = out_ref.shape[1]
    column = lax.broadcasted_iota(jnp.int32, (1, chunk), 1) + pl.program_id(0) * chunk
    source = (column // tall * 2 + place_ref[0] % 2) * shard + column % shard
    which = column % tall // shard
    hot = lax.broadcasted_iota(jnp.int32, (D, chunk), 0) == source
    found = dot(t_ref[...].astype(BF), jnp.where(hot, 1.0, 0.0).astype(BF))
    bias = jnp.zeros((1, chunk), F32)
    for row in range(tall // shard):
        bias = jnp.where(which == row, found[8 + row : 9 + row], bias)
    out_ref[...] = jnp.broadcast_to(bias, out_ref.shape)


def hidden_bias(place, vectors, width, shard, tall, chunk=512):
    return pl.pallas_call(
        functools.partial(hidden_bias_kernel, shard=shard, tall=tall),
        grid_spec=pltpu.PrefetchScalarGridSpec(
            num_scalar_prefetch=1,
            grid=(width // chunk,),
            in_specs=[pl.BlockSpec((16, D), lambda i, p: (0, 0))],
            out_specs=pl.BlockSpec((8, chunk), lambda i, p: (0, i)),
        ),
        out_shape=shape((8, width), F32),
        name="hidden_bias",
        **params(),
    )(place, vectors)


def hidden_kernel(place_ref, bias_ref, *refs, pieces):
    rows_in, refs = refs[:4], refs[4:]
    up_pieces, down_pieces, refs = refs[:pieces], refs[pieces : 2 * pieces], refs[2 * pieces :]
    b_ref, gn_ref, gn_other_ref, mlp_ref, mlp_other_ref = refs[:5]
    up_outs, down_outs = refs[5 : 5 + pieces], refs[5 + pieces : 5 + 2 * pieces]
    up, down, normed, cot, gn_sum, mlp_sum, up_total, down_total, *semaphores = refs[5 + 2 * pieces :]
    step = pl.program_id(0)
    chunk = bias_ref.shape[1]
    rows = gn_ref.shape[0]
    up_sem, down_sem, normed_sem, cot_sem = semaphores

    @pl.when(step == 0)
    def _():
        copies = load_blocks([(ref, slice(None), i) for i, ref in enumerate(rows_in[:2])], normed, normed_sem)
        copies += load_blocks(piece_blocks(up_pieces, place_ref), up, up_sem)
        copies += load_blocks([(ref, slice(None), i) for i, ref in enumerate(rows_in[2:])], cot, cot_sem)
        copies += load_blocks(piece_blocks(down_pieces, place_ref), down, down_sem)
        for copy in copies:
            copy.start()
        gn_sum[...] = jnp.zeros_like(gn_sum)
        mlp_sum[...] = jnp.zeros_like(mlp_sum)
        for copy in copies:
            copy.wait()

    here = pl.ds(pl.multiple_of(step * chunk, chunk), chunk)
    up_part, down_part = up[:, here], down[here, :]
    upward = dot(normed[...], up_part) + bias_ref[0:1]
    grad_active = dot(cot[...], down_part, NT)
    bell = 0.5 * (1.0 + lax.erf(upward * 0.7071067811865476))
    active = (upward * bell).astype(BF)
    slope = bell + upward * jnp.exp(-0.5 * upward * upward) * (1.0 / math.sqrt(2.0 * math.pi))
    grad_up = (grad_active * slope).astype(BF)
    b_ref[...] = jnp.broadcast_to(column_sums(grad_up.astype(F32)), b_ref.shape)
    gn_sum[...] += dot(grad_up, up_part, NT)
    mlp_sum[...] += dot(active, down_part)
    up_grad = dot(normed[...], grad_up, TN)
    down_grad = dot(active, cot[...], TN)
    if pieces == 1:
        up_outs[0][...] = up_grad.astype(BF)
        down_outs[0][...] = down_grad.astype(BF)
    else:
        up_total[...] = up_grad
        down_total[...] = down_grad
        for flip in range(4):
            for place in range(4):
                start = pl.multiple_of((place * 4 + (place_ref[1] ^ flip)) * (D // 16), D // 16)
                level = level_of(place ^ place_ref[3])
                up_outs[flip][level] = up_total[pl.ds(start, D // 16)].astype(BF)
            start = pl.multiple_of((place_ref[1] ^ flip) * (chunk // 4), chunk // 4)
            down_outs[flip][0] = down_total[pl.ds(start, chunk // 4)].astype(BF)

    @pl.when(step == pl.num_programs(0) - 1)
    def _():
        gn_ref[...] = gn_sum[:rows]
        mlp_ref[...] = mlp_sum[:rows]
        gn_other_ref[...] = gn_sum[rows:].astype(BF)
        mlp_other_ref[...] = mlp_sum[rows:].astype(BF)


def hidden(place, bias, own, other, cot, cot_other, up_pieces, down_pieces, extra):
    rows = own.shape[0]
    width = up_pieces[0].shape[-1]
    pieces = len(up_pieces)
    blocks = pieces * up_pieces[0].shape[0]
    chunk = width // 4

    def whole(*dims):
        return pl.BlockSpec(dims, lambda i, p: (0, 0))

    if pieces == 1:
        grad_specs = [
            pl.BlockSpec((D, chunk), lambda i, p: (0, i)),
            pl.BlockSpec((chunk, D), lambda i, p: (i, 0)),
        ]
        grad_shapes = [shape((D, width), BF), shape((width, D), BF)]
    else:
        grad_specs = [pl.BlockSpec((4, D // 16, chunk), lambda i, p: (0, 0, i))] * 4
        grad_specs += [
            pl.BlockSpec((1, chunk // 4, D), lambda i, p: (level_of(i ^ p[3]), 0, 0))
        ] * 4
        grad_shapes = [shape((4, D // 16, width), BF)] * 4
        grad_shapes += [shape((4, chunk // 4 + extra, D), BF)] * 4
    wide, low = shape((rows, D), F32), shape((rows, D), BF)
    lane_part = pl.BlockSpec((8, chunk), lambda i, p: (0, i))
    return pl.pallas_call(
        functools.partial(hidden_kernel, pieces=pieces),
        grid_spec=pltpu.PrefetchScalarGridSpec(
            num_scalar_prefetch=1,
            grid=(4,),
            in_specs=[lane_part] + [pl.BlockSpec(memory_space=pl.ANY)] * (4 + 2 * pieces),
            out_specs=[lane_part] + [whole(rows, D)] * 4 + grad_specs,
            scratch_shapes=[
                pltpu.VMEM((D, width), BF),
                pltpu.VMEM((width, D), BF),
                pltpu.VMEM((2 * rows, D), BF),
                pltpu.VMEM((2 * rows, D), BF),
                pltpu.VMEM((2 * rows, D), F32),
                pltpu.VMEM((2 * rows, D), F32),
                pltpu.VMEM((D, chunk), F32),
                pltpu.VMEM((chunk, D), F32),
                pltpu.SemaphoreType.DMA((blocks,)),
                pltpu.SemaphoreType.DMA((blocks,)),
                pltpu.SemaphoreType.DMA((2,)),
                pltpu.SemaphoreType.DMA((2,)),
            ],
        ),
        out_shape=[shape((8, width), F32), wide, low, wide, low] + grad_shapes,
        name="hidden",
        **params(limit=VMEM_MOST),
    )(place, bias, own, other, cot, cot_other, *up_pieces, *down_pieces)


def finish_kernel(mid_ref, mlp_ref, came_ref, t_ref, out_ref, s_ref, *, row):
    @pl.when(pl.program_id(0) == 0)
    def _():
        s_ref[...] = jnp.zeros_like(s_ref)

    mlp = mlp_ref[...] + came_ref[...].astype(F32) + t_ref[row : row + 1]
    final = mid_ref[...] + mlp
    out_ref[...] = final.astype(BF)
    s_ref[0:1] += column_sums(mlp * mlp)
    s_ref[1:2] += column_sums(final * final)


def finish(mid, mlp, came, vectors, row, rows=256):
    full = pl.BlockSpec((rows, D), lambda i: (i, 0))
    return pl.pallas_call(
        functools.partial(finish_kernel, row=row),
        grid=(mid.shape[0] // rows,),
        in_specs=[full, full, full, pl.BlockSpec((16, D), lambda i: (0, 0))],
        out_specs=[full, pl.BlockSpec((8, D), lambda i: (0, 0))],
        out_shape=[shape(mid.shape, BF), shape((8, D), F32)],
        name="finish",
        **params(),
    )(mid, mlp, came, vectors)


def append_kernel(place_ref, *refs):
    kept_ref, came_ref, outs = refs[0], refs[1], refs[-4:]
    for flip, out in enumerate(outs):
        for place in range(4):
            row = place_ref[1] ^ flip
            out[level_of(place ^ place_ref[3])] = kept_ref[place, row] + came_ref[place, row]


def append(place, kept, came, quarters):
    shard = kept.shape[2]
    spot = (quarters[0].shape[1] - shard) // shard
    part = pl.BlockSpec((4, 4, shard, D), lambda i, p: (0, 0, 0, 0))
    out = pl.BlockSpec((4, shard, D), lambda i, p: (0, spot, 0))
    return pl.pallas_call(
        append_kernel,
        grid_spec=pltpu.PrefetchScalarGridSpec(
            num_scalar_prefetch=1,
            grid=(1,),
            in_specs=[part, part] + [pl.BlockSpec(memory_space=pl.ANY)] * 4,
            out_specs=[out] * 4,
        ),
        out_shape=[shape(quarter.shape, BF) for quarter in quarters],
        name="append",
        **params({3: 0, 4: 1, 5: 2, 6: 3}),
    )(place, kept, came, *quarters)


def level_of(flip):
    return flip % 2 * 2 + flip // 2


def middle_back_kernel(place_ref, gn_ref, gn_other_ref, mid_ref, cot_ref, t_ref, *refs, four):
    o_refs, w_refs, outs = refs[:4], refs[4:8], refs[8:]
    gm_ref, go_refs, kept_ref, sent_ref, s_ref, total = outs[0], outs[1:5], *outs[5:9]
    step = pl.program_id(0)

    @pl.when(step == 0)
    def _():
        s_ref[...] = jnp.zeros_like(s_ref)
        total[...] = jnp.zeros_like(total)

    grad_two = gn_ref[...] + gn_other_ref[...].astype(F32)
    cot = cot_ref[...].astype(F32)
    unit, scale = norm_parts(mid_ref[...])
    grad_middle = cot + norm_back(unit, scale, grad_two, t_ref[6:7])
    gm_ref[...] = grad_middle
    grad_attn = grad_middle.astype(BF)
    s_ref[0:1] += column_sums(grad_attn.astype(F32))
    s_ref[1:2] += column_sums(grad_two * unit)
    s_ref[2:3] += column_sums(grad_two)
    s_ref[3:4] += column_sums(cot)
    for mask, o_ref, w_ref, go_ref in zip(MASK, o_refs, w_refs, go_refs):
        go_ref[...] = dot(grad_attn, w_ref[...], NT).astype(BF)
        start = pl.multiple_of((place_ref[0] ^ mask) * GROUP, GROUP)
        total[pl.ds(start, GROUP)] += dot(o_ref[...], grad_attn, TN)

    @pl.when(step == pl.num_programs(0) - 1)
    def _():
        if not four:
            kept_ref[...] = total[...].astype(BF)
            sent_ref[...] = jnp.zeros_like(sent_ref)
            return
        blocks, shard = kept_ref.shape[:2]
        for other, ref in enumerate((kept_ref, sent_ref)):
            for block in range(blocks):
                start = pl.multiple_of((2 * block + (place_ref[0] % 2 ^ other)) * shard, shard)
                ref[block] = total[pl.ds(start, shard)].astype(BF)


def middle_back(place, gn, gn_other, mid, cot, vectors, mixed, weight, shard, four, rows=512):
    count = mid.shape[0]
    full = pl.BlockSpec((rows, D), lambda i, p: (i, 0))
    part = pl.BlockSpec((rows, GROUP), lambda i, p: (i, 0))

    def whole(*dims):
        return pl.BlockSpec(dims, lambda i, p: (0, 0))

    if four:
        half = (D // (2 * shard), shard, D)
        out_specs = [pl.BlockSpec(half, lambda i, p: (0, 0, 0))] * 2
        out_shapes = [shape(half, BF)] * 2
    else:
        out_specs = [whole(D, D), whole(8, D)]
        out_shapes = [shape((D, D), BF), shape((8, D), BF)]
    return pl.pallas_call(
        functools.partial(middle_back_kernel, four=four),
        grid_spec=pltpu.PrefetchScalarGridSpec(
            num_scalar_prefetch=1,
            grid=(count // rows,),
            in_specs=[full, full, full, full, whole(16, D)]
            + mixed_specs(count, rows)
            + group_specs(),
            out_specs=[full] + [part] * 4 + out_specs + [whole(8, D)],
            scratch_shapes=[pltpu.VMEM((D, D), F32)],
        ),
        out_shape=[shape((count, D), F32)]
        + [shape((count, GROUP), BF)] * 4
        + out_shapes
        + [shape((8, D), F32)],
        name="middle_back",
        **params(),
    )(place, gn, gn_other, mid, cot, vectors, *mixed, mixed[2], *([weight] * 4))


def project_back_kernel(
    place_ref, n_ref, x_ref, w_ref, gq_ref, gk_ref, gv_ref, late_ref, up_ref, squares_ref, ends_ref,
    own_ref, other_ref, grad_ref, total, sums, *, shard, four
):
    step = pl.program_id(0)

    @pl.when(step == 0)
    def _():
        total[...] = jnp.zeros_like(total)
        sums[...] = jnp.zeros_like(sums)

    joined = jnp.concatenate([gq_ref[...], gk_ref[...], gv_ref[...]], axis=1)
    width = 3 * GROUP
    grad = dot(joined, w_ref[:, :width], NT)

    @pl.when(step < 2)
    def _():
        own_ref[...] = grad.astype(BF)

    @pl.when(step >= 2)
    def _():
        other_ref[...] = grad.astype(BF)

    total[...] += dot(n_ref[...], joined, TN)
    unit, _ = norm_parts(x_ref[...].astype(F32))
    sums[0:1] += column_sums(grad * unit)
    sums[1:2] += column_sums(grad)
    sums[2:3, :width] += column_sums(joined.astype(F32))

    @pl.when(step == pl.num_programs(0) - 1)
    def _():
        hot, part = bias_places(place_ref[0], shard)
        bias = sums[2:3, :width]
        spread = [
            dot(jnp.broadcast_to(jnp.where(part == j, bias, 0.0), (8, width)).astype(BF), hot, NT)
            for j in range(3)
        ]
        rows = [sums[0:1], sums[1:2], *[part[0:1] for part in spread]]
        rows += [late_ref[0:1], late_ref[1:2], late_ref[2:3]]
        wide = up_ref.shape[1]
        tall = 2 * wide * shard // D
        column = lax.broadcasted_iota(jnp.int32, (1, wide), 1)
        source = (column // tall * 2 + place_ref[0] % 2) * shard + column % shard
        which = column % tall // shard
        hot = lax.broadcasted_iota(jnp.int32, (D, wide), 0) == source
        ups = jnp.concatenate(
            [jnp.where(which == j, up_ref[0:1], 0.0) for j in range(tall // shard)]
            + [jnp.zeros((8 - tall // shard, wide), F32)],
            axis=0,
        )
        ups = dot(ups.astype(BF), jnp.where(hot, 1.0, 0.0).astype(BF), NT)
        rows += [ups[j : j + 1] for j in range(tall // shard)]
        rows += [late_ref[3:4]]
        for ref, j in ((squares_ref, 0), (squares_ref, 1), (squares_ref, 2), (ends_ref, 0), (ends_ref, 1)):
            rows += [jnp.broadcast_to(jnp.sum(ref[j : j + 1], axis=1, keepdims=True), (1, D))]
        rows += [jnp.zeros((128 - len(rows), D), F32)]
        vectors = jnp.concatenate(rows, axis=0).T.astype(BF)
        height = D // 8 if four else D
        for block in range(D // height):
            start = 0
            if four:
                flip = block // 2 ^ place_ref[3]
                start = pl.multiple_of(
                    (level_of(flip) * 2 + (block % 2 ^ place_ref[2])) * height, height
                )
            here = slice(block * height, (block + 1) * height)
            grad_ref[pl.ds(start, height), :width] = total[here].astype(BF)
            grad_ref[pl.ds(start, height), width:] = vectors[here]


def project_back(place, normed, values, weight, parts, late, shard, four, rows=512):
    count = normed.shape[0]
    width = 3 * GROUP

    def row_block(cols):
        return pl.BlockSpec((rows, cols), lambda i, p: (i, 0))

    def whole(*dims):
        return pl.BlockSpec(dims, lambda i, p: (0, 0))

    half = shape((count // 2, D), BF)
    return pl.pallas_call(
        functools.partial(project_back_kernel, shard=shard, four=four),
        grid_spec=pltpu.PrefetchScalarGridSpec(
            num_scalar_prefetch=1,
            grid=(count // rows,),
            in_specs=[row_block(D), row_block(D), whole(*weight.shape)]
            + [row_block(GROUP)] * 3
            + [whole(*part.shape) for part in late],
            out_specs=[
                pl.BlockSpec((rows, D), lambda i, p: (jnp.minimum(i, 1), 0)),
                pl.BlockSpec((rows, D), lambda i, p: (jnp.maximum(i - 2, 0), 0)),
                whole(*weight.shape),
            ],
            scratch_shapes=[pltpu.VMEM((D, width), F32), pltpu.VMEM((8, D), F32)],
        ),
        out_shape=[half, half, shape(weight.shape, BF)],
        name="project_back",
        **params(),
    )(place, normed, values, weight, *parts, *late)


def first_back_kernel(x_ref, gm_ref, t_ref, a_ref, b_ref, c_ref, out_ref):
    grad = a_ref[...].astype(F32) + b_ref[...].astype(F32) + c_ref[...].astype(F32)
    unit, scale = norm_parts(x_ref[...].astype(F32))
    out_ref[...] = gm_ref[...] + norm_back(unit, scale, grad, t_ref[0:1])


def first_back(tokens, grad_middle, vectors, parts, rows=256):
    full = pl.BlockSpec((rows, D), lambda i: (i, 0))
    return pl.pallas_call(
        first_back_kernel,
        grid=(tokens.shape[0] // rows,),
        in_specs=[full, full, pl.BlockSpec((16, D), lambda i: (0, 0)), full, full, full],
        out_specs=full,
        out_shape=shape(tokens.shape, F32),
        name="first_back",
        **params(),
    )(tokens, grad_middle, vectors, *parts)


def per_device(
    tokens,
    positions,
    ln1_gain,
    ln1_shift,
    qkv_weight,
    qkv_bias,
    out_weight,
    out_bias,
    ln2_gain,
    ln2_shift,
    up_weight,
    up_bias,
    down_weight,
    down_bias,
    cotangent,
):
    rows = tokens.shape[0]
    outer = lax.axis_size("o")
    o, y, x, c = (lax.axis_index(name) for name in ALL)
    ctx = 2 * x + c
    four = outer == 4
    place = jnp.stack([ctx, 2 * y + x, y, o]).astype(jnp.int32)
    shard = ln1_gain.shape[0]
    blocks = D // shard
    half_blocks = blocks // 2
    tall = up_bias.shape[0]
    ff_half = tall * half_blocks

    vector_parts = (
        ln1_gain,
        ln1_shift,
        qkv_bias,
        out_bias,
        ln2_gain,
        ln2_shift,
        up_bias,
        down_bias,
    )
    n_vectors = sum(part.shape[0] for part in vector_parts) // shard
    packed = pack(qkv_weight, [part.reshape(1, -1) for part in vector_parts])
    packed, down_weight, out_weight, up_weight = tie(packed, down_weight, out_weight, up_weight)
    packed = lax.all_to_all(packed, ("x", "c"), 0, 0, tiled=True).reshape(4 * shard, -1)

    up_parts = up_weight.reshape(shard, half_blocks, 2, tall)

    def column_half(which):
        return lax.dynamic_index_in_dim(up_parts, which, 2, keepdims=False).reshape(shard, -1)

    upper = jnp.concatenate(by_place(c, column_half(c), swap(column_half(1 - c), "c")), axis=0)

    packed, tokens, positions, upper, out_weight = tie(
        packed, tokens, positions, upper, out_weight
    )
    packed_far = far_half(packed)
    place_rows = jnp.zeros((16, D), BF).at[:3, :rows].set(positions.astype(BF))
    sent = jnp.concatenate([tokens, place_rows], axis=0)
    from_x = swap(sent, "x")
    out_far = far_half(out_weight)
    packed_far, out_far, packed, down_weight, out_weight = tie(
        packed_far, out_far, packed, down_weight, out_weight
    )
    lower_far = far_half(down_weight)
    out = near_half(out_weight, out_far)
    packed_pair, packed_near = near_half(packed, packed_far)
    packed_y = swap(packed_pair, "y")
    packed_near, packed_y, from_x, upper, lower_far, out = tie(
        packed_near, packed_y, from_x, upper, lower_far, out
    )
    out = all_blocks(out)
    out_x = swap(out, "x")
    if four:
        pieces = (packed_pair, packed_y, packed_near, swap(packed_near, "y"))
    else:
        pieces = (jnp.stack(by_place(y, packed_pair, packed_y), axis=1).reshape(1, D, -1),)
    lower = near_half(down_weight, lower_far)
    upper_far = far_half(upper)
    from_c = swap(jnp.stack([sent, from_x]), "c")
    clip_rows = jnp.concatenate(
        [tokens, from_x[:rows], from_c[0, :rows], from_c[1, :rows]], axis=0
    )
    places = jnp.concatenate(
        [
            positions.astype(F32),
            from_x[rows : rows + 3, :rows].astype(F32),
            from_c[0, rows : rows + 3, :rows].astype(F32),
            from_c[1, rows : rows + 3, :rows].astype(F32),
        ],
        axis=1,
    )
    cosine, sine = rotary_tables(places, PAIR)
    pieces, lower, out_x, upper, upper_far, clip_rows, cosine, sine = tie(
        pieces, lower, out_x, upper, upper_far, clip_rows, cosine, sine
    )
    lower = all_blocks(lower)
    out_y = swap(jnp.stack([out, out_x]), "y")
    lower_x, lower_y = swap(lower, "x"), swap(lower, "y")
    upper = near_half(upper, upper_far)
    normed, q, k, v, vectors, gathered = project(place, clip_rows, pieces, cosine, sine, shard)

    q, upper, out_y = tie(q, upper, out_y)
    upper = all_blocks(upper)
    upper_x, upper_y = swap(upper, "x"), swap(upper, "y")
    cotangent_other = swap(cotangent, "c")
    mixed_far, wide_far, logs_far = attend(q, k, v, 1)
    if four:
        out_own = jnp.stack([out, out_x, out_y[0], out_y[1]])
        out_sources = (out_own, swap(out_own, "c"))
    else:
        out_half = jnp.stack(place_four(y, x, (out, out_x, out_y[0], out_y[1])), axis=1)
        out_half = out_half.reshape(half_blocks, shard, D)
        out_half = jnp.stack(by_place(c, out_half, swap(out_half, "c")), axis=1)
        out_sources = (out_half.reshape(1, 1, D, D), out_half.reshape(1, 1, D, D))
    mixed_far, lower_x, lower_y, out_sources, cotangent_other, q = tie(
        mixed_far, lower_x, lower_y, out_sources, cotangent_other, q
    )
    came_x = swap(mixed_far, "x")
    mixed_near, wide_near, logs_near = attend(q, k, v, 0)
    mixed_near, came_x, upper_y, upper_x, lower_x = tie(
        mixed_near, came_x, upper_y, upper_x, lower_x
    )
    upper_xy = swap(upper_y, "x")
    lower_xy = swap(lower_x, "y")
    came_c = swap(jnp.concatenate([mixed_near[rows:], came_x[rows:]], axis=0), "c")
    mixed = (mixed_near, came_x, came_c)
    mid, normed_two, squares, out_full = middle(place, tokens, vectors, mixed, out_sources, four)

    normed_other = swap(normed_two, "c")
    if four:
        up_pieces = (upper, upper_x, upper_y, upper_xy)
        down_pieces = (lower, lower_x, lower_y, lower_xy)
    else:
        upper = jnp.stack(place_four(y, x, (upper, upper_x, upper_y, upper_xy)), axis=1)
        up_pieces = (upper.reshape(1, D, ff_half),)
        lower = jnp.stack(place_four(y, x, (lower, lower_x, lower_y, lower_xy)), axis=1)
        down_pieces = (lower.reshape(1, ff_half, D),)
    normed_two, bias_up = tie(normed_two, hidden_bias(place, vectors, ff_half, shard, tall))
    results = hidden(
        place,
        bias_up,
        normed_two,
        normed_other,
        cotangent,
        cotangent_other,
        up_pieces,
        down_pieces,
        shard,
    )
    up_bias_grad, gn, gn_sent, mlp, mlp_sent = results[:5]
    gn_came = swap(gn_sent, "c")
    mlp_came = swap(mlp_sent, "c")

    def quarter(values, flip):
        parts = values.reshape(outer, 4, -1, values.shape[-1])
        return lax.dynamic_index_in_dim(parts, (2 * y + x) ^ flip, 1, keepdims=False)

    if four:
        ups, downs = tuple(results[5:9]), tuple(results[9:])
    else:
        ups = tuple(quarter(results[5], flip) for flip in range(4))
        downs = ()
    grad_middle, go_own, go_x, go_c, go_xc, out_kept, out_sent, sums = middle_back(
        place, gn, gn_came, mid, cotangent, vectors, mixed, out_full, shard, four
    )
    go_c, ups = tie(go_c, ups)
    upper_passed = swap(ups[3], "y")
    go_came_c = swap(go_c, "c")
    go_came_x = swap(go_x, "x")
    go_came_xc = lax.ppermute(go_xc, ("x", "c"), DIAGONAL)
    if not four:
        out_grad = out_kept.reshape(half_blocks, 2, shard, D)
        out_sent = lax.dynamic_index_in_dim(out_grad, 1 - c, 1, keepdims=False)
        out_kept = lax.dynamic_index_in_dim(out_grad, c, 1, keepdims=False)
    out_came = swap(out_sent, "c")
    mlp_came, out_sent = tie(mlp_came, out_sent)
    final_low, ends = finish(mid, mlp, mlp_came, vectors, n_vectors - 1)
    go_came_c, out_came, final_low = tie(go_came_c, out_came, final_low)
    if four:
        downs = append(
            place,
            out_kept.reshape(4, 4, shard, D),
            out_came.reshape(4, 4, shard, D),
            downs,
        )
    else:
        out_sums = (out_kept + out_came).reshape(outer * 4, shard, D)
        lower_grad = results[6].reshape(outer * 4, tall, D)
        lower_grad = jnp.concatenate([lower_grad, out_sums], axis=1)
        downs = tuple(quarter(lower_grad, flip) for flip in range(4))

    downs, go_own, go_came_c, go_came_x, go_came_xc = tie(
        downs, go_own, go_came_c, go_came_x, go_came_xc
    )
    lower_passed = swap(downs[3], "x")
    first = attend_back(
        q, k, v, go_own, go_came_c, wide_near, logs_near, cosine, sine, 0
    )
    lower_passed, upper_passed, first, downs, ups = tie(
        lower_passed, upper_passed, first, downs, ups
    )
    upper_kept = swap(ups[2], "y")
    upper_second = swap(ups[1] + upper_passed, "x")
    lower_second = swap(downs[2] + lower_passed, "y")
    parts = attend_back(
        q, k, v, go_came_x, go_came_xc, wide_far, logs_far, cosine, sine, 1, before=first
    )
    upper_second, upper_kept, parts, downs = tie(upper_second, upper_kept, parts, downs)
    lower_kept = swap(downs[1], "x")
    upper_sum = near_sums(ups[0], upper_second, upper_kept)

    gn_low, gn_high, last = project_back(
        place,
        normed,
        clip_rows,
        gathered,
        parts,
        (sums, up_bias_grad, squares, ends),
        shard,
        four,
    )
    gn_low, gn_high, last, upper_sum, lower_kept, lower_second = tie(
        gn_low, gn_high, last, upper_sum, lower_kept, lower_second
    )
    gn_came = swap(gn_high, "c")

    cut = 512
    last = last.reshape(outer, 2, 4 * shard, -1)

    def over_y(values):
        axis = values.ndim - 3
        if four:
            kept, sent = (lax.index_in_dim(values, i, axis, keepdims=False) for i in (0, 1))
        else:
            kept = lax.dynamic_index_in_dim(values, y, axis, keepdims=False)
            sent = lax.dynamic_index_in_dim(values, 1 - y, axis, keepdims=False)
        return kept.astype(F32) + swap(sent.astype(BF), "y").astype(F32)

    high = near_sums(last[..., cut:])
    low = over_y(last[..., :cut]).astype(BF)
    gn_came, low, high, upper_sum, lower_kept = tie(gn_came, low, high, upper_sum, lower_kept)
    low = near_sums(low)
    high = far_sums(high)
    gn_x = swap(gn_low[rows:] + gn_came[rows:], "x")
    upper_grad = far_sums(upper_sum).astype(BF).reshape(2, shard, -1)
    lower_sum = near_sums(downs[0], lower_second, lower_kept)
    low, high = tie(low, high)
    low = far_sums(low)
    high = over_y(high)
    low, high, lower_sum, upper_grad = tie(low, high, lower_sum, upper_grad)
    upper_kept = lax.dynamic_index_in_dim(upper_grad, c, 0, keepdims=False)
    upper_came = swap(lax.dynamic_index_in_dim(upper_grad, 1 - c, 0, keepdims=False), "c")
    last = jnp.concatenate([low.astype(BF), high.astype(BF)], axis=1)
    last, tokens = tie(last, tokens)
    input_grad = first_back(tokens, grad_middle, vectors, (gn_low, gn_came, gn_x))
    last = lax.all_to_all(last.reshape(4, shard, -1), ("x", "c"), 0, 0, tiled=True)
    lower_grad = far_sums(lower_sum, last, input_grad)
    upper_pair = by_place(c, upper_kept, upper_came)
    up_weight_grad = jnp.stack(
        [part.reshape(shard, half_blocks, tall) for part in upper_pair], axis=2
    )
    last = last.astype(F32)
    qkv_weight_grad = last[:, :, : 3 * GROUP].reshape(4, shard, 3, GROUP).transpose(1, 2, 0, 3)
    vector_grads = jnp.sum(last[:, :, 3 * GROUP : 3 * GROUP + n_vectors + 5], axis=0).T
    entry_count = rows * lax.axis_size(ALL) * D
    norm_stats = jnp.sqrt(vector_grads[n_vectors:, 0] / entry_count)

    return (
        final_low,
        input_grad,
        vector_grads[0],
        vector_grads[1],
        qkv_weight_grad.reshape(shard, 3 * D),
        vector_grads[2:5].reshape(-1),
        lower_grad[tall:],
        vector_grads[5],
        vector_grads[6],
        vector_grads[7],
        up_weight_grad.reshape(shard, -1).astype(F32),
        vector_grads[8 : n_vectors - 1].reshape(-1),
        lower_grad[:tall],
        vector_grads[n_vectors - 1],
        norm_stats,
    )


def solution(mesh):
    fine = Mesh(mesh.devices.reshape(-1, 2, 2, 2), ALL)
    rows, vector, whole = P(ALL, None), P(ALL), P()
    in_specs = (
        rows,
        P(None, ALL),
        vector,
        vector,
        rows,
        vector,
        rows,
        vector,
        vector,
        vector,
        rows,
        vector,
        rows,
        vector,
        rows,
    )
    out_specs = (
        rows,
        rows,
        vector,
        vector,
        rows,
        vector,
        rows,
        vector,
        vector,
        vector,
        rows,
        vector,
        rows,
        vector,
        whole,
    )
    return jax.shard_map(
        per_device, mesh=fine, in_specs=in_specs, out_specs=out_specs, check_vma=False
    )
```
